512 devices in a mesh: ctx: 16 (over x, y_hi, core), exp: 8 (over z), hid: 4 (over y_lo).
Axes of the slice: x: 4, y: 8 (y_hi: 2, y_lo: 4; y = y_hi * 4 + y_lo), z: 8, core: 2. Of those that a mesh axis runs over, the one named last changes fastest.
Arguments:
- queries: bfloat16 [2048, 4096], P('ctx', ('exp', 'hid')), may hold values from -16 to 16
- key_heads: bfloat16 [2048, 1024], P('ctx', 'exp'), may hold values from -16 to 16
- value_heads: bfloat16 [2048, 1024], P('ctx', 'exp'), may hold values from -8 to 8
- residual: bfloat16 [2048, 4096], P(('ctx', 'exp'), 'hid'), may hold values from -3 to 3
- out_weight: bfloat16 [4096, 4096], P(('exp', 'hid')), may hold values from -0.09375 to 0.09375
- norm_gain: float32 [4096], P('hid'), may hold values from 0.1 to 1.9
- gate_weight: bfloat16 [8, 4096, 8192], P('exp', 'hid', 'ctx'), may hold values from -0.09375 to 0.09375
- up_weight: bfloat16 [8, 4096, 8192], P('exp', 'hid', 'ctx'), may hold values from -0.09375 to 0.09375
- down_weight: bfloat16 [8, 8192, 4096], P('exp', 'ctx', 'hid'), may hold values from -0.0625 to 0.0625
- expert_ids: int32 [2048, 2], P(('ctx', 'exp')), may hold values from 0 to 7, all different within a row; in each aligned block of 16 rows (0 to 15, 16 to 31, ...) at most 6 rows name the same one
- expert_weights: float32 [2048, 2], P(('ctx', 'exp')), may hold values from 0.5 to 2
Outputs:
- layer_out: bfloat16 [2048, 4096], P(('ctx', 'exp'), 'hid')
The draws below stay inside these ranges and needn't reach their ends.
Inputs may be any that keep to these rules, and one draw needn't show every extreme that they name: `expert_ids`: each row names 2 different experts. Within each aligned block of 16 rows no expert is named by more than 6 rows, a bound that some block reaches.
All inputs are finite; a program needn't handle non-finite values.
Results may differ from the reference program's by a relative error of at most 0.015.
Values may be sent and summed in bfloat16 or wider, within the bound.
No kernel may reach another device: no remote copies, remote signals or barrier semaphores. Data moves between devices by JAX's collectives and lax.ppermute only.
A program may use at most 64 MiB of HBM per device.

```python
import math
import jax
import jax.numpy as jnp
import numpy as np
from jax import lax

HEADS = 32
KV_HEADS = 8
HEAD = 128
D = 4096
FF = 8192
TOP = 2
EXPERTS = 8
TOKENS = 2048
ROWS_DEV = 16
CAP = 6
N_CTX = 16


def draw_queries(key, part):
    key = jax.random.fold_in(key, 1)
    values_out = jnp.clip(jax.random.normal(key, (TOKENS, HEADS, HEAD), jnp.float32), -4.0, 4.0)
    return values_out.reshape(TOKENS, HEADS * HEAD).astype(jnp.bfloat16)


def draw_key_heads(key, part):
    key = jax.random.fold_in(key, 2)
    values_out = jnp.clip(jax.random.normal(key, (TOKENS, KV_HEADS, HEAD), jnp.float32), -4.0, 4.0)
    return values_out.reshape(TOKENS, KV_HEADS * HEAD).astype(jnp.bfloat16)


def block_levels(own_key, shape, pieces, low, largest):
    def one(dim, shards_of):
        draws = jax.random.uniform(jax.random.fold_in(jax.random.fold_in(own_key, 6), dim), (shards_of,), jnp.float32, low / len(pieces), largest / len(pieces))
        return jnp.repeat(jnp.exp(draws), shape[dim] // shards_of).reshape((-1,) + (1,) * (len(shape) - dim - 1))

    factor_of = one(*pieces[0])
    for cut in pieces[1:]:
        factor_of = factor_of * one(*cut)
    return factor_of


def assign_block(rng, own, number, rows, amount, top, limit, skew):
    sequence = jax.random.permutation(rng, amount)
    heavy_load, common = shares(amount, rows * top, limit, skew, True), shares(amount, rows * top, limit, skew, False)
    places = jnp.arange(amount)

    def named(lengths, offset_by):
        used = int((lengths > 0).sum())
        fixed = max(1, used // 4)
        moved = fixed + (places - fixed + offset_by * (used - fixed)) % max(1, amount - fixed)
        return jnp.zeros((amount,), jnp.int32).at[sequence[jnp.where(places < fixed, places, moved)]].set(jnp.asarray(lengths, jnp.int32))

    lengths = jnp.where(number % 4 == 0, named(heavy_load, number // 4), named(common, number - number // 4 - 1))
    mixed = jax.random.permutation(jax.random.fold_in(own, 3), amount)
    source_of, taker = mixed[0:amount // 2 * 2:2], mixed[1:amount // 2 * 2:2]
    slack = jnp.minimum(lengths[source_of] - 1, limit - lengths[taker]) // 2
    slack = jnp.where((source_of == sequence[0]) | (taker == sequence[0]) | (lengths[taker] == 0), 0, jnp.maximum(slack, 0))
    moved = jax.random.randint(jax.random.fold_in(own, 4), (amount // 2,), 0, 1 << 20) % (slack + 1)
    lengths = lengths.at[source_of].add(-moved).at[taker].add(moved)
    members = jnp.searchsorted(jnp.cumsum(lengths), jnp.arange(rows * top), side="right").astype(jnp.int32)
    listing = members.reshape(top, rows).T
    listing = listing[jax.random.permutation(jax.random.fold_in(own, 1), rows)]
    offset_by = jax.random.randint(jax.random.fold_in(own, 2), (rows, 1), 0, top)
    return jnp.take_along_axis(listing, (jnp.arange(top)[None, :] + offset_by) % top, axis=1)


def shares(count, total, bound, skew, full):
    portions = [(1 << 20) // math.isqrt(grade ** skew) + 1 for grade in range(1, count + 1)]
    largest = bound if full else min(bound, max(-(-total // count), total * portions[0] // sum(portions)))
    least = 1 if total - largest >= count - 1 else 0
    given, spare = [largest] + [least] * (count - 1), total - largest - least * (count - 1)
    while spare > 0:
        free = [i for i in range(1, count) if given[i] < largest] or [i for i in range(1, count) if given[i] < bound]
        whole, remaining = sum([portions[i] for i in free]), spare
        for i in free:
            more = min(bound - given[i], max(1, remaining * portions[i] // whole), spare)
            given[i] = given[i] + more
            spare = spare - more
    return np.array(given)


def gaussian(rng, shape, spread, bound, cuts=(), kind=jnp.bfloat16):
    factor_of = block_levels(rng, shape, cuts, -0.22, 0.18) if cuts else 1.0
    drawn = jax.random.normal(rng, shape, jnp.float32) * spread * factor_of
    return jnp.minimum(jnp.maximum(drawn, -bound), bound).astype(kind)


def setup_inputs(seed: int = 0) -> dict:
    seeds = jax.random.split(jax.random.key(seed), 12)
    queries = draw_queries(jax.random.fold_in(seeds[11], 71), 0)
    key_heads = draw_key_heads(jax.random.fold_in(seeds[11], 71), 0)
    value_heads = gaussian(seeds[2], (TOKENS, KV_HEADS * HEAD), 2.0, 8.0, ((0, 16), (1, 8)))
    residual = gaussian(seeds[3], (TOKENS, D), 0.5, 3.0, ((0, 128), (1, 4)))
    out_weight = gaussian(seeds[4], (HEADS * HEAD, D), (HEADS * HEAD) ** -0.5, 0.09375, ((0, 32),))
    norm_gain = jnp.clip(1.0 + 0.18 * jax.random.normal(seeds[5], (D,), jnp.float32), 0.1, 1.9)
    gate_weight = gaussian(seeds[6], (EXPERTS, D, FF), D ** -0.5, 0.09375, ((0, 8), (1, 4), (2, 16)))
    up_weight = gaussian(seeds[7], (EXPERTS, D, FF), D ** -0.5, 0.09375, ((0, 8), (1, 4), (2, 16)))
    down_weight = gaussian(seeds[8], (EXPERTS, FF, D), FF ** -0.5, 0.0625, ((0, 8), (1, 16), (2, 4)))
    expert_ids_keys = jax.random.split(jax.random.fold_in(seeds[9], 1), TOKENS // ROWS_DEV)
    expert_ids_turns = jax.random.permutation(jax.random.fold_in(seeds[9], 3), TOKENS // ROWS_DEV)
    expert_ids = jax.vmap(lambda own, number: assign_block(jax.random.fold_in(seeds[9], 2), own, number, ROWS_DEV, EXPERTS, TOP, CAP, 2))(expert_ids_keys, expert_ids_turns).reshape((TOKENS, TOP))
    expert_weights = jnp.clip(0.5 + 1.5 * jax.random.uniform(seeds[10], (TOKENS, TOP), jnp.float32) ** block_levels(seeds[10], (TOKENS, TOP), ((0, 128),), -0.2, 0.2), 0.5, 2.0)
    return {"queries": queries, "key_heads": key_heads, "value_heads": value_heads, "residual": residual, "out_weight": out_weight, "norm_gain": norm_gain, "gate_weight": gate_weight, "up_weight": up_weight, "down_weight": down_weight, "expert_ids": expert_ids, "expert_weights": expert_weights}


def slot_table(expert_ids):
    blocks = expert_ids.reshape(-1, ROWS_DEV * TOP)
    onehot = (blocks[:, :, None] == jnp.arange(EXPERTS, dtype=jnp.int32)[None, None, :]).astype(jnp.int32)
    earlier = jnp.cumsum(onehot, axis=1) - onehot
    slot_index = lax.optimization_barrier(jnp.sum(earlier * onehot, axis=2)).astype(jnp.int32)
    return (blocks, slot_index)

def reference(queries, key_heads, value_heads, residual, out_weight, norm_gain, gate_weight, up_weight, down_weight, expert_ids, expert_weights):
    group_size = HEADS // KV_HEADS
    query_all = queries.reshape(TOKENS, HEADS, HEAD).transpose(1, 0, 2)
    key_all = key_heads.reshape(TOKENS, KV_HEADS, HEAD).transpose(1, 0, 2)
    value_all = value_heads.reshape(TOKENS, KV_HEADS, HEAD).transpose(1, 0, 2)
    position = jnp.arange(TOKENS, dtype=jnp.int32)
    causal = position[:, None] >= position[None, :]
    score_scale = 1.0 / math.sqrt(HEAD)

    def one_head(head_index):
        query_one = lax.dynamic_index_in_dim(query_all, head_index, 0, keepdims=False)
        key_one = lax.dynamic_index_in_dim(key_all, head_index // group_size, 0, keepdims=False)
        value_one = lax.dynamic_index_in_dim(value_all, head_index // group_size, 0, keepdims=False)
        scores = jnp.dot(query_one, key_one.T, preferred_element_type=jnp.float32) * score_scale
        scores = jnp.where(causal, scores, jnp.float32(-1e+30))
        row_max = lax.optimization_barrier(jnp.max(scores, axis=1, keepdims=True))
        weights = jnp.where(causal, jnp.exp(scores - row_max), jnp.float32(0.0))
        denom = lax.optimization_barrier(jnp.sum(weights, axis=1, keepdims=True))
        summed = jnp.dot(weights.astype(jnp.bfloat16), value_one, preferred_element_type=jnp.float32)
        return (summed / denom).astype(jnp.bfloat16)
    attended = lax.map(one_head, jnp.arange(HEADS, dtype=jnp.int32))
    attended = attended.transpose(1, 0, 2).reshape(TOKENS, HEADS * HEAD)
    stream = residual.astype(jnp.float32) + jnp.dot(attended, out_weight, preferred_element_type=jnp.float32)
    stream_bf = stream.astype(jnp.bfloat16)
    number_blocks = TOKENS // ROWS_DEV
    blocks, slot_index = slot_table(expert_ids)
    target = blocks * CAP + slot_index
    repeated = jnp.repeat(stream_bf.reshape(number_blocks, ROWS_DEV, D), TOP, axis=1)
    selector = (jnp.arange(EXPERTS * CAP, dtype=jnp.int32)[None, :, None] == target[:, None, :]).astype(jnp.float32)
    buffers = jnp.einsum('bsa,bad->bsd', selector, repeated.astype(jnp.float32), precision=lax.Precision.HIGHEST)
    expert_rows = buffers.astype(jnp.bfloat16).reshape(number_blocks, EXPERTS, CAP, D)
    expert_rows = expert_rows.transpose(1, 0, 2, 3).reshape(EXPERTS, number_blocks * CAP, D)
    slice_width = FF // N_CTX

    def one_expert(operands):
        rows_in, gate_one, up_one, down_one = operands
        widened = rows_in.astype(jnp.float32)
        scaled = (widened * norm_gain).astype(jnp.bfloat16)
        inverse = lax.rsqrt(lax.optimization_barrier(jnp.mean(widened * widened, axis=1)) + 1e-05)[:, None]
        gate_pre = jnp.dot(scaled, gate_one, preferred_element_type=jnp.float32) * inverse
        up_pre = jnp.dot(scaled, up_one, preferred_element_type=jnp.float32) * inverse
        active = (jax.nn.silu(gate_pre) * up_pre).astype(jnp.bfloat16)

        def add_slice(running, slice_index):
            part_in = lax.dynamic_slice_in_dim(active, slice_index * slice_width, slice_width, 1)
            part_weight = lax.dynamic_slice_in_dim(down_one, slice_index * slice_width, slice_width, 0)
            partial_value = jnp.dot(part_in, part_weight, preferred_element_type=jnp.float32).astype(jnp.bfloat16)
            return (running + partial_value.astype(jnp.float32), None)
        start_sum = jnp.zeros((number_blocks * CAP, D), jnp.float32)
        finished, _ = lax.scan(add_slice, start_sum, jnp.arange(N_CTX, dtype=jnp.int32))
        return finished
    expert_out = lax.map(one_expert, (expert_rows, gate_weight, up_weight, down_weight))
    lookup = blocks * (number_blocks * CAP) + jnp.arange(number_blocks, dtype=jnp.int32)[:, None] * CAP + slot_index
    picked = jnp.take(expert_out.reshape(EXPERTS * number_blocks * CAP, D), lookup.reshape(-1).astype(jnp.int32), axis=0)
    combined = lax.optimization_barrier(jnp.sum(picked.reshape(TOKENS, TOP, D) * expert_weights[:, :, None], axis=1))
    return (stream + combined).astype(jnp.bfloat16)
```

```python
import math

import jax
import jax.numpy as jnp
from jax import lax
from jax.sharding import Mesh
from jax.sharding import PartitionSpec as P

HEADS = 32
KV_HEADS = 8
HEAD = 128
D = 4096
TOP = 2
EXPERTS = 8
CAP = 6
CTX = ("x", "yh", "core")
PLANE = ("x", "yh")


def swap(value, axes):
    return lax.all_to_all(value, axes, split_axis=0, concat_axis=0, tiled=True)


def gather_ctx(value):
    plane = lax.axis_size(PLANE)
    spread = swap(jnp.broadcast_to(value[None], (plane,) + value.shape), PLANE)
    return lax.all_gather(spread, "core", axis=0, tiled=False)


def shards(
    queries,
    key_heads,
    value_heads,
    residual,
    out_weight,
    norm_gain,
    gate_weight,
    up_weight,
    down_weight,
    expert_ids,
    expert_weights,
):
    f32, bf16 = jnp.float32, jnp.bfloat16
    plane = lax.axis_size(PLANE)
    cores = lax.axis_size("core")
    exp_count = lax.axis_size("exp")
    hid_count = lax.axis_size("hid")
    ctx_count = plane * cores
    tok_rows = queries.shape[0]
    row_count = tok_rows // exp_count
    width_part = D // hid_count

    with jax.named_scope("kv_gather"):
        pieces = gather_ctx(jnp.concatenate([key_heads, value_heads], axis=1))
        pieces = pieces.reshape(ctx_count * tok_rows, 2 * HEAD)
        keys, values = pieces[:, :HEAD], pieces[:, HEAD:]
    with jax.named_scope("attention"):
        spot = lax.axis_index(CTX) * tok_rows + jnp.arange(tok_rows, dtype=jnp.int32)
        column = jnp.arange(ctx_count * tok_rows, dtype=jnp.int32)
        block, inside = column // tok_rows, column % tok_rows
        key_spot = ((block % plane) * cores + block // plane) * tok_rows + inside
        allowed = spot[:, None] >= key_spot[None, :]
        scores = lax.dot_general(queries, keys, (((1,), (1,)), ((), ())), preferred_element_type=f32)
        scores = jnp.where(allowed, scores * (1.0 / math.sqrt(HEAD)), -1e30)
        top = jnp.max(scores, axis=1, keepdims=True)
        weights = jnp.where(allowed, jnp.exp(scores - top), 0.0)
        denom = jnp.sum(weights, axis=1, keepdims=True)
        attended = jnp.dot(weights.astype(bf16), values, preferred_element_type=f32)
        attended = (attended / denom).astype(bf16)
    with jax.named_scope("projection"):
        projected = jnp.dot(attended, out_weight, preferred_element_type=f32).astype(bf16)
        partials = (
            projected.reshape(exp_count, row_count, hid_count, width_part)
            .transpose(0, 2, 1, 3)
            .reshape(exp_count * hid_count, row_count, width_part)
        )
        mixed = jnp.sum(swap(partials, ("exp", "hid")).astype(f32), axis=0)
        stream = residual.astype(f32) + mixed
        stream_bf = stream.astype(bf16)

    with jax.named_scope("routing"):
        assigned = row_count * TOP
        flat_ids = expert_ids.reshape(assigned)
        onehot = (flat_ids[:, None] == jnp.arange(EXPERTS, dtype=jnp.int32)[None, :]).astype(jnp.int32)
        slot_index = jnp.sum((jnp.cumsum(onehot, axis=0) - onehot) * onehot, axis=1)
        target = (flat_ids * CAP + slot_index).reshape(row_count, TOP)
        slots = jnp.arange(EXPERTS * CAP, dtype=jnp.int32)
        hits = target[:, :, None] == slots[None, None, :]
        selector = jnp.any(hits, axis=1).astype(bf16)
        mixer = jnp.sum(jnp.where(hits, expert_weights[:, :, None], 0.0), axis=1)
    with jax.named_scope("dispatch"):
        outgoing = lax.dot_general(
            selector, stream_bf, (((0,), (0,)), ((), ())), preferred_element_type=f32
        ).astype(bf16)
        arrived = swap(outgoing.reshape(exp_count, CAP, width_part), "exp")
        rows = gather_ctx(arrived.reshape(exp_count * CAP, width_part))
        total = ctx_count * exp_count * CAP
        rows = rows.reshape(total, width_part)

    with jax.named_scope("gate_up"):
        widened = rows.astype(f32)
        scaled = (widened * norm_gain).astype(bf16)
        square = jnp.sum(widened * widened, axis=1)
        high = square.astype(bf16)
        low = (square - high.astype(f32)).astype(bf16)
        ff_part = gate_weight.shape[2]
        piece = ff_part // hid_count
        norm_rows = total * 2 // (2 * piece)
        pad_rows = -(-norm_rows // 16) * 16
        tail = jnp.concatenate([high, low]).reshape(norm_rows, 2 * piece)
        tail = jnp.pad(tail, ((0, pad_rows - norm_rows), (0, 0)))
        gate = jnp.dot(scaled, gate_weight[0], preferred_element_type=f32).astype(bf16)
        up = jnp.dot(scaled, up_weight[0], preferred_element_type=f32).astype(bf16)
        outbound = jnp.stack(
            [
                jnp.concatenate(
                    [
                        jnp.concatenate(
                            [gate[:, h * piece : (h + 1) * piece], up[:, h * piece : (h + 1) * piece]], axis=1
                        ),
                        tail,
                    ],
                    axis=0,
                )
                for h in range(hid_count)
            ]
        )
        summed = jnp.sum(swap(outbound, "hid").astype(f32), axis=0)
        norms = summed[total : total + norm_rows].reshape(2, total)
        inverse = lax.rsqrt((norms[0] + norms[1]) / D + 1e-05)[:, None]
        gate_sum, up_sum = summed[:total, :piece], summed[:total, piece:]
        active = (jax.nn.silu(gate_sum * inverse) * (up_sum * inverse)).astype(bf16)
    with jax.named_scope("down"):
        active = lax.all_gather(active, "hid", axis=1, tiled=True)
        partial_out = jnp.dot(active, down_weight[0], preferred_element_type=f32).astype(bf16)
        back = swap(partial_out.reshape(cores, total // cores, width_part), "core")
        back = jnp.sum(back.astype(f32), axis=0).astype(bf16)
        back = swap(back.reshape(plane, exp_count * CAP, width_part), PLANE)
        back = jnp.sum(back.astype(f32), axis=0).astype(bf16)
        back = swap(back.reshape(exp_count, CAP, width_part), "exp")
        back = back.reshape(EXPERTS * CAP, width_part).astype(f32)
    with jax.named_scope("combine"):
        combined = jnp.dot(mixer, back, precision=lax.Precision.HIGHEST)
        return (stream + combined).astype(bf16)


def solution(mesh):
    ctx, exp, hid = mesh.devices.shape
    split = Mesh(mesh.devices.reshape(ctx // 4, 2, 2, exp, hid), CTX + ("exp", "hid"))
    return jax.shard_map(
        shards,
        mesh=split,
        in_specs=(
            P(CTX, ("exp", "hid")),
            P(CTX, "exp"),
            P(CTX, "exp"),
            P(CTX + ("exp",), "hid"),
            P(("exp", "hid"), None),
            P("hid"),
            P("exp", "hid", CTX),
            P("exp", "hid", CTX),
            P("exp", CTX, "hid"),
            P(CTX + ("exp",), None),
            P(CTX + ("exp",), None),
        ),
        out_specs=P(CTX + ("exp",), "hid"),
        check_vma=False,
    )
```

```python
import math

import jax
import jax.numpy as jnp
from jax import lax
from jax.sharding import Mesh
from jax.sharding import PartitionSpec as P

HEADS = 32
KV_HEADS = 8
HEAD = 128
D = 4096
TOP = 2
EXPERTS = 8
CAP = 6
CTX = ("x", "yh", "core")
PLANE = ("x", "yh")


def swap(value, axes):
    return lax.all_to_all(value, axes, split_axis=0, concat_axis=0, tiled=True)


def spread(value, axes):
    return swap(jnp.broadcast_to(value[None], (lax.axis_size(axes),) + value.shape), axes)


def both_cores(value):
    return value, lax.ppermute(value, "core", [(0, 1), (1, 0)])


def shards(
    queries,
    key_heads,
    value_heads,
    residual,
    out_weight,
    norm_gain,
    gate_weight,
    up_weight,
    down_weight,
    expert_ids,
    expert_weights,
):
    f32, bf16 = jnp.float32, jnp.bfloat16
    plane = lax.axis_size(PLANE)
    cores = lax.axis_size("core")
    exp_count = lax.axis_size("exp")
    hid_count = lax.axis_size("hid")
    ctx_count = plane * cores
    tok_rows = queries.shape[0]
    row_count = tok_rows // exp_count
    width_part = D // hid_count

    with jax.named_scope("kv_gather"):
        pieces = spread(jnp.concatenate([key_heads, value_heads], axis=1), PLANE)
        pieces = jnp.concatenate(both_cores(pieces), axis=0)
        pieces = pieces.reshape(ctx_count * tok_rows, 2 * HEAD)
        keys, values = pieces[:, :HEAD], pieces[:, HEAD:]
    with jax.named_scope("attention"):
        spot = lax.axis_index(CTX) * tok_rows + jnp.arange(tok_rows, dtype=jnp.int32)
        column = jnp.arange(ctx_count * tok_rows, dtype=jnp.int32)
        block, inside = column // tok_rows, column % tok_rows
        core = lax.axis_index("core") ^ (block // plane)
        key_spot = ((block % plane) * cores + core) * tok_rows + inside
        allowed = spot[:, None] >= key_spot[None, :]
        scores = lax.dot_general(queries, keys, (((1,), (1,)), ((), ())), preferred_element_type=f32)
        scores = jnp.where(allowed, scores * (1.0 / math.sqrt(HEAD)), -1e30)
        top = jnp.max(scores, axis=1, keepdims=True)
        weights = jnp.where(allowed, jnp.exp(scores - top), 0.0)
        denom = jnp.sum(weights, axis=1, keepdims=True)
        attended = jnp.dot(weights.astype(bf16), values, preferred_element_type=f32)
        attended = (attended / denom).astype(bf16)
    with jax.named_scope("projection"):
        projected = jnp.dot(attended, out_weight, preferred_element_type=f32).astype(bf16)
        partials = (
            projected.reshape(exp_count, row_count, hid_count, width_part)
            .transpose(2, 0, 1, 3)
            .reshape(hid_count * exp_count, row_count, width_part)
        )
        mixed = jnp.sum(swap(partials, ("hid", "exp")).astype(f32), axis=0)
        stream = residual.astype(f32) + mixed
        stream_bf = stream.astype(bf16)

    with jax.named_scope("routing"):
        assigned = row_count * TOP
        flat_ids = expert_ids.reshape(assigned)
        onehot = (flat_ids[:, None] == jnp.arange(EXPERTS, dtype=jnp.int32)[None, :]).astype(jnp.int32)
        slot_index = jnp.sum((jnp.cumsum(onehot, axis=0) - onehot) * onehot, axis=1)
        target = (flat_ids * CAP + slot_index).reshape(row_count, TOP)
        slots = jnp.arange(EXPERTS * CAP, dtype=jnp.int32)
        hits = target[:, :, None] == slots[None, None, :]
        selector = jnp.any(hits, axis=1).astype(bf16)
        mixer = jnp.sum(jnp.where(hits, expert_weights[:, :, None], 0.0), axis=1)
    with jax.named_scope("dispatch"):
        outgoing = lax.dot_general(
            selector, stream_bf, (((0,), (0,)), ((), ())), preferred_element_type=f32
        ).astype(bf16)
        outgoing = outgoing.reshape(1, exp_count, CAP, width_part)
        halves = lax.axis_size("yh")
        outgoing = jnp.broadcast_to(outgoing, (halves, exp_count, CAP, width_part))
        arrived = swap(outgoing.reshape(halves * exp_count, CAP, width_part), ("yh", "exp"))
        arrived = spread(arrived.reshape(halves * exp_count * CAP, width_part), "x")
        total = ctx_count * exp_count * CAP
        rows = jnp.concatenate(both_cores(arrived), axis=0).reshape(total, width_part)

    with jax.named_scope("gate_up"):
        widened = rows.astype(f32)
        scaled = (widened * norm_gain).astype(bf16)
        square = jnp.sum(widened * widened, axis=1)
        high = square.astype(bf16)
        low = (square - high.astype(f32)).astype(bf16)
        ff_part = gate_weight.shape[2]
        piece = ff_part // hid_count
        norm_rows = total * 2 // (2 * piece)
        pad_rows = -(-norm_rows // 16) * 16
        tail = jnp.concatenate([high, low]).reshape(norm_rows, 2 * piece)
        tail = jnp.pad(tail, ((0, pad_rows - norm_rows), (0, 0)))
        gate = jnp.dot(scaled, gate_weight[0], preferred_element_type=f32).astype(bf16)
        up = jnp.dot(scaled, up_weight[0], preferred_element_type=f32).astype(bf16)
        outbound = jnp.stack(
            [
                jnp.concatenate(
                    [
                        jnp.concatenate(
                            [gate[:, h * piece : (h + 1) * piece], up[:, h * piece : (h + 1) * piece]], axis=1
                        ),
                        tail,
                    ],
                    axis=0,
                )
                for h in range(hid_count)
            ]
        )
        summed = jnp.sum(swap(outbound, "hid").astype(f32), axis=0)
        norms = summed[total : total + norm_rows].reshape(2, total)
        inverse = lax.rsqrt((norms[0] + norms[1]) / D + 1e-05)[:, None]
        gate_sum, up_sum = summed[:total, :piece], summed[:total, piece:]
        active = (jax.nn.silu(gate_sum * inverse) * (up_sum * inverse)).astype(bf16)
    with jax.named_scope("down"):
        active = lax.all_gather(active, "hid", axis=1, tiled=True)
        partial_out = jnp.dot(active, down_weight[0], preferred_element_type=f32).astype(bf16)
        own, other = jnp.split(partial_out, 2, axis=0)
        other = lax.ppermute(other, "core", [(0, 1), (1, 0)])
        back = (own.astype(f32) + other.astype(f32)).astype(bf16)
        lines = lax.axis_size("x")
        back = swap(back.reshape(lines, total // cores // lines, width_part), "x")
        back = jnp.sum(back.astype(f32), axis=0).astype(bf16)
        back = swap(back.reshape(halves * exp_count, CAP, width_part), ("yh", "exp"))
        back = back.reshape(halves, EXPERTS * CAP, width_part).astype(f32)
        back = jnp.sum(back, axis=0)
    with jax.named_scope("combine"):
        combined = jnp.dot(mixer, back, precision=lax.Precision.HIGHEST)
        return (stream + combined).astype(bf16)


def solution(mesh):
    ctx, exp, hid = mesh.devices.shape
    split = Mesh(mesh.devices.reshape(ctx // 4, 2, 2, exp, hid), CTX + ("exp", "hid"))
    return jax.shard_map(
        shards,
        mesh=split,
        in_specs=(
            P(CTX, ("exp", "hid")),
            P(CTX, "exp"),
            P(CTX, "exp"),
            P(CTX + ("exp",), "hid"),
            P(("exp", "hid"), None),
            P("hid"),
            P("exp", "hid", CTX),
            P("exp", "hid", CTX),
            P("exp", CTX, "hid"),
            P(CTX + ("exp",), None),
            P(CTX + ("exp",), None),
        ),
        out_specs=P(CTX + ("exp",), "hid"),
        check_vma=False,
    )
```

```python
import math

import jax
import jax.numpy as jnp
from jax import lax
from jax.experimental import pallas as pl
from jax.experimental.pallas import tpu as pltpu
from jax.sharding import Mesh
from jax.sharding import PartitionSpec as P

HEADS = 32
KV_HEADS = 8
HEAD = 128
D = 4096
TOP = 2
EXPERTS = 8
CAP = 6
CTX = ("x", "yh", "core")
PLANE = ("x", "yh")
F32, BF16 = jnp.float32, jnp.bfloat16
TAIL = 16


def swap(value, axes):
    return lax.all_to_all(value, axes, split_axis=0, concat_axis=0, tiled=True)


def spread(value, axes):
    return swap(jnp.broadcast_to(value[None], (lax.axis_size(axes),) + value.shape), axes)


def other_core(value):
    return lax.ppermute(value, "core", [(0, 1), (1, 0)])


def whole(kernel, out_shapes, flops, smem=0):
    def call(*operands):
        spaces = [pltpu.SMEM] * smem + [pltpu.VMEM] * (len(operands) - smem)
        moved = sum(math.prod(a.shape) * a.dtype.itemsize for a in operands)
        moved += sum(math.prod(a.shape) * a.dtype.itemsize for a in out_shapes)
        return pl.pallas_call(
            kernel,
            out_shape=out_shapes,
            in_specs=[pl.BlockSpec(memory_space=space) for space in spaces],
            out_specs=[pl.BlockSpec(memory_space=pltpu.VMEM)] * len(out_shapes),
            compiler_params=pltpu.CompilerParams(vmem_limit_bytes=24 * 1024 * 1024),
            cost_estimate=pl.CostEstimate(flops=flops, bytes_accessed=moved, transcendentals=0),
        )(*operands)

    return call


def dot_nt(left, right):
    return lax.dot_general(left, right, (((1,), (1,)), ((), ())), preferred_element_type=F32)


def attention_kernel(place, query, near, far, weight, ids, shares, out, selector, mixer):
    ctx, core = place[0], place[1]
    rows, keys = query.shape[0], near.shape[0]
    spot = ctx * rows + lax.broadcasted_iota(jnp.int32, (rows, keys), 0)
    column = lax.broadcasted_iota(jnp.int32, (rows, keys), 1)
    base = (column // rows) * (2 * rows) + column % rows
    scores = []
    for half, source in enumerate((near, far)):
        key_spot = base + (core ^ half) * rows
        product = dot_nt(query[...], source[:, :HEAD]) * (1.0 / math.sqrt(HEAD))
        scores.append(jnp.where(spot >= key_spot, product, -1e30))
    top = jnp.maximum(*(jnp.max(score, axis=1, keepdims=True) for score in scores))
    denom, total = 0.0, 0.0
    for score, source in zip(scores, (near, far)):
        weights = jnp.exp(score - top)
        denom = denom + jnp.sum(weights, axis=1, keepdims=True)
        total = total + jnp.dot(weights.astype(BF16), source[:, HEAD:], preferred_element_type=F32)
    attended = (total / denom).astype(BF16)
    parts, _, width = out.shape
    for part in range(parts):
        columns = weight[:, part * width : (part + 1) * width]
        out[part] = jnp.dot(attended, columns, preferred_element_type=F32).astype(BF16)

    tokens, slots = mixer.shape
    lane = lax.broadcasted_iota(jnp.int32, (tokens, 128), 1)
    chosen = [ids[:, k : k + 1] for k in range(TOP)]
    named = [(lane == chosen[k]).astype(F32) for k in range(TOP)]
    earlier = lax.broadcasted_iota(jnp.int32, (tokens, tokens), 0) > lax.broadcasted_iota(
        jnp.int32, (tokens, tokens), 1
    )
    before = jnp.dot(earlier.astype(BF16), (named[0] + named[1]).astype(BF16), preferred_element_type=F32)
    slot_lane = lax.broadcasted_iota(jnp.int32, (tokens, slots), 1)
    mixed, picked = 0.0, 0.0
    for k in range(TOP):
        slot = jnp.sum(before * named[k], axis=1, keepdims=True).astype(jnp.int32)
        hit = (slot_lane == chosen[k] * CAP + slot).astype(F32)
        picked = picked + hit
        mixed = mixed + hit * shares[:, k : k + 1]
    selector[...] = picked.astype(BF16)
    mixer[...] = mixed


def gate_up_kernel(place, near, far, gain, gate, up, *outs):
    hid = place[0]
    piece = gate.shape[1] // len(outs)
    half = near.shape[0]
    ones = jnp.ones((8, near.shape[1]), BF16)
    sums = []
    for index, source in enumerate((near, far)):
        rows = source[...].astype(F32)
        scaled = (rows * gain[...]).astype(BF16)
        for k, out in enumerate(outs):
            start = pl.multiple_of((hid ^ k) * piece, piece)
            weight = jnp.concatenate([gate[:, pl.ds(start, piece)], up[:, pl.ds(start, piece)]], axis=1)
            product = jnp.dot(scaled, weight, preferred_element_type=F32)
            out[index * half : (index + 1) * half, :] = product.astype(BF16)
        square = rows * rows
        high = square.astype(BF16)
        low = (square - high.astype(F32)).astype(BF16)
        sums.append(dot_nt(ones, high) + dot_nt(ones, low))
    norm = jnp.concatenate(sums, axis=1)
    high = norm.astype(BF16).astype(F32)
    low = norm - high
    width = 2 * piece
    groups = norm.shape[1] // width
    line = lax.broadcasted_iota(jnp.int32, (8, width), 0)
    tail = jnp.zeros((8, width), F32)
    for group in range(groups):
        lanes = slice(group * width, (group + 1) * width)
        tail = jnp.where(line == group, high[:, lanes], tail)
        tail = jnp.where(line == group + groups, low[:, lanes], tail)
    tail = jnp.concatenate([tail, jnp.zeros((TAIL - 8, width), F32)], axis=0).astype(BF16)
    for out in outs:
        out[2 * half :, :] = tail


def active_kernel(*refs):
    parts, out = refs[:-1], refs[-1]
    total, piece = out.shape
    width = 2 * piece
    groups = total // width
    tail = sum(part[total:, :].astype(F32) for part in parts)
    for group in range(groups):
        norm = tail[group : group + 1, :] + tail[group + groups : group + groups + 1, :]
        inverse = lax.rsqrt(norm / D + 1e-05)
        inverse = jnp.broadcast_to(inverse, (piece, width)).T
        rows = slice(group * width, (group + 1) * width)
        summed = sum(part[rows, :].astype(F32) for part in parts)
        gate = summed[:, :piece] * inverse
        up = summed[:, piece:] * inverse
        out[rows, :] = (gate / (1.0 + jnp.exp(-gate)) * up).astype(BF16)


def down_kernel(active, weight, near, far):
    half = near.shape[0]
    for index, out in enumerate((near, far)):
        rows = slice(index * half, (index + 1) * half)
        left = jnp.concatenate([active[h, rows, :] for h in range(active.shape[0])], axis=1)
        out[...] = jnp.dot(left, weight[...], preferred_element_type=F32).astype(BF16)


def shards(
    queries,
    key_heads,
    value_heads,
    residual,
    out_weight,
    norm_gain,
    gate_weight,
    up_weight,
    down_weight,
    expert_ids,
    expert_weights,
):
    plane = lax.axis_size(PLANE)
    lines, halves = lax.axis_size("x"), lax.axis_size("yh")
    exp_count = lax.axis_size("exp")
    hid_count = lax.axis_size("hid")
    tok_rows = queries.shape[0]
    row_count = tok_rows // exp_count
    width_part = D // hid_count
    shape = jax.ShapeDtypeStruct

    with jax.named_scope("kv_gather"):
        near = spread(jnp.concatenate([key_heads, value_heads], axis=1), PLANE)
        near = near.reshape(plane * tok_rows, 2 * HEAD)
        far = other_core(near)
    with jax.named_scope("attention"):
        place = jnp.stack([lax.axis_index(CTX), lax.axis_index("core")]).astype(jnp.int32)
        partials, selector, mixer = whole(
            attention_kernel,
            [
                shape((hid_count, tok_rows, width_part), BF16),
                shape((row_count, EXPERTS * CAP), BF16),
                shape((row_count, EXPERTS * CAP), F32),
            ],
            flops=2 * tok_rows * HEAD * (4 * plane * tok_rows + D),
            smem=1,
        )(place, queries, near, far, out_weight, expert_ids, expert_weights)
    with jax.named_scope("projection"):
        partials = partials.reshape(hid_count * exp_count, row_count, width_part)
        mixed = jnp.sum(swap(partials, ("hid", "exp")).astype(F32), axis=0)
        stream = residual.astype(F32) + mixed
        stream_bf = stream.astype(BF16)

    with jax.named_scope("dispatch"):
        outgoing = lax.dot_general(
            selector, stream_bf, (((0,), (0,)), ((), ())), preferred_element_type=F32
        ).astype(BF16)
        outgoing = outgoing.reshape(1, exp_count, CAP, width_part)
        outgoing = jnp.broadcast_to(outgoing, (halves, exp_count, CAP, width_part))
        arrived = swap(outgoing.reshape(halves * exp_count, CAP, width_part), ("yh", "exp"))
        arrived = spread(arrived.reshape(halves * exp_count * CAP, width_part), "x")
        half = plane * exp_count * CAP
        total = 2 * half
        near = arrived.reshape(half, width_part)
        far = other_core(near)

    with jax.named_scope("gate_up"):
        ff_part = gate_weight.shape[2]
        piece = ff_part // hid_count
        parts = whole(
            gate_up_kernel,
            [shape((total + TAIL, 2 * piece), BF16)] * hid_count,
            flops=4 * total * width_part * ff_part,
            smem=1,
        )(
            lax.axis_index("hid").astype(jnp.int32).reshape(1),
            near,
            far,
            norm_gain.reshape(1, width_part),
            gate_weight[0],
            up_weight[0],
        )
        arrivals = [parts[0]]
        for k in reversed(range(1, hid_count)):
            arrivals.append(lax.ppermute(parts[k], "hid", [(h, h ^ k) for h in range(hid_count)]))
    with jax.named_scope("active"):
        (active,) = whole(active_kernel, [shape((total, piece), BF16)], flops=total * piece * 20)(*arrivals)
        active = lax.all_gather(active, "hid", axis=0, tiled=False)
    with jax.named_scope("down"):
        near, far = whole(
            down_kernel, [shape((half, width_part), BF16)] * 2, flops=2 * total * ff_part * width_part
        )(active, down_weight[0])
        far = other_core(far)
        back = (near.astype(F32) + far.astype(F32)).astype(BF16)
        back = swap(back.reshape(lines, half // lines, width_part), "x")
        back = jnp.sum(back.astype(F32), axis=0).astype(BF16)
        back = swap(back.reshape(halves * exp_count, CAP, width_part), ("yh", "exp"))
        back = back.reshape(halves, EXPERTS * CAP, width_part).astype(F32)
        back = jnp.sum(back, axis=0)
    with jax.named_scope("combine"):
        combined = jnp.dot(mixer, back, precision=lax.Precision.HIGHEST)
        return (stream + combined).astype(BF16)


def solution(mesh):
    ctx, exp, hid = mesh.devices.shape
    split = Mesh(mesh.devices.reshape(ctx // 4, 2, 2, exp, hid), CTX + ("exp", "hid"))
    return jax.shard_map(
        shards,
        mesh=split,
        in_specs=(
            P(CTX, ("exp", "hid")),
            P(CTX, "exp"),
            P(CTX, "exp"),
            P(CTX + ("exp",), "hid"),
            P(("exp", "hid"), None),
            P("hid"),
            P("exp", "hid", CTX),
            P("exp", "hid", CTX),
            P("exp", CTX, "hid"),
            P(CTX + ("exp",), None),
            P(CTX + ("exp",), None),
        ),
        out_specs=P(CTX + ("exp",), "hid"),
        check_vma=False,
    )
```

```python
import math

import jax
import jax.numpy as jnp
from jax import lax
from jax.experimental import pallas as pl
from jax.experimental.pallas import tpu as pltpu
from jax.sharding import Mesh
from jax.sharding import PartitionSpec as P

HEADS = 32
KV_HEADS = 8
HEAD = 128
D = 4096
TOP = 2
EXPERTS = 8
CAP = 6
CTX = ("x", "yh", "core")
PLANE = ("x", "yh")
F32, BF16 = jnp.float32, jnp.bfloat16
TAIL = 16


def swap(value, axes):
    return lax.all_to_all(value, axes, split_axis=0, concat_axis=0, tiled=True)


def spread(value, axes):
    return swap(jnp.broadcast_to(value[None], (lax.axis_size(axes),) + value.shape), axes)


def other_core(value):
    return lax.ppermute(value, "core", [(0, 1), (1, 0)])


def to_peer(value, offset):
    return lax.ppermute(value, "hid", [(h, h ^ offset) for h in range(lax.axis_size("hid"))])


def whole(kernel, out_shapes, flops, smem=0):
    def call(*operands):
        spaces = [pltpu.SMEM] * smem + [pltpu.VMEM] * (len(operands) - smem)
        moved = sum(math.prod(a.shape) * a.dtype.itemsize for a in operands)
        moved += sum(math.prod(a.shape) * a.dtype.itemsize for a in out_shapes)
        return pl.pallas_call(
            kernel,
            out_shape=out_shapes,
            in_specs=[pl.BlockSpec(memory_space=space) for space in spaces],
            out_specs=[pl.BlockSpec(memory_space=pltpu.VMEM)] * len(out_shapes),
            compiler_params=pltpu.CompilerParams(vmem_limit_bytes=24 * 1024 * 1024),
            cost_estimate=pl.CostEstimate(flops=flops, bytes_accessed=moved, transcendentals=0),
        )(*operands)

    return call


def dot_nt(left, right):
    return lax.dot_general(left, right, (((1,), (1,)), ((), ())), preferred_element_type=F32)


def attention_kernel(place, query, near, far, weight, ids, shares, out, selector, mixer):
    ctx, core = place[0], place[1]
    rows, keys = query.shape[0], near.shape[0]
    spot = ctx * rows + lax.broadcasted_iota(jnp.int32, (rows, keys), 0)
    column = lax.broadcasted_iota(jnp.int32, (rows, keys), 1)
    base = (column // rows) * (2 * rows) + column % rows
    scores = []
    for half, source in enumerate((near, far)):
        key_spot = base + (core ^ half) * rows
        product = dot_nt(query[...], source[:, :HEAD]) * (1.0 / math.sqrt(HEAD))
        scores.append(jnp.where(spot >= key_spot, product, -1e30))
    top = jnp.maximum(*(jnp.max(score, axis=1, keepdims=True) for score in scores))
    denom, total = 0.0, 0.0
    for score, source in zip(scores, (near, far)):
        weights = jnp.exp(score - top)
        denom = denom + jnp.sum(weights, axis=1, keepdims=True)
        total = total + jnp.dot(weights.astype(BF16), source[:, HEAD:], preferred_element_type=F32)
    attended = (total / denom).astype(BF16)
    parts, _, width = out.shape
    for part in range(parts):
        columns = weight[:, part * width : (part + 1) * width]
        out[part] = jnp.dot(attended, columns, preferred_element_type=F32).astype(BF16)

    tokens, slots = mixer.shape
    lane = lax.broadcasted_iota(jnp.int32, (tokens, 128), 1)
    chosen = [ids[:, k : k + 1] for k in range(TOP)]
    named = [(lane == chosen[k]).astype(F32) for k in range(TOP)]
    earlier = lax.broadcasted_iota(jnp.int32, (tokens, tokens), 0) > lax.broadcasted_iota(
        jnp.int32, (tokens, tokens), 1
    )
    before = jnp.dot(earlier.astype(BF16), (named[0] + named[1]).astype(BF16), preferred_element_type=F32)
    slot_lane = lax.broadcasted_iota(jnp.int32, (tokens, slots), 1)
    mixed, picked = 0.0, 0.0
    for k in range(TOP):
        slot = jnp.sum(before * named[k], axis=1, keepdims=True).astype(jnp.int32)
        hit = (slot_lane == chosen[k] * CAP + slot).astype(F32)
        picked = picked + hit
        mixed = mixed + hit * shares[:, k : k + 1]
    selector[...] = picked.astype(BF16)
    mixer[...] = mixed


def gate_up_kernel(place, rows, gain, weight, *refs):
    outs, scaled, product = refs[:-2], refs[-2], refs[-1]
    step, hid = pl.program_id(0), place[0]
    count, depth = rows.shape
    piece = outs[0].shape[1] // 2

    @pl.when(step == 0)
    def _():
        widened = rows[...].astype(F32)
        scaled[...] = (widened * gain[...]).astype(BF16)
        square = jnp.concatenate([widened * widened, jnp.zeros((128 - count, depth), F32)], axis=0)
        high = square.astype(BF16)
        low = (square - high.astype(F32)).astype(BF16)
        ones = jnp.ones((TAIL, depth), BF16)
        norm = dot_nt(ones, high) + dot_nt(ones, low)
        high = norm.astype(BF16).astype(F32)
        line = lax.broadcasted_iota(jnp.int32, (TAIL, 128), 0)
        tail = jnp.where(line == 0, high, jnp.where(line == 1, norm - high, 0.0)).astype(BF16)
        for out in outs:
            out[count:, :] = jnp.concatenate([tail, jnp.zeros((TAIL, 2 * piece - 128), BF16)], axis=1)

    @pl.when(step > 0)
    def _():
        for out in outs:
            out[count:, :] = jnp.zeros((TAIL, 2 * piece), BF16)

    product[...] = jnp.dot(scaled[...], weight[0], preferred_element_type=F32)
    for k, out in enumerate(outs):
        start = pl.multiple_of((hid ^ k) * piece, piece)
        other = pl.multiple_of((hid ^ k) * piece + len(outs) * piece, piece)
        out[:count, :piece] = product[:, pl.ds(start, piece)].astype(BF16)
        out[:count, piece:] = product[:, pl.ds(other, piece)].astype(BF16)


def gate_up(place, rows, gain, weight, peers):
    count, depth = rows.shape
    slices, _, columns = weight.shape
    share = columns // peers
    return pl.pallas_call(
        gate_up_kernel,
        out_shape=[jax.ShapeDtypeStruct((count + TAIL, slices * share), BF16)] * peers,
        grid=(slices,),
        in_specs=[
            pl.BlockSpec(memory_space=pltpu.SMEM),
            pl.BlockSpec((count, depth), lambda s: (0, 0)),
            pl.BlockSpec((1, depth), lambda s: (0, 0)),
            pl.BlockSpec((1, depth, columns), lambda s: (s, 0, 0)),
        ],
        out_specs=[pl.BlockSpec((count + TAIL, share), lambda s: (0, s))] * peers,
        scratch_shapes=[pltpu.VMEM((count, depth), BF16), pltpu.VMEM((count, columns), F32)],
        compiler_params=pltpu.CompilerParams(vmem_limit_bytes=52 * 1024 * 1024),
        cost_estimate=pl.CostEstimate(
            flops=2 * count * depth * columns * slices,
            bytes_accessed=2 * depth * columns * slices,
            transcendentals=0,
        ),
    )(place, rows, gain, weight)


def active_kernel(*refs):
    parts, out = refs[:-1], refs[-1]
    piece = out.shape[1]
    count = parts[0].shape[0] - TAIL
    tail = sum(part[count:, :piece].astype(F32) for part in parts)
    inverse = lax.rsqrt((tail[0:1, :] + tail[1:2, :]) / D + 1e-05)
    inverse = jnp.broadcast_to(inverse, (piece, piece)).T[:count, :]
    for index in range(out.shape[0] // count):
        start = 2 * index * piece
        gate = sum(part[:count, start : start + piece].astype(F32) for part in parts) * inverse
        up = sum(part[:count, start + piece : start + 2 * piece].astype(F32) for part in parts) * inverse
        out[index * count : (index + 1) * count, :] = (gate / (1.0 + jnp.exp(-gate)) * up).astype(BF16)


def down_kernel(place, *refs):
    parts, (weight, out, left, total) = refs[:-4], refs[-4:]
    step, hid = pl.program_id(0), place[0]
    piece = parts[0].shape[1]
    for k, part in enumerate(parts):
        left[:, pl.ds(pl.multiple_of((hid ^ k) * piece, piece), piece)] = part[...]
    product = jnp.dot(left[...], weight[0], preferred_element_type=F32)

    @pl.when(step == 0)
    def _():
        total[...] = product

    @pl.when(step > 0)
    def _():
        total[...] += product

    @pl.when(step == pl.num_programs(0) - 1)
    def _():
        out[...] = total[...].astype(BF16)


def down(place, parts, weight):
    rows, piece = parts[0].shape
    slices, depth, columns = weight.shape
    count = rows // slices
    return pl.pallas_call(
        down_kernel,
        out_shape=jax.ShapeDtypeStruct((count, columns), BF16),
        grid=(slices,),
        in_specs=[pl.BlockSpec(memory_space=pltpu.SMEM)]
        + [pl.BlockSpec((count, piece), lambda s: (s, 0))] * len(parts)
        + [pl.BlockSpec((1, depth, columns), lambda s: (s, 0, 0))],
        out_specs=pl.BlockSpec((count, columns), lambda s: (0, 0)),
        scratch_shapes=[pltpu.VMEM((count, depth), BF16), pltpu.VMEM((count, columns), F32)],
        compiler_params=pltpu.CompilerParams(vmem_limit_bytes=52 * 1024 * 1024),
        cost_estimate=pl.CostEstimate(
            flops=2 * count * depth * columns * slices,
            bytes_accessed=2 * depth * columns * slices,
            transcendentals=0,
        ),
    )(place, *parts, weight)


def shards(
    queries,
    key_heads,
    value_heads,
    residual,
    out_weight,
    norm_gain,
    gate_weight,
    up_weight,
    down_weight,
    expert_ids,
    expert_weights,
):
    plane = lax.axis_size(PLANE)
    halves = lax.axis_size("yh")
    exp_count = lax.axis_size("exp")
    hid_count = lax.axis_size("hid")
    tok_rows = queries.shape[0]
    row_count = tok_rows // exp_count
    width_part = D // hid_count
    shape = jax.ShapeDtypeStruct

    with jax.named_scope("weight_gather"):
        gate_up_weight = jnp.concatenate([gate_weight[0], up_weight[0]], axis=1)
        gate_up_weight = lax.all_gather(gate_up_weight, ("x", "core"), axis=0, tiled=False)
        down_all = lax.all_gather(down_weight[0], ("x", "core"), axis=0, tiled=False)
    with jax.named_scope("kv_gather"):
        near = spread(jnp.concatenate([key_heads, value_heads], axis=1), PLANE)
        near = near.reshape(plane * tok_rows, 2 * HEAD)
        far = other_core(near)
    with jax.named_scope("attention"):
        place = jnp.stack([lax.axis_index(CTX), lax.axis_index("core")]).astype(jnp.int32)
        partials, selector, mixer = whole(
            attention_kernel,
            [
                shape((hid_count, tok_rows, width_part), BF16),
                shape((row_count, EXPERTS * CAP), BF16),
                shape((row_count, EXPERTS * CAP), F32),
            ],
            flops=2 * tok_rows * HEAD * (4 * plane * tok_rows + D),
            smem=1,
        )(place, queries, near, far, out_weight, expert_ids, expert_weights)
    with jax.named_scope("projection"):
        partials = partials.reshape(hid_count * exp_count, row_count, width_part)
        mixed = jnp.sum(swap(partials, ("hid", "exp")).astype(F32), axis=0)
        stream = residual.astype(F32) + mixed
        stream_bf = stream.astype(BF16)

    with jax.named_scope("dispatch"):
        outgoing = lax.dot_general(
            selector, stream_bf, (((0,), (0,)), ((), ())), preferred_element_type=F32
        ).astype(BF16)
        outgoing = outgoing.reshape(1, exp_count, CAP, width_part)
        outgoing = jnp.broadcast_to(outgoing, (halves, exp_count, CAP, width_part))
        arrived = swap(outgoing.reshape(halves * exp_count, CAP, width_part), ("yh", "exp"))
        rows = arrived.reshape(halves * exp_count * CAP, width_part)

    with jax.named_scope("gate_up"):
        spot = lax.axis_index("hid").astype(jnp.int32).reshape(1)
        parts = gate_up(spot, rows, norm_gain.reshape(1, width_part), gate_up_weight, hid_count)
        arrivals = [parts[0]] + [to_peer(parts[k], k) for k in reversed(range(1, hid_count))]
    with jax.named_scope("active"):
        piece = down_weight.shape[1] // hid_count
        count = rows.shape[0] * gate_up_weight.shape[0]
        (active,) = whole(active_kernel, [shape((count, piece), BF16)], flops=count * piece * 20)(*arrivals)
        actives = {0: active} | {k: to_peer(active, k) for k in reversed(range(1, hid_count))}
    with jax.named_scope("down"):
        back = down(spot, [actives[k] for k in range(hid_count)], down_all)
        back = swap(back.reshape(halves * exp_count, CAP, width_part), ("yh", "exp"))
        back = back.reshape(halves, EXPERTS * CAP, width_part).astype(F32)
        back = jnp.sum(back, axis=0)
    with jax.named_scope("combine"):
        combined = jnp.dot(mixer, back, precision=lax.Precision.HIGHEST)
        return (stream + combined).astype(BF16)


def solution(mesh):
    ctx, exp, hid = mesh.devices.shape
    split = Mesh(mesh.devices.reshape(ctx // 4, 2, 2, exp, hid), CTX + ("exp", "hid"))
    return jax.shard_map(
        shards,
        mesh=split,
        in_specs=(
            P(CTX, ("exp", "hid")),
            P(CTX, "exp"),
            P(CTX, "exp"),
            P(CTX + ("exp",), "hid"),
            P(("exp", "hid"), None),
            P("hid"),
            P("exp", "hid", CTX),
            P("exp", "hid", CTX),
            P("exp", CTX, "hid"),
            P(CTX + ("exp",), None),
            P(CTX + ("exp",), None),
        ),
        out_specs=P(CTX + ("exp",), "hid"),
        check_vma=False,
    )
```

```python
import math

import jax
import jax.numpy as jnp
from jax import lax
from jax.experimental import pallas as pl
from jax.experimental.pallas import tpu as pltpu
from jax.sharding import Mesh
from jax.sharding import PartitionSpec as P

HEADS = 32
KV_HEADS = 8
HEAD = 128
D = 4096
TOP = 2
EXPERTS = 8
CAP = 6
CTX = ("x", "yh", "core")
PLANE = ("x", "yh")
F32, BF16 = jnp.float32, jnp.bfloat16
TAIL = 16


def swap(value, axes):
    return lax.all_to_all(value, axes, split_axis=0, concat_axis=0, tiled=True)


def spread(value, axes):
    return swap(jnp.broadcast_to(value[None], (lax.axis_size(axes),) + value.shape), axes)


def other_core(value):
    return lax.ppermute(value, "core", [(0, 1), (1, 0)])


def whole(kernel, out_shapes, flops, smem=0, held=(0, 0), scratch=()):
    def call(*operands):
        spaces = [pltpu.SMEM] * smem + [pltpu.VMEM] * (len(operands) - smem - held[0]) + [pl.ANY] * held[0]
        out_spaces = [pltpu.VMEM] * (len(out_shapes) - held[1]) + [pl.ANY] * held[1]
        moved = sum(math.prod(a.shape) * a.dtype.itemsize for a in operands)
        moved += sum(math.prod(a.shape) * a.dtype.itemsize for a in out_shapes)
        return pl.pallas_call(
            kernel,
            out_shape=out_shapes,
            in_specs=[pl.BlockSpec(memory_space=space) for space in spaces],
            out_specs=[pl.BlockSpec(memory_space=space) for space in out_spaces],
            scratch_shapes=scratch,
            compiler_params=pltpu.CompilerParams(vmem_limit_bytes=24 * 1024 * 1024),
            cost_estimate=pl.CostEstimate(flops=flops, bytes_accessed=moved, transcendentals=0),
        )(*operands)

    return call


def dot_nt(left, right):
    return lax.dot_general(left, right, (((1,), (1,)), ((), ())), preferred_element_type=F32)


def attention_kernel(
    place, query, near, far, weight, ids, shares, gate, up, down, out, selector, mixer, gate_up, down_out, sems
):
    columns = gate.shape[1]
    copies = [
        pltpu.make_async_copy(gate, gate_up.at[:, pl.ds(0, columns)], sems.at[0]),
        pltpu.make_async_copy(up, gate_up.at[:, pl.ds(columns, columns)], sems.at[1]),
        pltpu.make_async_copy(down, down_out, sems.at[2]),
    ]
    for copy in copies:
        copy.start()
    ctx, core = place[0], place[1]
    rows, keys = query.shape[0], near.shape[0]
    spot = ctx * rows + lax.broadcasted_iota(jnp.int32, (rows, keys), 0)
    column = lax.broadcasted_iota(jnp.int32, (rows, keys), 1)
    base = (column // rows) * (2 * rows) + column % rows
    scores = []
    for half, source in enumerate((near, far)):
        key_spot = base + (core ^ half) * rows
        product = dot_nt(query[...], source[:, :HEAD]) * (1.0 / math.sqrt(HEAD))
        scores.append(jnp.where(spot >= key_spot, product, -1e30))
    top = jnp.maximum(*(jnp.max(score, axis=1, keepdims=True) for score in scores))
    denom, total = 0.0, 0.0
    for score, source in zip(scores, (near, far)):
        weights = jnp.exp(score - top)
        denom = denom + jnp.sum(weights, axis=1, keepdims=True)
        total = total + jnp.dot(weights.astype(BF16), source[:, HEAD:], preferred_element_type=F32)
    attended = (total / denom).astype(BF16)
    parts, _, width = out.shape
    for part in range(parts):
        columns = weight[:, part * width : (part + 1) * width]
        out[part] = jnp.dot(attended, columns, preferred_element_type=F32).astype(BF16)

    tokens, slots = mixer.shape
    lane = lax.broadcasted_iota(jnp.int32, (tokens, 128), 1)
    chosen = [ids[:, k : k + 1] for k in range(TOP)]
    named = [(lane == chosen[k]).astype(F32) for k in range(TOP)]
    earlier = lax.broadcasted_iota(jnp.int32, (tokens, tokens), 0) > lax.broadcasted_iota(
        jnp.int32, (tokens, tokens), 1
    )
    before = jnp.dot(earlier.astype(BF16), (named[0] + named[1]).astype(BF16), preferred_element_type=F32)
    slot_lane = lax.broadcasted_iota(jnp.int32, (tokens, slots), 1)
    mixed, picked = 0.0, 0.0
    for k in range(TOP):
        slot = jnp.sum(before * named[k], axis=1, keepdims=True).astype(jnp.int32)
        hit = (slot_lane == chosen[k] * CAP + slot).astype(F32)
        picked = picked + hit
        mixed = mixed + hit * shares[:, k : k + 1]
    selector[...] = picked.astype(BF16)
    mixer[...] = mixed
    for copy in copies:
        copy.wait()


def gate_up_kernel(place, rows, gain, near, far, *outs):
    hid = place[0]
    count, depth = rows.shape
    piece = outs[0].shape[1] // 4
    widened = rows[...].astype(F32)
    scaled = (widened * gain[...]).astype(BF16)
    for k, out in enumerate(outs):
        start = pl.multiple_of((hid ^ k) * piece, piece)
        other = pl.multiple_of((hid ^ k) * piece + len(outs) * piece, piece)
        for index, weight in enumerate((near, far)):
            columns = jnp.concatenate([weight[:, pl.ds(start, piece)], weight[:, pl.ds(other, piece)]], axis=1)
            product = jnp.dot(scaled, columns, preferred_element_type=F32)
            out[:count, 2 * index * piece : 2 * (index + 1) * piece] = product.astype(BF16)
    square = widened * widened
    high = square.astype(BF16)
    low = (square - high.astype(F32)).astype(BF16)
    ones = jnp.ones((TAIL, depth), BF16)
    norm = dot_nt(ones, high) + dot_nt(ones, low)
    high = norm.astype(BF16).astype(F32)
    line = lax.broadcasted_iota(jnp.int32, norm.shape, 0)
    tail = jnp.where(line == 0, high, jnp.where(line == 1, norm - high, 0.0)).astype(BF16)
    tail = jnp.concatenate([tail, jnp.zeros((TAIL, 4 * piece - count), BF16)], axis=1)
    for out in outs:
        out[count:, :] = tail


def active_kernel(*refs):
    parts, out = refs[:-1], refs[-1]
    piece = out.shape[1]
    count = parts[0].shape[0] - TAIL
    tail = sum(part[count:, :].astype(F32) for part in parts)
    inverse = lax.rsqrt((tail[0:1, :] + tail[1:2, :]) / D + 1e-05)
    for group in range(count // piece):
        first = group * piece
        factor = jnp.broadcast_to(inverse[:, first : first + piece], (piece, piece)).T
        summed = sum(part[first : first + piece, :].astype(F32) for part in parts)
        for index in range(out.shape[0] // count):
            gate = summed[:, 2 * index * piece : (2 * index + 1) * piece] * factor
            up = summed[:, (2 * index + 1) * piece : 2 * (index + 1) * piece] * factor
            active = (gate / (1.0 + jnp.exp(-gate)) * up).astype(BF16)
            out[index * count + first : index * count + first + piece, :] = active


def down_kernel(active, near, far, out):
    count = out.shape[0]
    total = 0.0
    for index, weight in enumerate((near, far)):
        rows = slice(index * count, (index + 1) * count)
        left = jnp.concatenate([active[h, rows, :] for h in range(active.shape[0])], axis=1)
        total = total + jnp.dot(left, weight[...], preferred_element_type=F32)
    out[...] = total.astype(BF16)


def shards(
    queries,
    key_heads,
    value_heads,
    residual,
    out_weight,
    norm_gain,
    gate_weight,
    up_weight,
    down_weight,
    expert_ids,
    expert_weights,
):
    plane = lax.axis_size(PLANE)
    lines, halves = lax.axis_size("x"), lax.axis_size("yh")
    exp_count = lax.axis_size("exp")
    hid_count = lax.axis_size("hid")
    tok_rows = queries.shape[0]
    row_count = tok_rows // exp_count
    width_part = D // hid_count
    ff_part = gate_weight.shape[2]
    piece = ff_part // hid_count
    shape = jax.ShapeDtypeStruct

    with jax.named_scope("kv_gather"):
        near = spread(jnp.concatenate([key_heads, value_heads], axis=1), PLANE)
        near = near.reshape(plane * tok_rows, 2 * HEAD)
        far = other_core(near)
    with jax.named_scope("attention"):
        place = jnp.stack([lax.axis_index(CTX), lax.axis_index("core")]).astype(jnp.int32)
        partials, selector, mixer, gate_up_near, down_near = whole(
            attention_kernel,
            [
                shape((hid_count, tok_rows, width_part), BF16),
                shape((row_count, EXPERTS * CAP), BF16),
                shape((row_count, EXPERTS * CAP), F32),
                shape((width_part, 2 * ff_part), BF16),
                shape((ff_part, width_part), BF16),
            ],
            flops=2 * tok_rows * HEAD * (4 * plane * tok_rows + D),
            smem=1,
            held=(3, 2),
            scratch=[pltpu.SemaphoreType.DMA((3,))],
        )(
            place,
            queries,
            near,
            far,
            out_weight,
            expert_ids,
            expert_weights,
            gate_weight[0],
            up_weight[0],
            down_weight[0],
        )
        gate_up_far, down_far = other_core(gate_up_near), other_core(down_near)
    with jax.named_scope("projection"):
        partials = partials.reshape(hid_count * exp_count, row_count, width_part)
        mixed = jnp.sum(swap(partials, ("hid", "exp")).astype(F32), axis=0)
        stream = residual.astype(F32) + mixed
        stream_bf = stream.astype(BF16)

    with jax.named_scope("dispatch"):
        outgoing = lax.dot_general(
            selector, stream_bf, (((0,), (0,)), ((), ())), preferred_element_type=F32
        ).astype(BF16)
        outgoing = outgoing.reshape(1, exp_count, CAP, width_part)
        outgoing = jnp.broadcast_to(outgoing, (halves, exp_count, CAP, width_part))
        arrived = swap(outgoing.reshape(halves * exp_count, CAP, width_part), ("yh", "exp"))
        arrived = spread(arrived.reshape(halves * exp_count * CAP, width_part), "x")
        count = lines * halves * exp_count * CAP
        rows = arrived.reshape(count, width_part)

    with jax.named_scope("gate_up"):
        parts = whole(
            gate_up_kernel,
            [shape((count + TAIL, 4 * piece), BF16)] * hid_count,
            flops=8 * count * width_part * ff_part,
            smem=1,
        )(
            lax.axis_index("hid").astype(jnp.int32).reshape(1),
            rows,
            norm_gain.reshape(1, width_part),
            gate_up_near,
            gate_up_far,
        )
        arrivals = [parts[0]]
        for k in reversed(range(1, hid_count)):
            arrivals.append(lax.ppermute(parts[k], "hid", [(h, h ^ k) for h in range(hid_count)]))
    with jax.named_scope("active"):
        (active,) = whole(active_kernel, [shape((2 * count, piece), BF16)], flops=count * piece * 40)(*arrivals)
        active = lax.all_gather(active, "hid", axis=0, tiled=False)
    with jax.named_scope("down"):
        (back,) = whole(
            down_kernel, [shape((count, width_part), BF16)], flops=4 * count * ff_part * width_part
        )(active, down_near, down_far)
        back = swap(back.reshape(lines, count // lines, width_part), "x")
        back = jnp.sum(back.astype(F32), axis=0).astype(BF16)
        back = swap(back.reshape(halves * exp_count, CAP, width_part), ("yh", "exp"))
        back = back.reshape(halves, EXPERTS * CAP, width_part).astype(F32)
        back = jnp.sum(back, axis=0)
    with jax.named_scope("combine"):
        combined = jnp.dot(mixer, back, precision=lax.Precision.HIGHEST)
        return (stream + combined).astype(BF16)


def solution(mesh):
    ctx, exp, hid = mesh.devices.shape
    split = Mesh(mesh.devices.reshape(ctx // 4, 2, 2, exp, hid), CTX + ("exp", "hid"))
    return jax.shard_map(
        shards,
        mesh=split,
        in_specs=(
            P(CTX, ("exp", "hid")),
            P(CTX, "exp"),
            P(CTX, "exp"),
            P(CTX + ("exp",), "hid"),
            P(("exp", "hid"), None),
            P("hid"),
            P("exp", "hid", CTX),
            P("exp", "hid", CTX),
            P("exp", CTX, "hid"),
            P(CTX + ("exp",), None),
            P(CTX + ("exp",), None),
        ),
        out_specs=P(CTX + ("exp",), "hid"),
        check_vma=False,
    )
```

```python
import math

import jax
import jax.numpy as jnp
from jax import lax
from jax.experimental import pallas as pl
from jax.experimental.pallas import tpu as pltpu
from jax.sharding import Mesh
from jax.sharding import PartitionSpec as P

HEADS = 32
KV_HEADS = 8
HEAD = 128
D = 4096
TOP = 2
EXPERTS = 8
CAP = 6
CTX = ("x", "yh", "core")
PLANE = ("x", "yh")
F32, BF16 = jnp.float32, jnp.bfloat16
TAIL = 16


def swap(value, axes):
    return lax.all_to_all(value, axes, split_axis=0, concat_axis=0, tiled=True)


def spread(value, axes):
    return swap(jnp.broadcast_to(value[None], (lax.axis_size(axes),) + value.shape), axes)


def other_core(value):
    return lax.ppermute(value, "core", [(0, 1), (1, 0)])


def whole(kernel, out_shapes, flops, smem=0, held=(0, 0), space=pl.ANY, scratch=(), vmem=24):
    def call(*operands):
        spaces = [pltpu.SMEM] * smem + [pltpu.VMEM] * (len(operands) - smem - held[0]) + [space] * held[0]
        out_spaces = [pltpu.VMEM] * (len(out_shapes) - held[1]) + [space] * held[1]
        moved = sum(math.prod(a.shape) * a.dtype.itemsize for a in operands)
        moved += sum(math.prod(a.shape) * a.dtype.itemsize for a in out_shapes)
        return pl.pallas_call(
            kernel,
            out_shape=out_shapes,
            in_specs=[pl.BlockSpec(memory_space=each) for each in spaces],
            out_specs=[pl.BlockSpec(memory_space=each) for each in out_spaces],
            scratch_shapes=scratch,
            compiler_params=pltpu.CompilerParams(vmem_limit_bytes=vmem * 1024 * 1024),
            cost_estimate=pl.CostEstimate(flops=flops, bytes_accessed=moved, transcendentals=0),
        )(*operands)

    return call


def dot_nt(left, right):
    return lax.dot_general(left, right, (((1,), (1,)), ((), ())), preferred_element_type=F32)


def attention_kernel(place, query, near, far, weight, ids, shares, out, selector, mixer):
    ctx, core = place[0], place[1]
    rows, keys = query.shape[0], near.shape[0]
    spot = ctx * rows + lax.broadcasted_iota(jnp.int32, (rows, keys), 0)
    column = lax.broadcasted_iota(jnp.int32, (rows, keys), 1)
    base = (column // rows) * (2 * rows) + column % rows
    scores = []
    for half, source in enumerate((near, far)):
        key_spot = base + (core ^ half) * rows
        product = dot_nt(query[...], source[:, :HEAD]) * (1.0 / math.sqrt(HEAD))
        scores.append(jnp.where(spot >= key_spot, product, -1e30))
    top = jnp.maximum(*(jnp.max(score, axis=1, keepdims=True) for score in scores))
    denom, total = 0.0, 0.0
    for score, source in zip(scores, (near, far)):
        weights = jnp.exp(score - top)
        denom = denom + jnp.sum(weights, axis=1, keepdims=True)
        total = total + jnp.dot(weights.astype(BF16), source[:, HEAD:], preferred_element_type=F32)
    attended = (total / denom).astype(BF16)
    parts, _, width = out.shape
    for part in range(parts):
        columns = weight[:, part * width : (part + 1) * width]
        out[part] = jnp.dot(attended, columns, preferred_element_type=F32).astype(BF16)

    slots, tokens = mixer.shape
    expert = lax.broadcasted_iota(jnp.int32, (EXPERTS, tokens), 0)
    named = [(expert == ids[k : k + 1, :]).astype(F32) for k in range(TOP)]
    later = lax.broadcasted_iota(jnp.int32, (tokens, tokens), 0) < lax.broadcasted_iota(
        jnp.int32, (tokens, tokens), 1
    )
    before = jnp.dot((named[0] + named[1]).astype(BF16), later.astype(BF16), preferred_element_type=F32)
    line = lax.broadcasted_iota(jnp.int32, (slots, tokens), 0)
    mixed, picked = 0.0, 0.0
    for k in range(TOP):
        slot = jnp.sum(before * named[k], axis=0, keepdims=True).astype(jnp.int32)
        hit = (line == ids[k : k + 1, :] * CAP + slot).astype(F32)
        picked = picked + hit
        mixed = mixed + hit * shares[k : k + 1, :]
    selector[...] = picked.astype(BF16)
    mixer[...] = mixed


def stack_kernel(gate, up, down, after, out, sems):
    depth, columns = gate.shape
    copies = [
        pltpu.make_async_copy(gate, out.at[pl.ds(0, depth), pl.ds(0, columns)], sems.at[0]),
        pltpu.make_async_copy(up, out.at[pl.ds(0, depth), pl.ds(columns, columns)], sems.at[1]),
        pltpu.make_async_copy(down, out.at[pl.ds(depth, columns), :], sems.at[2]),
    ]
    for copy in copies:
        copy.start()
    for copy in copies:
        copy.wait()


def select_kernel(arrived, residual, selector, weights, stream, outgoing):
    mixed = sum(arrived[index].astype(F32) for index in range(arrived.shape[0]))
    total = residual[...].astype(F32) + mixed
    stream[...] = total
    rows = jnp.dot(selector[...], total.astype(BF16), preferred_element_type=F32)
    halves, experts, slots, _ = outgoing.shape
    for expert in range(experts):
        part = rows[expert * slots : (expert + 1) * slots, :].astype(BF16)
        for half in range(halves):
            outgoing[half, expert] = part


def gate_up_kernel(place, rows, gain, gate_near, up_near, weights, *outs):
    hid = place[0]
    count, depth = rows.shape
    piece = outs[0].shape[1] // 4
    columns = gate_near.shape[1]
    gate_far, up_far = weights.at[:depth, :columns], weights.at[:depth, columns:]
    widened = rows[...].astype(F32)
    scaled = (widened * gain[...]).astype(BF16)
    for k, out in enumerate(outs):
        start = pl.multiple_of((hid ^ k) * piece, piece)
        for index, (gate, up) in enumerate(((gate_near, up_near), (gate_far, up_far))):
            weight = jnp.concatenate([gate[:, pl.ds(start, piece)], up[:, pl.ds(start, piece)]], axis=1)
            product = jnp.dot(scaled, weight, preferred_element_type=F32)
            out[:count, 2 * index * piece : 2 * (index + 1) * piece] = product.astype(BF16)
    square = widened * widened
    high = square.astype(BF16)
    low = (square - high.astype(F32)).astype(BF16)
    ones = jnp.ones((TAIL, depth), BF16)
    norm = dot_nt(ones, high) + dot_nt(ones, low)
    high = norm.astype(BF16).astype(F32)
    line = lax.broadcasted_iota(jnp.int32, norm.shape, 0)
    tail = jnp.where(line == 0, high, jnp.where(line == 1, norm - high, 0.0)).astype(BF16)
    tail = jnp.concatenate([tail, jnp.zeros((TAIL, 4 * piece - count), BF16)], axis=1)
    for out in outs:
        out[count:, :] = tail


def active_kernel(*refs):
    parts, out = refs[:-1], refs[-1]
    piece = out.shape[1]
    count = parts[0].shape[0] - TAIL
    tail = sum(part[count:, :].astype(F32) for part in parts)
    inverse = lax.rsqrt((tail[0:1, :] + tail[1:2, :]) / D + 1e-05)
    for group in range(count // piece):
        first = group * piece
        factor = jnp.broadcast_to(inverse[:, first : first + piece], (piece, piece)).T
        summed = sum(part[first : first + piece, :].astype(F32) for part in parts)
        for index in range(out.shape[0] // count):
            gate = summed[:, 2 * index * piece : (2 * index + 1) * piece] * factor
            up = summed[:, (2 * index + 1) * piece : 2 * (index + 1) * piece] * factor
            active = (gate / (1.0 + jnp.exp(-gate)) * up).astype(BF16)
            out[index * count + first : index * count + first + piece, :] = active


def down_kernel(active, near, weights, out):
    count = out.shape[0]
    far = weights.at[weights.shape[0] - near.shape[0] :, :]
    total = 0.0
    for index, weight in enumerate((near, far)):
        rows = slice(index * count, (index + 1) * count)
        left = jnp.concatenate([active[h, rows, :] for h in range(active.shape[0])], axis=1)
        total = total + jnp.dot(left, weight[...], preferred_element_type=F32)
    out[...] = total.astype(BF16)


def shards(
    queries,
    key_heads,
    value_heads,
    residual,
    out_weight,
    norm_gain,
    gate_weight,
    up_weight,
    down_weight,
    expert_ids,
    expert_weights,
):
    plane = lax.axis_size(PLANE)
    lines, halves = lax.axis_size("x"), lax.axis_size("yh")
    exp_count = lax.axis_size("exp")
    hid_count = lax.axis_size("hid")
    tok_rows = queries.shape[0]
    row_count = tok_rows // exp_count
    width_part = D // hid_count
    ff_part = gate_weight.shape[2]
    piece = ff_part // hid_count
    shape = jax.ShapeDtypeStruct

    with jax.named_scope("kv_gather"):
        near = spread(jnp.concatenate([key_heads, value_heads], axis=1), PLANE)
        near = near.reshape(plane * tok_rows, 2 * HEAD)
        far = other_core(near)
    with jax.named_scope("attention"):
        place = jnp.stack([lax.axis_index(CTX), lax.axis_index("core")]).astype(jnp.int32)
        partials, selector, mixer = whole(
            attention_kernel,
            [
                shape((hid_count, tok_rows, width_part), BF16),
                shape((EXPERTS * CAP, row_count), BF16),
                shape((EXPERTS * CAP, row_count), F32),
            ],
            flops=2 * tok_rows * HEAD * (4 * plane * tok_rows + D),
            smem=1,
        )(place, queries, near, far, out_weight, expert_ids.T, expert_weights.T)
    with jax.named_scope("weight_exchange"):
        (weights,) = whole(
            stack_kernel,
            [shape((width_part + ff_part, width_part), BF16)],
            flops=0,
            held=(4, 1),
            scratch=[pltpu.SemaphoreType.DMA((3,))],
            vmem=58,
        )(gate_weight[0], up_weight[0], down_weight[0], selector)
        weights = other_core(weights)
    with jax.named_scope("projection"):
        arrived = swap(partials.reshape(hid_count * exp_count, row_count, width_part), ("hid", "exp"))
        stream, outgoing = whole(
            select_kernel,
            [shape((row_count, width_part), F32), shape((halves, exp_count, CAP, width_part), BF16)],
            flops=2 * arrived.size,
            held=(1, 0),
        )(arrived, residual, selector, weights)

    with jax.named_scope("dispatch"):
        arrived = swap(outgoing.reshape(halves * exp_count, CAP, width_part), ("yh", "exp"))
        arrived = spread(arrived.reshape(halves * exp_count * CAP, width_part), "x")
        count = lines * halves * exp_count * CAP
        rows = arrived.reshape(count, width_part)

    with jax.named_scope("gate_up"):
        parts = whole(
            gate_up_kernel,
            [shape((count + TAIL, 4 * piece), BF16)] * hid_count,
            flops=8 * count * width_part * ff_part,
            smem=1,
        )(
            lax.axis_index("hid").astype(jnp.int32).reshape(1),
            rows,
            norm_gain.reshape(1, width_part),
            gate_weight[0],
            up_weight[0],
            weights,
        )
        arrivals = [parts[0]]
        for k in reversed(range(1, hid_count)):
            arrivals.append(lax.ppermute(parts[k], "hid", [(h, h ^ k) for h in range(hid_count)]))
    with jax.named_scope("active"):
        (active,) = whole(active_kernel, [shape((2 * count, piece), BF16)], flops=count * piece * 40)(*arrivals)
        active = lax.all_gather(active, "hid", axis=0, tiled=False)
    with jax.named_scope("down"):
        (back,) = whole(
            down_kernel, [shape((count, width_part), BF16)], flops=4 * count * ff_part * width_part
        )(active, down_weight[0], weights)
        back = swap(back.reshape(lines, count // lines, width_part), "x")
        back = jnp.sum(back.astype(F32), axis=0).astype(BF16)
        back = swap(back.reshape(halves * exp_count, CAP, width_part), ("yh", "exp"))
        back = back.reshape(halves, EXPERTS * CAP, width_part).astype(F32)
        back = jnp.sum(back, axis=0)
    with jax.named_scope("combine"):
        combined = lax.dot_general(mixer, back, (((0,), (0,)), ((), ())), precision=lax.Precision.HIGHEST)
        return (stream + combined).astype(BF16)


def solution(mesh):
    ctx, exp, hid = mesh.devices.shape
    split = Mesh(mesh.devices.reshape(ctx // 4, 2, 2, exp, hid), CTX + ("exp", "hid"))
    return jax.shard_map(
        shards,
        mesh=split,
        in_specs=(
            P(CTX, ("exp", "hid")),
            P(CTX, "exp"),
            P(CTX, "exp"),
            P(CTX + ("exp",), "hid"),
            P(("exp", "hid"), None),
            P("hid"),
            P("exp", "hid", CTX),
            P("exp", "hid", CTX),
            P("exp", CTX, "hid"),
            P(CTX + ("exp",), None),
            P(CTX + ("exp",), None),
        ),
        out_specs=P(CTX + ("exp",), "hid"),
        check_vma=False,
    )
```

```python
import math

import jax
import jax.numpy as jnp
from jax import lax
from jax.experimental import pallas as pl
from jax.experimental.pallas import tpu as pltpu
from jax.sharding import Mesh
from jax.sharding import PartitionSpec as P

HEADS = 32
KV_HEADS = 8
HEAD = 128
D = 4096
TOP = 2
EXPERTS = 8
CAP = 6
CTX = ("x", "yh", "core")
PLANE = ("x", "yh")
F32, BF16 = jnp.float32, jnp.bfloat16
TAIL = 16


def swap(value, axes):
    return lax.all_to_all(value, axes, split_axis=0, concat_axis=0, tiled=True)


def spread(value, axes):
    return swap(jnp.broadcast_to(value[None], (lax.axis_size(axes),) + value.shape), axes)


def other_core(value):
    return lax.ppermute(value, "core", [(0, 1), (1, 0)])


def whole(kernel, out_shapes, flops, smem=0, held=0):
    def call(*operands):
        spaces = [pltpu.SMEM] * smem + [pltpu.VMEM] * (len(operands) - smem - held) + [pl.ANY] * held
        moved = sum(math.prod(a.shape) * a.dtype.itemsize for a in operands)
        moved += sum(math.prod(a.shape) * a.dtype.itemsize for a in out_shapes)
        return pl.pallas_call(
            kernel,
            out_shape=out_shapes,
            in_specs=[pl.BlockSpec(memory_space=space) for space in spaces],
            out_specs=[pl.BlockSpec(memory_space=pltpu.VMEM)] * len(out_shapes),
            compiler_params=pltpu.CompilerParams(vmem_limit_bytes=24 * 1024 * 1024),
            cost_estimate=pl.CostEstimate(flops=flops, bytes_accessed=moved, transcendentals=0),
        )(*operands)

    return call


def dot_nt(left, right):
    return lax.dot_general(left, right, (((1,), (1,)), ((), ())), preferred_element_type=F32)


def attention_kernel(place, query, near, far, weight, routes, out, selector, mixer, zero):
    ctx, core = place[0], place[1]
    rows, keys = query.shape[0], near.shape[0]
    spot = ctx * rows + lax.broadcasted_iota(jnp.int32, (rows, keys), 0)
    column = lax.broadcasted_iota(jnp.int32, (rows, keys), 1)
    base = (column // rows) * (2 * rows) + column % rows
    scores = []
    for half, source in enumerate((near, far)):
        key_spot = base + (core ^ half) * rows
        product = dot_nt(query[...], source[:, :HEAD]) * (1.0 / math.sqrt(HEAD))
        scores.append(jnp.where(spot >= key_spot, product, -1e30))
    top = jnp.maximum(*(jnp.max(score, axis=1, keepdims=True) for score in scores))
    denom, total = 0.0, 0.0
    for score, source in zip(scores, (near, far)):
        weights = jnp.exp(score - top)
        denom = denom + jnp.sum(weights, axis=1, keepdims=True)
        total = total + jnp.dot(weights.astype(BF16), source[:, HEAD:], preferred_element_type=F32)
    attended = (total / denom).astype(BF16)
    parts, _, width = out.shape
    for part in range(parts):
        columns = weight[:, part * width : (part + 1) * width]
        out[part] = jnp.dot(attended, columns, preferred_element_type=F32).astype(BF16)

    ids, shares = routes[:TOP, :].astype(jnp.int32), routes[TOP:, :]
    slots, tokens = mixer.shape
    expert = lax.broadcasted_iota(jnp.int32, (EXPERTS, tokens), 0)
    named = [(expert == ids[k : k + 1, :]).astype(F32) for k in range(TOP)]
    later = lax.broadcasted_iota(jnp.int32, (tokens, tokens), 0) < lax.broadcasted_iota(
        jnp.int32, (tokens, tokens), 1
    )
    before = jnp.dot((named[0] + named[1]).astype(BF16), later.astype(BF16), preferred_element_type=F32)
    line = lax.broadcasted_iota(jnp.int32, (slots, tokens), 0)
    mixed, picked = 0.0, 0.0
    for k in range(TOP):
        slot = jnp.sum(before * named[k], axis=0, keepdims=True).astype(jnp.int32)
        hit = (line == ids[k : k + 1, :] * CAP + slot).astype(F32)
        picked = picked + hit
        mixed = mixed + hit * shares[k : k + 1, :]
    selector[...] = picked.astype(BF16)
    mixer[...] = mixed
    zero[...] = jnp.zeros_like(zero)


def select_kernel(arrived, residual, selector, weights, stream, outgoing):
    mixed = sum(arrived[index].astype(F32) for index in range(arrived.shape[0]))
    total = residual[...].astype(F32) + mixed
    stream[...] = total
    rows = jnp.dot(selector[...], total.astype(BF16), preferred_element_type=F32)
    halves, experts, slots, _ = outgoing.shape
    for expert in range(experts):
        part = rows[expert * slots : (expert + 1) * slots, :].astype(BF16)
        for half in range(halves):
            outgoing[half, expert] = part


def gate_up_kernel(place, rows, gain, gate_near, up_near, weights, *outs):
    hid = place[0]
    count, depth = rows.shape
    piece = outs[0].shape[1] // 4
    columns = gate_near.shape[1]
    gate_far, up_far = weights.at[:depth, :columns], weights.at[:depth, columns:]
    widened = rows[...].astype(F32)
    scaled = (widened * gain[...]).astype(BF16)
    for k, out in enumerate(outs):
        start = pl.multiple_of((hid ^ k) * piece, piece)
        for index, (gate, up) in enumerate(((gate_near, up_near), (gate_far, up_far))):
            weight = jnp.concatenate([gate[:, pl.ds(start, piece)], up[:, pl.ds(start, piece)]], axis=1)
            product = jnp.dot(scaled, weight, preferred_element_type=F32)
            out[:count, 2 * index * piece : 2 * (index + 1) * piece] = product.astype(BF16)
    square = widened * widened
    high = square.astype(BF16)
    low = (square - high.astype(F32)).astype(BF16)
    ones = jnp.ones((TAIL, depth), BF16)
    norm = dot_nt(ones, high) + dot_nt(ones, low)
    high = norm.astype(BF16).astype(F32)
    line = lax.broadcasted_iota(jnp.int32, norm.shape, 0)
    tail = jnp.where(line == 0, high, jnp.where(line == 1, norm - high, 0.0)).astype(BF16)
    tail = jnp.concatenate([tail, jnp.zeros((TAIL, 4 * piece - count), BF16)], axis=1)
    for out in outs:
        out[count:, :] = tail


def active_kernel(*refs):
    parts, out = refs[:-1], refs[-1]
    piece = out.shape[1]
    count = parts[0].shape[0] - TAIL
    tail = sum(part[count:, :].astype(F32) for part in parts)
    inverse = lax.rsqrt((tail[0:1, :] + tail[1:2, :]) / D + 1e-05)
    for group in range(count // piece):
        first = group * piece
        factor = jnp.broadcast_to(inverse[:, first : first + piece], (piece, piece)).T
        summed = sum(part[first : first + piece, :].astype(F32) for part in parts)
        for index in range(out.shape[0] // count):
            gate = summed[:, 2 * index * piece : (2 * index + 1) * piece] * factor
            up = summed[:, (2 * index + 1) * piece : 2 * (index + 1) * piece] * factor
            active = (gate / (1.0 + jnp.exp(-gate)) * up).astype(BF16)
            out[index * count + first : index * count + first + piece, :] = active


def down_kernel(active, near, weights, out):
    count = out.shape[0]
    far = weights.at[weights.shape[0] - near.shape[0] :, :]
    total = 0.0
    for index, weight in enumerate((near, far)):
        rows = slice(index * count, (index + 1) * count)
        left = jnp.concatenate([active[h, rows, :] for h in range(active.shape[0])], axis=1)
        total = total + jnp.dot(left, weight[...], preferred_element_type=F32)
    out[...] = total.astype(BF16)


def shards(
    queries,
    key_heads,
    value_heads,
    residual,
    out_weight,
    norm_gain,
    gate_weight,
    up_weight,
    down_weight,
    expert_ids,
    expert_weights,
):
    plane = lax.axis_size(PLANE)
    lines, halves = lax.axis_size("x"), lax.axis_size("yh")
    exp_count = lax.axis_size("exp")
    hid_count = lax.axis_size("hid")
    tok_rows = queries.shape[0]
    row_count = tok_rows // exp_count
    width_part = D // hid_count
    ff_part = gate_weight.shape[2]
    piece = ff_part // hid_count
    shape = jax.ShapeDtypeStruct

    with jax.named_scope("kv_gather"):
        near = spread(jnp.concatenate([key_heads, value_heads], axis=1), PLANE)
        near = near.reshape(plane * tok_rows, 2 * HEAD)
        far = other_core(near)
    with jax.named_scope("attention"):
        routes = jnp.concatenate([expert_ids.T.astype(F32), expert_weights.T], axis=0)
        place = jnp.stack([lax.axis_index(CTX), lax.axis_index("core")]).astype(jnp.int32)
        partials, selector, mixer, zero = whole(
            attention_kernel,
            [
                shape((hid_count, tok_rows, width_part), BF16),
                shape((EXPERTS * CAP, row_count), BF16),
                shape((EXPERTS * CAP, row_count), F32),
                shape((16, 128), BF16),
            ],
            flops=2 * tok_rows * HEAD * (4 * plane * tok_rows + D),
            smem=1,
        )(place, queries, near, far, out_weight, routes)
    with jax.named_scope("weight_exchange"):
        weights = jnp.concatenate(
            [jnp.concatenate([gate_weight[0], up_weight[0]], axis=1), down_weight[0]], axis=0
        )
        weights = other_core(weights + zero[0, 0])
    with jax.named_scope("projection"):
        arrived = swap(partials.reshape(hid_count * exp_count, row_count, width_part), ("hid", "exp"))
        stream, outgoing = whole(
            select_kernel,
            [shape((row_count, width_part), F32), shape((halves, exp_count, CAP, width_part), BF16)],
            flops=2 * arrived.size,
            held=1,
        )(arrived, residual, selector, weights)

    with jax.named_scope("dispatch"):
        arrived = swap(outgoing.reshape(halves * exp_count, CAP, width_part), ("yh", "exp"))
        arrived = spread(arrived.reshape(halves * exp_count * CAP, width_part), "x")
        count = lines * halves * exp_count * CAP
        rows = arrived.reshape(count, width_part)

    with jax.named_scope("gate_up"):
        parts = whole(
            gate_up_kernel,
            [shape((count + TAIL, 4 * piece), BF16)] * hid_count,
            flops=8 * count * width_part * ff_part,
            smem=1,
        )(
            lax.axis_index("hid").astype(jnp.int32).reshape(1),
            rows,
            norm_gain.reshape(1, width_part),
            gate_weight[0],
            up_weight[0],
            weights,
        )
        arrivals = [parts[0]]
        for k in reversed(range(1, hid_count)):
            arrivals.append(lax.ppermute(parts[k], "hid", [(h, h ^ k) for h in range(hid_count)]))
    with jax.named_scope("active"):
        (active,) = whole(active_kernel, [shape((2 * count, piece), BF16)], flops=count * piece * 40)(*arrivals)
        active = lax.all_gather(active, "hid", axis=0, tiled=False)
    with jax.named_scope("down"):
        (back,) = whole(
            down_kernel, [shape((count, width_part), BF16)], flops=4 * count * ff_part * width_part
        )(active, down_weight[0], weights)
        back = swap(back.reshape(lines, count // lines, width_part), "x")
        back = jnp.sum(back.astype(F32), axis=0).astype(BF16)
        back = swap(back.reshape(halves * exp_count, CAP, width_part), ("yh", "exp"))
        back = back.reshape(halves, EXPERTS * CAP, width_part).astype(F32)
        back = jnp.sum(back, axis=0)
    with jax.named_scope("combine"):
        combined = lax.dot_general(mixer, back, (((0,), (0,)), ((), ())), precision=lax.Precision.HIGHEST)
        return (stream + combined).astype(BF16)


def solution(mesh):
    ctx, exp, hid = mesh.devices.shape
    split = Mesh(mesh.devices.reshape(ctx // 4, 2, 2, exp, hid), CTX + ("exp", "hid"))
    return jax.shard_map(
        shards,
        mesh=split,
        in_specs=(
            P(CTX, ("exp", "hid")),
            P(CTX, "exp"),
            P(CTX, "exp"),
            P(CTX + ("exp",), "hid"),
            P(("exp", "hid"), None),
            P("hid"),
            P("exp", "hid", CTX),
            P("exp", "hid", CTX),
            P("exp", CTX, "hid"),
            P(CTX + ("exp",), None),
            P(CTX + ("exp",), None),
        ),
        out_specs=P(CTX + ("exp",), "hid"),
        check_vma=False,
    )
```

```python
import math

import jax
import jax.numpy as jnp
from jax import lax
from jax.experimental import pallas as pl
from jax.experimental.pallas import tpu as pltpu
from jax.sharding import Mesh
from jax.sharding import PartitionSpec as P

HEADS = 32
KV_HEADS = 8
HEAD = 128
D = 4096
TOP = 2
EXPERTS = 8
CAP = 6
CTX = ("x", "yh", "core")
PLANE = ("x", "yh")
F32, BF16 = jnp.float32, jnp.bfloat16
TAIL = 16


def swap(value, axes):
    return lax.all_to_all(value, axes, split_axis=0, concat_axis=0, tiled=True)


def spread(value, axes):
    return swap(jnp.broadcast_to(value[None], (lax.axis_size(axes),) + value.shape), axes)


def other_core(value):
    return lax.ppermute(value, "core", [(0, 1), (1, 0)])


def whole(kernel, out_shapes, flops, smem=0, scratch=()):
    def call(*operands):
        spaces = [pltpu.SMEM] * smem + [pltpu.VMEM] * (len(operands) - smem)
        moved = sum(math.prod(a.shape) * a.dtype.itemsize for a in operands)
        moved += sum(math.prod(a.shape) * a.dtype.itemsize for a in out_shapes)
        return pl.pallas_call(
            kernel,
            out_shape=out_shapes,
            in_specs=[pl.BlockSpec(memory_space=space) for space in spaces],
            out_specs=[pl.BlockSpec(memory_space=pltpu.VMEM)] * len(out_shapes),
            scratch_shapes=scratch,
            compiler_params=pltpu.CompilerParams(vmem_limit_bytes=24 * 1024 * 1024),
            cost_estimate=pl.CostEstimate(flops=flops, bytes_accessed=moved, transcendentals=0),
        )(*operands)

    return call


def dot_nt(left, right):
    return lax.dot_general(left, right, (((1,), (1,)), ((), ())), preferred_element_type=F32)


def attention_kernel(place, query, near, far, weight, out, done):
    done[...] = jnp.zeros_like(done)
    ctx, core = place[0], place[1]
    rows, keys = query.shape[0], near.shape[0]
    spot = ctx * rows + lax.broadcasted_iota(jnp.int32, (rows, keys), 0)
    column = lax.broadcasted_iota(jnp.int32, (rows, keys), 1)
    base = (column // rows) * (2 * rows) + column % rows
    scores = []
    for half, source in enumerate((near, far)):
        key_spot = base + (core ^ half) * rows
        product = dot_nt(query[...], source[:, :HEAD]) * (1.0 / math.sqrt(HEAD))
        scores.append(jnp.where(spot >= key_spot, product, -1e30))
    top = jnp.maximum(*(jnp.max(score, axis=1, keepdims=True) for score in scores))
    denom, total = 0.0, 0.0
    for score, source in zip(scores, (near, far)):
        weights = jnp.exp(score - top)
        denom = denom + jnp.sum(weights, axis=1, keepdims=True)
        total = total + jnp.dot(weights.astype(BF16), source[:, HEAD:], preferred_element_type=F32)
    attended = (total / denom).astype(BF16)
    parts, _, width = out.shape
    for part in range(parts):
        columns = weight[:, part * width : (part + 1) * width]
        out[part] = jnp.dot(attended, columns, preferred_element_type=F32).astype(BF16)


def prepare_kernel(after, ids, shares, gate, up, selector, mixer, weights, sems):
    columns = gate.shape[1]
    copies = [
        pltpu.make_async_copy(gate, weights.at[:, pl.ds(0, columns)], sems.at[0]),
        pltpu.make_async_copy(up, weights.at[:, pl.ds(columns, columns)], sems.at[1]),
    ]
    for copy in copies:
        copy.start()
    slots, tokens = mixer.shape
    expert = lax.broadcasted_iota(jnp.int32, (EXPERTS, tokens), 0)
    named = [(expert == ids[k : k + 1, :]).astype(F32) for k in range(TOP)]
    later = lax.broadcasted_iota(jnp.int32, (tokens, tokens), 0) < lax.broadcasted_iota(
        jnp.int32, (tokens, tokens), 1
    )
    before = jnp.dot((named[0] + named[1]).astype(BF16), later.astype(BF16), preferred_element_type=F32)
    line = lax.broadcasted_iota(jnp.int32, (slots, tokens), 0)
    mixed, picked = 0.0, 0.0
    for k in range(TOP):
        slot = jnp.sum(before * named[k], axis=0, keepdims=True).astype(jnp.int32)
        hit = (line == ids[k : k + 1, :] * CAP + slot).astype(F32)
        picked = picked + hit
        mixed = mixed + hit * shares[k : k + 1, :]
    selector[...] = picked.astype(BF16)
    mixer[...] = mixed
    for copy in copies:
        copy.wait()


def select_kernel(arrived, residual, selector, stream, outgoing):
    mixed = sum(arrived[index].astype(F32) for index in range(arrived.shape[0]))
    total = residual[...].astype(F32) + mixed
    stream[...] = total
    rows = jnp.dot(selector[...], total.astype(BF16), preferred_element_type=F32)
    halves, experts, slots, _ = outgoing.shape
    for expert in range(experts):
        part = rows[expert * slots : (expert + 1) * slots, :].astype(BF16)
        for half in range(halves):
            outgoing[half, expert] = part


def gate_up_kernel(place, rows, gain, near, far, down, *refs):
    outs, (down_out, sem) = refs[:-2], refs[-2:]
    copy = pltpu.make_async_copy(down, down_out, sem)
    copy.start()
    hid = place[2]
    count, depth = rows.shape
    piece = outs[0].shape[1] // 4
    widened = rows[...].astype(F32)
    scaled = (widened * gain[...]).astype(BF16)
    for k, out in enumerate(outs):
        start = pl.multiple_of((hid ^ k) * piece, piece)
        other = pl.multiple_of((hid ^ k) * piece + len(outs) * piece, piece)
        for index, source in enumerate((near, far)):
            weight = jnp.concatenate([source[:depth, pl.ds(start, piece)], source[:depth, pl.ds(other, piece)]], axis=1)
            product = jnp.dot(scaled, weight, preferred_element_type=F32)
            out[:count, 2 * index * piece : 2 * (index + 1) * piece] = product.astype(BF16)
    square = widened * widened
    high = square.astype(BF16)
    low = (square - high.astype(F32)).astype(BF16)
    ones = jnp.ones((TAIL, depth), BF16)
    norm = dot_nt(ones, high) + dot_nt(ones, low)
    high = norm.astype(BF16).astype(F32)
    line = lax.broadcasted_iota(jnp.int32, norm.shape, 0)
    tail = jnp.where(line == 0, high, jnp.where(line == 1, norm - high, 0.0)).astype(BF16)
    tail = jnp.concatenate([tail, jnp.zeros((TAIL, 4 * piece - count), BF16)], axis=1)
    for out in outs:
        out[count:, :] = tail
    copy.wait()


def active_kernel(*refs):
    parts, out = refs[:-1], refs[-1]
    piece = out.shape[1]
    count = parts[0].shape[0] - TAIL
    tail = sum(part[count:, :].astype(F32) for part in parts)
    inverse = lax.rsqrt((tail[0:1, :] + tail[1:2, :]) / D + 1e-05)
    for group in range(count // piece):
        first = group * piece
        factor = jnp.broadcast_to(inverse[:, first : first + piece], (piece, piece)).T
        summed = sum(part[first : first + piece, :].astype(F32) for part in parts)
        for index in range(out.shape[0] // count):
            gate = summed[:, 2 * index * piece : (2 * index + 1) * piece] * factor
            up = summed[:, (2 * index + 1) * piece : 2 * (index + 1) * piece] * factor
            active = (gate / (1.0 + jnp.exp(-gate)) * up).astype(BF16)
            out[index * count + first : index * count + first + piece, :] = active


def down_kernel(active, near, far, out):
    count = out.shape[0]
    total = 0.0
    for index, weight in enumerate((near, far)):
        rows = slice(index * count, (index + 1) * count)
        left = jnp.concatenate([active[h, rows, :] for h in range(active.shape[0])], axis=1)
        total = total + jnp.dot(left, weight[...], preferred_element_type=F32)
    out[...] = total.astype(BF16)


def shards(
    queries,
    key_heads,
    value_heads,
    residual,
    out_weight,
    norm_gain,
    gate_weight,
    up_weight,
    down_weight,
    expert_ids,
    expert_weights,
):
    plane = lax.axis_size(PLANE)
    lines, halves = lax.axis_size("x"), lax.axis_size("yh")
    exp_count = lax.axis_size("exp")
    hid_count = lax.axis_size("hid")
    tok_rows = queries.shape[0]
    row_count = tok_rows // exp_count
    width_part = D // hid_count
    ff_part = gate_weight.shape[2]
    piece = ff_part // hid_count
    shape = jax.ShapeDtypeStruct

    with jax.named_scope("kv_gather"):
        near = spread(jnp.concatenate([key_heads, value_heads], axis=1), PLANE)
        near = near.reshape(plane * tok_rows, 2 * HEAD)
        far = other_core(near)
    with jax.named_scope("attention"):
        place = [lax.axis_index(CTX), lax.axis_index("core"), lax.axis_index("hid")]
        place = jnp.stack(place).astype(jnp.int32)
        partials, done = whole(
            attention_kernel,
            [shape((hid_count, tok_rows, width_part), BF16), shape((8, 128), F32)],
            flops=2 * tok_rows * HEAD * (4 * plane * tok_rows + D),
            smem=1,
        )(place, queries, near, far, out_weight)
    with jax.named_scope("prepare"):
        selector, mixer, near_weights = whole(
            prepare_kernel,
            [
                shape((EXPERTS * CAP, row_count), BF16),
                shape((EXPERTS * CAP, row_count), F32),
                shape((width_part, 2 * ff_part), BF16),
            ],
            flops=0,
            scratch=[pltpu.SemaphoreType.DMA((2,))],
        )(done, expert_ids.T, expert_weights.T, gate_weight[0], up_weight[0])
        far_weights = other_core(near_weights)
    with jax.named_scope("projection"):
        arrived = swap(partials.reshape(hid_count * exp_count, row_count, width_part), ("hid", "exp"))
        stream, outgoing = whole(
            select_kernel,
            [shape((row_count, width_part), F32), shape((halves, exp_count, CAP, width_part), BF16)],
            flops=2 * arrived.size,
        )(arrived, residual, selector)

    with jax.named_scope("dispatch"):
        arrived = swap(outgoing.reshape(halves * exp_count, CAP, width_part), ("yh", "exp"))
        arrived = spread(arrived.reshape(halves * exp_count * CAP, width_part), "x")
        count = lines * halves * exp_count * CAP
        rows = arrived.reshape(count, width_part)

    with jax.named_scope("gate_up"):
        *parts, near_down = whole(
            gate_up_kernel,
            [shape((count + TAIL, 4 * piece), BF16)] * hid_count + [shape((ff_part, width_part), BF16)],
            flops=8 * count * width_part * ff_part,
            smem=1,
            scratch=[pltpu.SemaphoreType.DMA],
        )(
            place,
            rows,
            norm_gain.reshape(1, width_part),
            near_weights,
            far_weights,
            down_weight[0],
        )
        arrivals = [parts[0]]
        for k in reversed(range(1, hid_count)):
            arrivals.append(lax.ppermute(parts[k], "hid", [(h, h ^ k) for h in range(hid_count)]))
        far_down = other_core(near_down)
    with jax.named_scope("active"):
        (active,) = whole(active_kernel, [shape((2 * count, piece), BF16)], flops=count * piece * 40)(*arrivals)
        active = lax.all_gather(active, "hid", axis=0, tiled=False)
    with jax.named_scope("down"):
        (back,) = whole(
            down_kernel, [shape((count, width_part), BF16)], flops=4 * count * ff_part * width_part
        )(active, near_down, far_down)
        back = swap(back.reshape(lines, count // lines, width_part), "x")
        back = jnp.sum(back.astype(F32), axis=0).astype(BF16)
        back = swap(back.reshape(halves * exp_count, CAP, width_part), ("yh", "exp"))
        back = back.reshape(halves, EXPERTS * CAP, width_part).astype(F32)
        back = jnp.sum(back, axis=0)
    with jax.named_scope("combine"):
        combined = lax.dot_general(mixer, back, (((0,), (0,)), ((), ())), precision=lax.Precision.HIGHEST)
        return (stream + combined).astype(BF16)


def solution(mesh):
    ctx, exp, hid = mesh.devices.shape
    split = Mesh(mesh.devices.reshape(ctx // 4, 2, 2, exp, hid), CTX + ("exp", "hid"))
    return jax.shard_map(
        shards,
        mesh=split,
        in_specs=(
            P(CTX, ("exp", "hid")),
            P(CTX, "exp"),
            P(CTX, "exp"),
            P(CTX + ("exp",), "hid"),
            P(("exp", "hid"), None),
            P("hid"),
            P("exp", "hid", CTX),
            P("exp", "hid", CTX),
            P("exp", CTX, "hid"),
            P(CTX + ("exp",), None),
            P(CTX + ("exp",), None),
        ),
        out_specs=P(CTX + ("exp",), "hid"),
        check_vma=False,
    )
```

```python
import math

import jax
import jax.numpy as jnp
from jax import lax
from jax.experimental import pallas as pl
from jax.experimental.pallas import tpu as pltpu
from jax.sharding import Mesh
from jax.sharding import PartitionSpec as P

HEADS = 32
KV_HEADS = 8
HEAD = 128
D = 4096
TOP = 2
EXPERTS = 8
CAP = 6
CTX = ("x", "yh", "core")
PLANE = ("x", "yh")
F32, BF16 = jnp.float32, jnp.bfloat16
TAIL = 16


def swap(value, axes):
    return lax.all_to_all(value, axes, split_axis=0, concat_axis=0, tiled=True)


def spread(value, axes):
    return swap(jnp.broadcast_to(value[None], (lax.axis_size(axes),) + value.shape), axes)


def other_core(value):
    return lax.ppermute(value, "core", [(0, 1), (1, 0)])


def whole(kernel, out_shapes, flops, smem=0, held=0, scratch=()):
    def call(*operands):
        spaces = [pltpu.SMEM] * smem + [pltpu.VMEM] * (len(operands) - smem - held) + [pl.ANY] * held
        moved = sum(math.prod(a.shape) * a.dtype.itemsize for a in operands)
        moved += sum(math.prod(a.shape) * a.dtype.itemsize for a in out_shapes)
        return pl.pallas_call(
            kernel,
            out_shape=out_shapes,
            in_specs=[pl.BlockSpec(memory_space=space) for space in spaces],
            out_specs=[pl.BlockSpec(memory_space=pltpu.VMEM)] * len(out_shapes),
            scratch_shapes=scratch,
            compiler_params=pltpu.CompilerParams(vmem_limit_bytes=24 * 1024 * 1024),
            cost_estimate=pl.CostEstimate(flops=flops, bytes_accessed=moved, transcendentals=0),
        )(*operands)

    return call


def dot_nt(left, right):
    return lax.dot_general(left, right, (((1,), (1,)), ((), ())), preferred_element_type=F32)


def attention_kernel(place, query, near, far, weight, out, done):
    done[...] = jnp.zeros_like(done)
    ctx, core = place[0], place[1]
    rows, keys = query.shape[0], near.shape[0]
    spot = ctx * rows + lax.broadcasted_iota(jnp.int32, (rows, keys), 0)
    column = lax.broadcasted_iota(jnp.int32, (rows, keys), 1)
    base = (column // rows) * (2 * rows) + column % rows
    scores = []
    for half, source in enumerate((near, far)):
        key_spot = base + (core ^ half) * rows
        product = dot_nt(query[...], source[:, :HEAD]) * (1.0 / math.sqrt(HEAD))
        scores.append(jnp.where(spot >= key_spot, product, -1e30))
    top = jnp.maximum(*(jnp.max(score, axis=1, keepdims=True) for score in scores))
    denom, total = 0.0, 0.0
    for score, source in zip(scores, (near, far)):
        weights = jnp.exp(score - top)
        denom = denom + jnp.sum(weights, axis=1, keepdims=True)
        total = total + jnp.dot(weights.astype(BF16), source[:, HEAD:], preferred_element_type=F32)
    attended = (total / denom).astype(BF16)
    parts, _, width = out.shape
    for part in range(parts):
        columns = weight[:, part * width : (part + 1) * width]
        out[part] = jnp.dot(attended, columns, preferred_element_type=F32).astype(BF16)


def prepare_kernel(after, ids, shares, gate, up, down, selector, mixer, weights, down_out, sems):
    columns = gate.shape[1]
    copies = [
        pltpu.make_async_copy(gate, weights.at[:, pl.ds(0, columns)], sems.at[0]),
        pltpu.make_async_copy(up, weights.at[:, pl.ds(columns, columns)], sems.at[1]),
        pltpu.make_async_copy(down, down_out, sems.at[2]),
    ]
    for copy in copies:
        copy.start()
    slots, tokens = mixer.shape
    expert = lax.broadcasted_iota(jnp.int32, (EXPERTS, tokens), 0)
    named = [(expert == ids[k : k + 1, :]).astype(F32) for k in range(TOP)]
    later = lax.broadcasted_iota(jnp.int32, (tokens, tokens), 0) < lax.broadcasted_iota(
        jnp.int32, (tokens, tokens), 1
    )
    before = jnp.dot((named[0] + named[1]).astype(BF16), later.astype(BF16), preferred_element_type=F32)
    line = lax.broadcasted_iota(jnp.int32, (slots, tokens), 0)
    mixed, picked = 0.0, 0.0
    for k in range(TOP):
        slot = jnp.sum(before * named[k], axis=0, keepdims=True).astype(jnp.int32)
        hit = (line == ids[k : k + 1, :] * CAP + slot).astype(F32)
        picked = picked + hit
        mixed = mixed + hit * shares[k : k + 1, :]
    selector[...] = picked.astype(BF16)
    mixer[...] = mixed
    for copy in copies:
        copy.wait()


def select_kernel(arrived, residual, selector, stream, outgoing):
    mixed = sum(arrived[index].astype(F32) for index in range(arrived.shape[0]))
    total = residual[...].astype(F32) + mixed
    stream[...] = total
    rows = jnp.dot(selector[...], total.astype(BF16), preferred_element_type=F32)
    halves, experts, slots, _ = outgoing.shape
    for expert in range(experts):
        part = rows[expert * slots : (expert + 1) * slots, :].astype(BF16)
        for half in range(halves):
            outgoing[half, expert] = part


def gate_up_kernel(place, rows, gain, near, far, down, *outs):
    hid = place[2]
    count, depth = rows.shape
    piece = outs[0].shape[1] // 4
    widened = rows[...].astype(F32)
    scaled = (widened * gain[...]).astype(BF16)
    for k, out in enumerate(outs):
        start = pl.multiple_of((hid ^ k) * piece, piece)
        other = pl.multiple_of((hid ^ k) * piece + len(outs) * piece, piece)
        for index, source in enumerate((near, far)):
            weight = jnp.concatenate([source[:depth, pl.ds(start, piece)], source[:depth, pl.ds(other, piece)]], axis=1)
            product = jnp.dot(scaled, weight, preferred_element_type=F32)
            out[:count, 2 * index * piece : 2 * (index + 1) * piece] = product.astype(BF16)
    square = widened * widened
    high = square.astype(BF16)
    low = (square - high.astype(F32)).astype(BF16)
    ones = jnp.ones((TAIL, depth), BF16)
    norm = dot_nt(ones, high) + dot_nt(ones, low)
    high = norm.astype(BF16).astype(F32)
    line = lax.broadcasted_iota(jnp.int32, norm.shape, 0)
    tail = jnp.where(line == 0, high, jnp.where(line == 1, norm - high, 0.0)).astype(BF16)
    tail = jnp.concatenate([tail, jnp.zeros((TAIL, 4 * piece - count), BF16)], axis=1)
    for out in outs:
        out[count:, :] = tail


def active_kernel(*refs):
    parts, out = refs[:-1], refs[-1]
    piece = out.shape[1]
    count = parts[0].shape[0] - TAIL
    tail = sum(part[count:, :].astype(F32) for part in parts)
    inverse = lax.rsqrt((tail[0:1, :] + tail[1:2, :]) / D + 1e-05)
    for group in range(count // piece):
        first = group * piece
        factor = jnp.broadcast_to(inverse[:, first : first + piece], (piece, piece)).T
        summed = sum(part[first : first + piece, :].astype(F32) for part in parts)
        for index in range(out.shape[0] // count):
            gate = summed[:, 2 * index * piece : (2 * index + 1) * piece] * factor
            up = summed[:, (2 * index + 1) * piece : 2 * (index + 1) * piece] * factor
            active = (gate / (1.0 + jnp.exp(-gate)) * up).astype(BF16)
            out[index * count + first : index * count + first + piece, :] = active


def down_kernel(active, near, far, out):
    count = out.shape[0]
    total = 0.0
    for index, weight in enumerate((near, far)):
        rows = slice(index * count, (index + 1) * count)
        left = jnp.concatenate([active[h, rows, :] for h in range(active.shape[0])], axis=1)
        total = total + jnp.dot(left, weight[...], preferred_element_type=F32)
    out[...] = total.astype(BF16)


def shards(
    queries,
    key_heads,
    value_heads,
    residual,
    out_weight,
    norm_gain,
    gate_weight,
    up_weight,
    down_weight,
    expert_ids,
    expert_weights,
):
    plane = lax.axis_size(PLANE)
    lines, halves = lax.axis_size("x"), lax.axis_size("yh")
    exp_count = lax.axis_size("exp")
    hid_count = lax.axis_size("hid")
    tok_rows = queries.shape[0]
    row_count = tok_rows // exp_count
    width_part = D // hid_count
    ff_part = gate_weight.shape[2]
    piece = ff_part // hid_count
    shape = jax.ShapeDtypeStruct

    with jax.named_scope("kv_gather"):
        near = spread(jnp.concatenate([key_heads, value_heads], axis=1), PLANE)
        near = near.reshape(plane * tok_rows, 2 * HEAD)
        far = other_core(near)
    with jax.named_scope("attention"):
        place = [lax.axis_index(CTX), lax.axis_index("core"), lax.axis_index("hid")]
        place = jnp.stack(place).astype(jnp.int32)
        partials, done = whole(
            attention_kernel,
            [shape((hid_count, tok_rows, width_part), BF16), shape((8, 128), F32)],
            flops=2 * tok_rows * HEAD * (4 * plane * tok_rows + D),
            smem=1,
        )(place, queries, near, far, out_weight)
    with jax.named_scope("prepare"):
        selector, mixer, near_weights, near_down = whole(
            prepare_kernel,
            [
                shape((EXPERTS * CAP, row_count), BF16),
                shape((EXPERTS * CAP, row_count), F32),
                shape((width_part, 2 * ff_part), BF16),
                shape((ff_part, width_part), BF16),
            ],
            flops=0,
            scratch=[pltpu.SemaphoreType.DMA((3,))],
        )(done, expert_ids.T, expert_weights.T, gate_weight[0], up_weight[0], down_weight[0])
        far_weights, far_down = other_core(near_weights), other_core(near_down)
    with jax.named_scope("projection"):
        arrived = swap(partials.reshape(hid_count * exp_count, row_count, width_part), ("hid", "exp"))
        stream, outgoing = whole(
            select_kernel,
            [shape((row_count, width_part), F32), shape((halves, exp_count, CAP, width_part), BF16)],
            flops=2 * arrived.size,
        )(arrived, residual, selector)

    with jax.named_scope("dispatch"):
        arrived = swap(outgoing.reshape(halves * exp_count, CAP, width_part), ("yh", "exp"))
        arrived = spread(arrived.reshape(halves * exp_count * CAP, width_part), "x")
        count = lines * halves * exp_count * CAP
        rows = arrived.reshape(count, width_part)

    with jax.named_scope("gate_up"):
        parts = whole(
            gate_up_kernel,
            [shape((count + TAIL, 4 * piece), BF16)] * hid_count,
            flops=8 * count * width_part * ff_part,
            smem=1,
            held=1,
        )(
            place,
            rows,
            norm_gain.reshape(1, width_part),
            near_weights,
            far_weights,
            far_down,
        )
        arrivals = [parts[0]]
        for k in reversed(range(1, hid_count)):
            arrivals.append(lax.ppermute(parts[k], "hid", [(h, h ^ k) for h in range(hid_count)]))
    with jax.named_scope("active"):
        (active,) = whole(active_kernel, [shape((2 * count, piece), BF16)], flops=count * piece * 40)(*arrivals)
        active = lax.all_gather(active, "hid", axis=0, tiled=False)
    with jax.named_scope("down"):
        (back,) = whole(
            down_kernel, [shape((count, width_part), BF16)], flops=4 * count * ff_part * width_part
        )(active, near_down, far_down)
        back = swap(back.reshape(lines, count // lines, width_part), "x")
        back = jnp.sum(back.astype(F32), axis=0).astype(BF16)
        back = swap(back.reshape(halves * exp_count, CAP, width_part), ("yh", "exp"))
        back = back.reshape(halves, EXPERTS * CAP, width_part).astype(F32)
        back = jnp.sum(back, axis=0)
    with jax.named_scope("combine"):
        combined = lax.dot_general(mixer, back, (((0,), (0,)), ((), ())), precision=lax.Precision.HIGHEST)
        return (stream + combined).astype(BF16)


def solution(mesh):
    ctx, exp, hid = mesh.devices.shape
    split = Mesh(mesh.devices.reshape(ctx // 4, 2, 2, exp, hid), CTX + ("exp", "hid"))
    return jax.shard_map(
        shards,
        mesh=split,
        in_specs=(
            P(CTX, ("exp", "hid")),
            P(CTX, "exp"),
            P(CTX, "exp"),
            P(CTX + ("exp",), "hid"),
            P(("exp", "hid"), None),
            P("hid"),
            P("exp", "hid", CTX),
            P("exp", "hid", CTX),
            P("exp", CTX, "hid"),
            P(CTX + ("exp",), None),
            P(CTX + ("exp",), None),
        ),
        out_specs=P(CTX + ("exp",), "hid"),
        check_vma=False,
    )
```

```python
import math

import jax
import jax.numpy as jnp
from jax import lax
from jax.experimental import pallas as pl
from jax.experimental.pallas import tpu as pltpu
from jax.sharding import Mesh
from jax.sharding import PartitionSpec as P

HEADS = 32
KV_HEADS = 8
HEAD = 128
D = 4096
TOP = 2
EXPERTS = 8
CAP = 6
CTX = ("x", "yh", "core")
PLANE = ("x", "yh")
F32, BF16 = jnp.float32, jnp.bfloat16
TAIL = 16


def swap(value, axes):
    return lax.all_to_all(value, axes, split_axis=0, concat_axis=0, tiled=True)


def spread(value, axes):
    return swap(jnp.broadcast_to(value[None], (lax.axis_size(axes),) + value.shape), axes)


def other_core(value):
    return lax.ppermute(value, "core", [(0, 1), (1, 0)])


def to_peer(value, offset):
    return lax.ppermute(value, "hid", [(h, h ^ offset) for h in range(lax.axis_size("hid"))])


def whole(kernel, out_shapes, flops, smem=0, held=0, scratch=()):
    def call(*operands):
        spaces = [pltpu.SMEM] * smem + [pltpu.VMEM] * (len(operands) - smem - held) + [pl.ANY] * held
        moved = sum(math.prod(a.shape) * a.dtype.itemsize for a in operands)
        moved += sum(math.prod(a.shape) * a.dtype.itemsize for a in out_shapes)
        return pl.pallas_call(
            kernel,
            out_shape=out_shapes,
            in_specs=[pl.BlockSpec(memory_space=space) for space in spaces],
            out_specs=[pl.BlockSpec(memory_space=pltpu.VMEM)] * len(out_shapes),
            scratch_shapes=scratch,
            compiler_params=pltpu.CompilerParams(vmem_limit_bytes=24 * 1024 * 1024),
            cost_estimate=pl.CostEstimate(flops=flops, bytes_accessed=moved, transcendentals=0),
        )(*operands)

    return call


def dot_nt(left, right):
    return lax.dot_general(left, right, (((1,), (1,)), ((), ())), preferred_element_type=F32)


def attention_kernel(place, query, near, far, weight, out, done):
    done[...] = jnp.zeros_like(done)
    ctx, core = place[0], place[1]
    rows, keys = query.shape[0], near.shape[0]
    spot = ctx * rows + lax.broadcasted_iota(jnp.int32, (rows, keys), 0)
    column = lax.broadcasted_iota(jnp.int32, (rows, keys), 1)
    base = (column // rows) * (2 * rows) + column % rows
    scores = []
    for half, source in enumerate((near, far)):
        key_spot = base + (core ^ half) * rows
        product = dot_nt(query[...], source[:, :HEAD]) * (1.0 / math.sqrt(HEAD))
        scores.append(jnp.where(spot >= key_spot, product, -1e30))
    top = jnp.maximum(*(jnp.max(score, axis=1, keepdims=True) for score in scores))
    denom, total = 0.0, 0.0
    for score, source in zip(scores, (near, far)):
        weights = jnp.exp(score - top)
        denom = denom + jnp.sum(weights, axis=1, keepdims=True)
        total = total + jnp.dot(weights.astype(BF16), source[:, HEAD:], preferred_element_type=F32)
    attended = (total / denom).astype(BF16)
    parts, _, width = out.shape
    for part in range(parts):
        columns = weight[:, part * width : (part + 1) * width]
        out[part] = jnp.dot(attended, columns, preferred_element_type=F32).astype(BF16)


def prepare_kernel(after, ids, shares, gate, up, down, selector, mixer, weights, down_out, sems):
    peers = (sems.shape[0] - 1) // 2
    piece = gate.shape[1] // peers
    copies = [pltpu.make_async_copy(down, down_out, sems.at[2 * peers])]
    for index in range(peers):
        for which, source in enumerate((gate, up)):
            place = 2 * index + which
            taken = source.at[:, pl.ds(index * piece, piece)]
            copies.append(
                pltpu.make_async_copy(taken, weights.at[:, pl.ds(place * piece, piece)], sems.at[place])
            )
    for copy in copies:
        copy.start()
    slots, tokens = mixer.shape
    expert = lax.broadcasted_iota(jnp.int32, (EXPERTS, tokens), 0)
    named = [(expert == ids[k : k + 1, :]).astype(F32) for k in range(TOP)]
    later = lax.broadcasted_iota(jnp.int32, (tokens, tokens), 0) < lax.broadcasted_iota(
        jnp.int32, (tokens, tokens), 1
    )
    before = jnp.dot((named[0] + named[1]).astype(BF16), later.astype(BF16), preferred_element_type=F32)
    line = lax.broadcasted_iota(jnp.int32, (slots, tokens), 0)
    mixed, picked = 0.0, 0.0
    for k in range(TOP):
        slot = jnp.sum(before * named[k], axis=0, keepdims=True).astype(jnp.int32)
        hit = (line == ids[k : k + 1, :] * CAP + slot).astype(F32)
        picked = picked + hit
        mixed = mixed + hit * shares[k : k + 1, :]
    selector[...] = picked.astype(BF16)
    mixer[...] = mixed
    for copy in copies:
        copy.wait()


def select_kernel(arrived, residual, selector, stream, outgoing):
    mixed = sum(arrived[index].astype(F32) for index in range(arrived.shape[0]))
    total = residual[...].astype(F32) + mixed
    stream[...] = total
    rows = jnp.dot(selector[...], total.astype(BF16), preferred_element_type=F32)
    halves, experts, slots, _ = outgoing.shape
    for expert in range(experts):
        part = rows[expert * slots : (expert + 1) * slots, :].astype(BF16)
        for half in range(halves):
            outgoing[half, expert] = part


def arrange_kernel(arrived, weights, down, out):
    rows = jnp.concatenate([arrived[index].astype(F32) for index in range(arrived.shape[0])], axis=0).astype(BF16)
    for index in range(out.shape[0]):
        out[index] = rows


def share_of(place, scaled, near, far, offset, out):
    width = out.shape[1] // 2
    start = pl.multiple_of((place[2] ^ offset) * width, width)
    for index, source in enumerate((near, far)):
        product = jnp.dot(scaled, source[:, pl.ds(start, width)], preferred_element_type=F32)
        out[: scaled.shape[0], index * width : (index + 1) * width] = product.astype(BF16)


def first_kernel(place, rows, gain, near, far, third, second, scaled_out, tail_out):
    count, depth = rows.shape
    widened = rows[...].astype(F32)
    scaled = (widened * gain[...]).astype(BF16)
    scaled_out[...] = scaled
    square = widened * widened
    high = square.astype(BF16)
    low = (square - high.astype(F32)).astype(BF16)
    ones = jnp.ones((TAIL, depth), BF16)
    norm = dot_nt(ones, high) + dot_nt(ones, low)
    high = norm.astype(BF16).astype(F32)
    line = lax.broadcasted_iota(jnp.int32, norm.shape, 0)
    tail = jnp.where(line == 0, high, jnp.where(line == 1, norm - high, 0.0)).astype(BF16)
    tail = jnp.concatenate([tail, jnp.zeros((TAIL, third.shape[1] - count), BF16)], axis=1)
    for out in (third, second, tail_out):
        out[out.shape[0] - TAIL :, :] = tail
    share_of(place, scaled, near, far, 3, third)
    share_of(place, scaled, near, far, 2, second)


def last_kernel(place, scaled, tail, near, far, first, own):
    for offset, out in ((1, first), (0, own)):
        out[scaled.shape[0] :, :] = tail[...]
        share_of(place, scaled[...], near, far, offset, out)


def active_kernel(*refs):
    parts, out = refs[:-1], refs[-1]
    piece = out.shape[1]
    count = parts[0].shape[0] - TAIL
    tail = sum(part[count:, :].astype(F32) for part in parts)
    inverse = lax.rsqrt((tail[0:1, :] + tail[1:2, :]) / D + 1e-05)
    for group in range(count // piece):
        first = group * piece
        factor = jnp.broadcast_to(inverse[:, first : first + piece], (piece, piece)).T
        summed = sum(part[first : first + piece, :].astype(F32) for part in parts)
        for index in range(out.shape[0] // count):
            gate = summed[:, 2 * index * piece : (2 * index + 1) * piece] * factor
            up = summed[:, (2 * index + 1) * piece : 2 * (index + 1) * piece] * factor
            active = (gate / (1.0 + jnp.exp(-gate)) * up).astype(BF16)
            out[index * count + first : index * count + first + piece, :] = active


def down_kernel(active, near, far, out):
    count = out.shape[0]
    total = 0.0
    for index, weight in enumerate((near, far)):
        rows = slice(index * count, (index + 1) * count)
        left = jnp.concatenate([active[h, rows, :] for h in range(active.shape[0])], axis=1)
        total = total + jnp.dot(left, weight[...], preferred_element_type=F32)
    out[...] = total.astype(BF16)


def shards(
    queries,
    key_heads,
    value_heads,
    residual,
    out_weight,
    norm_gain,
    gate_weight,
    up_weight,
    down_weight,
    expert_ids,
    expert_weights,
):
    plane = lax.axis_size(PLANE)
    lines, halves = lax.axis_size("x"), lax.axis_size("yh")
    exp_count = lax.axis_size("exp")
    hid_count = lax.axis_size("hid")
    tok_rows = queries.shape[0]
    row_count = tok_rows // exp_count
    width_part = D // hid_count
    ff_part = gate_weight.shape[2]
    piece = ff_part // hid_count
    shape = jax.ShapeDtypeStruct

    with jax.named_scope("kv_gather"):
        near = spread(jnp.concatenate([key_heads, value_heads], axis=1), PLANE)
        near = near.reshape(plane * tok_rows, 2 * HEAD)
        far = other_core(near)
    with jax.named_scope("attention"):
        place = [lax.axis_index(CTX), lax.axis_index("core"), lax.axis_index("hid")]
        place = jnp.stack(place).astype(jnp.int32)
        partials, done = whole(
            attention_kernel,
            [shape((hid_count, tok_rows, width_part), BF16), shape((8, 128), F32)],
            flops=2 * tok_rows * HEAD * (4 * plane * tok_rows + D),
            smem=1,
        )(place, queries, near, far, out_weight)
    with jax.named_scope("prepare"):
        selector, mixer, near_weights, near_down = whole(
            prepare_kernel,
            [
                shape((EXPERTS * CAP, row_count), BF16),
                shape((EXPERTS * CAP, row_count), F32),
                shape((width_part, 2 * ff_part), BF16),
                shape((ff_part, width_part), BF16),
            ],
            flops=0,
            scratch=[pltpu.SemaphoreType.DMA((2 * hid_count + 1,))],
        )(done, expert_ids.T, expert_weights.T, gate_weight[0], up_weight[0], down_weight[0])
        far_weights, far_down = other_core(near_weights), other_core(near_down)
    with jax.named_scope("projection"):
        arrived = swap(partials.reshape(hid_count * exp_count, row_count, width_part), ("hid", "exp"))
        stream, outgoing = whole(
            select_kernel,
            [shape((row_count, width_part), F32), shape((halves, exp_count, CAP, width_part), BF16)],
            flops=2 * arrived.size,
        )(arrived, residual, selector)

    with jax.named_scope("dispatch"):
        arrived = swap(outgoing.reshape(halves * exp_count, CAP, width_part), ("yh", "exp"))
        (copies,) = whole(
            arrange_kernel,
            [shape((lines, halves * exp_count * CAP, width_part), BF16)],
            flops=0,
            held=2,
        )(arrived, far_weights, far_down)
        arrived = swap(copies, "x")
        count = lines * halves * exp_count * CAP
        rows = arrived.reshape(count, width_part)

    with jax.named_scope("gate_up"):
        part = shape((count + TAIL, 4 * piece), BF16)
        third, second, scaled, tail = whole(
            first_kernel,
            [part, part, shape((count, width_part), BF16), shape((TAIL, 4 * piece), BF16)],
            flops=4 * count * width_part * ff_part,
            smem=1,
        )(place, rows, norm_gain.reshape(1, width_part), near_weights, far_weights)
        third, second = to_peer(third, 3), to_peer(second, 2)
        first, own = whole(
            last_kernel, [part, part], flops=4 * count * width_part * ff_part, smem=1
        )(place, scaled, tail, near_weights, far_weights)
        arrivals = [third, second, to_peer(first, 1), own]
    with jax.named_scope("active"):
        (active,) = whole(active_kernel, [shape((2 * count, piece), BF16)], flops=count * piece * 40)(*arrivals)
        active = lax.all_gather(active, "hid", axis=0, tiled=False)
    with jax.named_scope("down"):
        (back,) = whole(
            down_kernel, [shape((count, width_part), BF16)], flops=4 * count * ff_part * width_part
        )(active, near_down, far_down)
        back = swap(back.reshape(lines, count // lines, width_part), "x")
        back = jnp.sum(back.astype(F32), axis=0).astype(BF16)
        back = swap(back.reshape(halves * exp_count, CAP, width_part), ("yh", "exp"))
        back = back.reshape(halves, EXPERTS * CAP, width_part).astype(F32)
        back = jnp.sum(back, axis=0)
    with jax.named_scope("combine"):
        combined = lax.dot_general(mixer, back, (((0,), (0,)), ((), ())), precision=lax.Precision.HIGHEST)
        return (stream + combined).astype(BF16)


def solution(mesh):
    ctx, exp, hid = mesh.devices.shape
    split = Mesh(mesh.devices.reshape(ctx // 4, 2, 2, exp, hid), CTX + ("exp", "hid"))
    return jax.shard_map(
        shards,
        mesh=split,
        in_specs=(
            P(CTX, ("exp", "hid")),
            P(CTX, "exp"),
            P(CTX, "exp"),
            P(CTX + ("exp",), "hid"),
            P(("exp", "hid"), None),
            P("hid"),
            P("exp", "hid", CTX),
            P("exp", "hid", CTX),
            P("exp", CTX, "hid"),
            P(CTX + ("exp",), None),
            P(CTX + ("exp",), None),
        ),
        out_specs=P(CTX + ("exp",), "hid"),
        check_vma=False,
    )
```

```python
import math

import jax
import jax.numpy as jnp
from jax import lax
from jax.experimental import pallas as pl
from jax.experimental.pallas import tpu as pltpu
from jax.sharding import Mesh
from jax.sharding import PartitionSpec as P

HEADS = 32
KV_HEADS = 8
HEAD = 128
D = 4096
TOP = 2
EXPERTS = 8
CAP = 6
CTX = ("x", "yh", "core")
PLANE = ("x", "yh")
F32, BF16 = jnp.float32, jnp.bfloat16
TAIL = 16


def swap(value, axes):
    return lax.all_to_all(value, axes, split_axis=0, concat_axis=0, tiled=True)


def spread(value, axes):
    return swap(jnp.broadcast_to(value[None], (lax.axis_size(axes),) + value.shape), axes)


def other_core(value):
    return lax.ppermute(value, "core", [(0, 1), (1, 0)])


def to_peer(value, offset):
    return lax.ppermute(value, "hid", [(h, h ^ offset) for h in range(lax.axis_size("hid"))])


def whole(kernel, out_shapes, flops, smem=0, held=0, scratch=()):
    def call(*operands):
        spaces = [pltpu.SMEM] * smem + [pltpu.VMEM] * (len(operands) - smem - held) + [pl.ANY] * held
        moved = sum(math.prod(a.shape) * a.dtype.itemsize for a in operands)
        moved += sum(math.prod(a.shape) * a.dtype.itemsize for a in out_shapes)
        return pl.pallas_call(
            kernel,
            out_shape=out_shapes,
            in_specs=[pl.BlockSpec(memory_space=space) for space in spaces],
            out_specs=[pl.BlockSpec(memory_space=pltpu.VMEM)] * len(out_shapes),
            scratch_shapes=scratch,
            compiler_params=pltpu.CompilerParams(vmem_limit_bytes=24 * 1024 * 1024),
            cost_estimate=pl.CostEstimate(flops=flops, bytes_accessed=moved, transcendentals=0),
        )(*operands)

    return call


def dot_nt(left, right):
    return lax.dot_general(left, right, (((1,), (1,)), ((), ())), preferred_element_type=F32)


def attention_kernel(place, query, near, far, weight, out, done):
    done[...] = jnp.zeros_like(done)
    ctx, core = place[0], place[1]
    rows, keys = query.shape[0], near.shape[0]
    spot = ctx * rows + lax.broadcasted_iota(jnp.int32, (rows, keys), 0)
    column = lax.broadcasted_iota(jnp.int32, (rows, keys), 1)
    base = (column // rows) * (2 * rows) + column % rows
    scores = []
    for half, source in enumerate((near, far)):
        key_spot = base + (core ^ half) * rows
        product = dot_nt(query[...], source[:, :HEAD]) * (1.0 / math.sqrt(HEAD))
        scores.append(jnp.where(spot >= key_spot, product, -1e30))
    top = jnp.maximum(*(jnp.max(score, axis=1, keepdims=True) for score in scores))
    denom, total = 0.0, 0.0
    for score, source in zip(scores, (near, far)):
        weights = jnp.exp(score - top)
        denom = denom + jnp.sum(weights, axis=1, keepdims=True)
        total = total + jnp.dot(weights.astype(BF16), source[:, HEAD:], preferred_element_type=F32)
    attended = (total / denom).astype(BF16)
    parts, _, width = out.shape
    for part in range(parts):
        columns = weight[:, part * width : (part + 1) * width]
        out[part] = jnp.dot(attended, columns, preferred_element_type=F32).astype(BF16)


def prepare_kernel(after, ids, shares, gate, up, down, selector, mixer, weights, down_out, sems):
    peers = (sems.shape[0] - 1) // 2
    piece = gate.shape[1] // peers
    copies = [pltpu.make_async_copy(down, down_out, sems.at[2 * peers])]
    for index in range(peers):
        for which, source in enumerate((gate, up)):
            place = 2 * index + which
            taken = source.at[:, pl.ds(index * piece, piece)]
            copies.append(
                pltpu.make_async_copy(taken, weights.at[:, pl.ds(place * piece, piece)], sems.at[place])
            )
    for copy in copies:
        copy.start()
    slots, tokens = mixer.shape
    expert = lax.broadcasted_iota(jnp.int32, (EXPERTS, tokens), 0)
    named = [(expert == ids[k : k + 1, :]).astype(F32) for k in range(TOP)]
    later = lax.broadcasted_iota(jnp.int32, (tokens, tokens), 0) < lax.broadcasted_iota(
        jnp.int32, (tokens, tokens), 1
    )
    before = jnp.dot((named[0] + named[1]).astype(BF16), later.astype(BF16), preferred_element_type=F32)
    line = lax.broadcasted_iota(jnp.int32, (slots, tokens), 0)
    mixed, picked = 0.0, 0.0
    for k in range(TOP):
        slot = jnp.sum(before * named[k], axis=0, keepdims=True).astype(jnp.int32)
        hit = (line == ids[k : k + 1, :] * CAP + slot).astype(F32)
        picked = picked + hit
        mixed = mixed + hit * shares[k : k + 1, :]
    selector[...] = picked.astype(BF16)
    mixer[...] = mixed
    for copy in copies:
        copy.wait()


def select_kernel(arrived, residual, selector, stream, outgoing):
    mixed = sum(arrived[index].astype(F32) for index in range(arrived.shape[0]))
    total = residual[...].astype(F32) + mixed
    stream[...] = total
    rows = jnp.dot(selector[...], total.astype(BF16), preferred_element_type=F32)
    halves, experts, slots, _ = outgoing.shape
    for expert in range(experts):
        part = rows[expert * slots : (expert + 1) * slots, :].astype(BF16)
        for half in range(halves):
            outgoing[half, expert] = part


def share_of(place, scaled, near, far, offset, out):
    width = out.shape[1] // 2
    start = pl.multiple_of((place[2] ^ offset) * width, width)
    for index, source in enumerate((near, far)):
        product = jnp.dot(scaled, source[:, pl.ds(start, width)], preferred_element_type=F32)
        out[: scaled.shape[0], index * width : (index + 1) * width] = product.astype(BF16)


def tail_of(norm, lines):
    high = norm.astype(BF16).astype(F32)
    line = lax.broadcasted_iota(jnp.int32, (lines, norm.shape[1]), 0)
    return jnp.where(line == 0, high, jnp.where(line == 1, norm - high, 0.0)).astype(BF16)


def first_kernel(place, rows, gain, near, far, down, third, scaled_out, tail_out):
    count, depth = rows.shape
    widened = rows[...].astype(F32)
    scaled = (widened * gain[...]).astype(BF16)
    scaled_out[...] = scaled
    square = widened * widened
    high = square.astype(BF16)
    low = (square - high.astype(F32)).astype(BF16)
    ones = jnp.ones((TAIL, depth), BF16)
    norm = (dot_nt(ones, high) + dot_nt(ones, low))[:1, :]
    norm = jnp.concatenate([norm, jnp.zeros((1, third.shape[1] - count), F32)], axis=1)
    tail = tail_of(norm, TAIL)
    third[count:, :] = tail
    tail_out[...] = tail
    share_of(place, scaled, near, far, 3, third)


def others_kernel(place, scaled, tail, near, far, second, first, own):
    for offset, out in ((2, second), (1, first), (0, own)):
        out[scaled.shape[0] :, :] = tail[...]
        share_of(place, scaled[...], near, far, offset, out)


def pair_kernel(own, arrived, first, pair, first_out):
    count = own.shape[0] - TAIL
    pair[:count, :] = (own[:count, :].astype(F32) + arrived[:count, :].astype(F32)).astype(BF16)
    tail = own[count:, :].astype(F32) + arrived[count:, :].astype(F32)
    pair[count:, :] = tail_of(tail[0:1, :] + tail[1:2, :], TAIL)
    first_out[...] = first[...]


def active_kernel(*refs):
    parts, out = refs[:-1], refs[-1]
    piece = out.shape[1]
    count = parts[0].shape[0] - TAIL
    tail = sum(part[count:, :].astype(F32) for part in parts)
    inverse = lax.rsqrt((tail[0:1, :] + tail[1:2, :]) / D + 1e-05)
    for group in range(count // piece):
        first = group * piece
        factor = jnp.broadcast_to(inverse[:, first : first + piece], (piece, piece)).T
        summed = sum(part[first : first + piece, :].astype(F32) for part in parts)
        for index in range(out.shape[0] // count):
            gate = summed[:, 2 * index * piece : (2 * index + 1) * piece] * factor
            up = summed[:, (2 * index + 1) * piece : 2 * (index + 1) * piece] * factor
            active = (gate / (1.0 + jnp.exp(-gate)) * up).astype(BF16)
            out[index * count + first : index * count + first + piece, :] = active


def down_kernel(active, near, far, out):
    count = out.shape[0]
    total = 0.0
    for index, weight in enumerate((near, far)):
        rows = slice(index * count, (index + 1) * count)
        left = jnp.concatenate([active[h, rows, :] for h in range(active.shape[0])], axis=1)
        total = total + jnp.dot(left, weight[...], preferred_element_type=F32)
    out[...] = total.astype(BF16)


def shards(
    queries,
    key_heads,
    value_heads,
    residual,
    out_weight,
    norm_gain,
    gate_weight,
    up_weight,
    down_weight,
    expert_ids,
    expert_weights,
):
    plane = lax.axis_size(PLANE)
    lines, halves = lax.axis_size("x"), lax.axis_size("yh")
    exp_count = lax.axis_size("exp")
    hid_count = lax.axis_size("hid")
    tok_rows = queries.shape[0]
    row_count = tok_rows // exp_count
    width_part = D // hid_count
    ff_part = gate_weight.shape[2]
    piece = ff_part // hid_count
    shape = jax.ShapeDtypeStruct

    with jax.named_scope("kv_gather"):
        near = spread(jnp.concatenate([key_heads, value_heads], axis=1), PLANE)
        near = near.reshape(plane * tok_rows, 2 * HEAD)
        far = other_core(near)
    with jax.named_scope("attention"):
        place = [lax.axis_index(CTX), lax.axis_index("core"), lax.axis_index("hid")]
        place = jnp.stack(place).astype(jnp.int32)
        partials, done = whole(
            attention_kernel,
            [shape((hid_count, tok_rows, width_part), BF16), shape((8, 128), F32)],
            flops=2 * tok_rows * HEAD * (4 * plane * tok_rows + D),
            smem=1,
        )(place, queries, near, far, out_weight)
    with jax.named_scope("prepare"):
        selector, mixer, near_weights, near_down = whole(
            prepare_kernel,
            [
                shape((EXPERTS * CAP, row_count), BF16),
                shape((EXPERTS * CAP, row_count), F32),
                shape((width_part, 2 * ff_part), BF16),
                shape((ff_part, width_part), BF16),
            ],
            flops=0,
            scratch=[pltpu.SemaphoreType.DMA((2 * hid_count + 1,))],
        )(done, expert_ids.T, expert_weights.T, gate_weight[0], up_weight[0], down_weight[0])
        far_weights, far_down = other_core(near_weights), other_core(near_down)
    with jax.named_scope("projection"):
        arrived = swap(partials.reshape(hid_count * exp_count, row_count, width_part), ("hid", "exp"))
        stream, outgoing = whole(
            select_kernel,
            [shape((row_count, width_part), F32), shape((halves, exp_count, CAP, width_part), BF16)],
            flops=2 * arrived.size,
        )(arrived, residual, selector)

    with jax.named_scope("dispatch"):
        arrived = swap(outgoing.reshape(halves * exp_count, CAP, width_part), ("yh", "exp"))
        arrived = spread(arrived.reshape(halves * exp_count * CAP, width_part), "x")
        count = lines * halves * exp_count * CAP
        rows = arrived.reshape(count, width_part)

    with jax.named_scope("gate_up"):
        part = shape((count + TAIL, 4 * piece), BF16)
        third, scaled, tail = whole(
            first_kernel,
            [part, shape((count, width_part), BF16), shape((TAIL, 4 * piece), BF16)],
            flops=2 * count * width_part * ff_part,
            smem=1,
            held=1,
        )(place, rows, norm_gain.reshape(1, width_part), near_weights, far_weights, far_down)
        third = to_peer(third, 1)
        second, first, own = whole(
            others_kernel, [part] * 3, flops=6 * count * width_part * ff_part, smem=1
        )(place, scaled, tail, near_weights, far_weights)
        pair, first = whole(pair_kernel, [part] * 2, flops=count * piece * 8)(second, third, first)
        arrivals = [to_peer(pair, 2), to_peer(first, 1), own]
    with jax.named_scope("active"):
        (active,) = whole(active_kernel, [shape((2 * count, piece), BF16)], flops=count * piece * 40)(*arrivals)
        active = lax.all_gather(active, "hid", axis=0, tiled=False)
    with jax.named_scope("down"):
        (back,) = whole(
            down_kernel, [shape((count, width_part), BF16)], flops=4 * count * ff_part * width_part
        )(active, near_down, far_down)
        back = swap(back.reshape(lines, count // lines, width_part), "x")
        back = jnp.sum(back.astype(F32), axis=0).astype(BF16)
        back = swap(back.reshape(halves * exp_count, CAP, width_part), ("yh", "exp"))
        back = back.reshape(halves, EXPERTS * CAP, width_part).astype(F32)
        back = jnp.sum(back, axis=0)
    with jax.named_scope("combine"):
        combined = lax.dot_general(mixer, back, (((0,), (0,)), ((), ())), precision=lax.Precision.HIGHEST)
        return (stream + combined).astype(BF16)


def solution(mesh):
    ctx, exp, hid = mesh.devices.shape
    split = Mesh(mesh.devices.reshape(ctx // 4, 2, 2, exp, hid), CTX + ("exp", "hid"))
    return jax.shard_map(
        shards,
        mesh=split,
        in_specs=(
            P(CTX, ("exp", "hid")),
            P(CTX, "exp"),
            P(CTX, "exp"),
            P(CTX + ("exp",), "hid"),
            P(("exp", "hid"), None),
            P("hid"),
            P("exp", "hid", CTX),
            P("exp", "hid", CTX),
            P("exp", CTX, "hid"),
            P(CTX + ("exp",), None),
            P(CTX + ("exp",), None),
        ),
        out_specs=P(CTX + ("exp",), "hid"),
        check_vma=False,
    )
```

```python
import math

import jax
import jax.numpy as jnp
from jax import lax
from jax.experimental import pallas as pl
from jax.experimental.pallas import tpu as pltpu
from jax.sharding import Mesh
from jax.sharding import PartitionSpec as P

HEADS = 32
KV_HEADS = 8
HEAD = 128
D = 4096
TOP = 2
EXPERTS = 8
CAP = 6
CTX = ("x", "yh", "core")
PLANE = ("x", "yh")
F32, BF16 = jnp.float32, jnp.bfloat16
TAIL = 16


def swap(value, axes):
    return lax.all_to_all(value, axes, split_axis=0, concat_axis=0, tiled=True)


def spread(value, axes):
    return swap(jnp.broadcast_to(value[None], (lax.axis_size(axes),) + value.shape), axes)


def other_core(value):
    return lax.ppermute(value, "core", [(0, 1), (1, 0)])


def to_peer(value, offset):
    return lax.ppermute(value, "hid", [(h, h ^ offset) for h in range(lax.axis_size("hid"))])


def whole(kernel, out_shapes, flops, smem=0, held=0, scratch=()):
    def call(*operands):
        spaces = [pltpu.SMEM] * smem + [pltpu.VMEM] * (len(operands) - smem - held) + [pl.ANY] * held
        moved = sum(math.prod(a.shape) * a.dtype.itemsize for a in operands)
        moved += sum(math.prod(a.shape) * a.dtype.itemsize for a in out_shapes)
        return pl.pallas_call(
            kernel,
            out_shape=out_shapes,
            in_specs=[pl.BlockSpec(memory_space=space) for space in spaces],
            out_specs=[pl.BlockSpec(memory_space=pltpu.VMEM)] * len(out_shapes),
            scratch_shapes=scratch,
            compiler_params=pltpu.CompilerParams(vmem_limit_bytes=24 * 1024 * 1024),
            cost_estimate=pl.CostEstimate(flops=flops, bytes_accessed=moved, transcendentals=0),
        )(*operands)

    return call


def dot_nt(left, right):
    return lax.dot_general(left, right, (((1,), (1,)), ((), ())), preferred_element_type=F32)


def attention_kernel(place, query, near, far, weight, out, done):
    done[...] = jnp.zeros_like(done)
    ctx, core = place[0], place[1]
    rows, keys = query.shape[0], near.shape[0]
    spot = ctx * rows + lax.broadcasted_iota(jnp.int32, (rows, keys), 0)
    column = lax.broadcasted_iota(jnp.int32, (rows, keys), 1)
    base = (column // rows) * (2 * rows) + column % rows
    scores = []
    for half, source in enumerate((near, far)):
        key_spot = base + (core ^ half) * rows
        product = dot_nt(query[...], source[:, :HEAD]) * (1.0 / math.sqrt(HEAD))
        scores.append(jnp.where(spot >= key_spot, product, -1e30))
    top = jnp.maximum(*(jnp.max(score, axis=1, keepdims=True) for score in scores))
    denom, total = 0.0, 0.0
    for score, source in zip(scores, (near, far)):
        weights = jnp.exp(score - top)
        denom = denom + jnp.sum(weights, axis=1, keepdims=True)
        total = total + jnp.dot(weights.astype(BF16), source[:, HEAD:], preferred_element_type=F32)
    attended = (total / denom).astype(BF16)
    parts, _, width = out.shape
    for part in range(parts):
        columns = weight[:, part * width : (part + 1) * width]
        out[part] = jnp.dot(attended, columns, preferred_element_type=F32).astype(BF16)


def prepare_kernel(after, ids, shares, gate, up, down, selector, mixer, weights, down_out, sems):
    peers = (sems.shape[0] - 1) // 2
    piece = gate.shape[1] // peers
    copies = [pltpu.make_async_copy(down, down_out, sems.at[2 * peers])]
    for index in range(peers):
        for which, source in enumerate((gate, up)):
            place = 2 * index + which
            taken = source.at[:, pl.ds(index * piece, piece)]
            copies.append(
                pltpu.make_async_copy(taken, weights.at[:, pl.ds(place * piece, piece)], sems.at[place])
            )
    for copy in copies:
        copy.start()
    slots, tokens = mixer.shape
    expert = lax.broadcasted_iota(jnp.int32, (EXPERTS, tokens), 0)
    named = [(expert == ids[k : k + 1, :]).astype(F32) for k in range(TOP)]
    later = lax.broadcasted_iota(jnp.int32, (tokens, tokens), 0) < lax.broadcasted_iota(
        jnp.int32, (tokens, tokens), 1
    )
    before = jnp.dot((named[0] + named[1]).astype(BF16), later.astype(BF16), preferred_element_type=F32)
    line = lax.broadcasted_iota(jnp.int32, (slots, tokens), 0)
    mixed, picked = 0.0, 0.0
    for k in range(TOP):
        slot = jnp.sum(before * named[k], axis=0, keepdims=True).astype(jnp.int32)
        hit = (line == ids[k : k + 1, :] * CAP + slot).astype(F32)
        picked = picked + hit
        mixed = mixed + hit * shares[k : k + 1, :]
    selector[...] = picked.astype(BF16)
    mixer[...] = mixed
    for copy in copies:
        copy.wait()


def select_kernel(arrived, residual, selector, stream, outgoing):
    mixed = sum(arrived[index].astype(F32) for index in range(arrived.shape[0]))
    total = residual[...].astype(F32) + mixed
    stream[...] = total
    rows = jnp.dot(selector[...], total.astype(BF16), preferred_element_type=F32)
    halves, experts, slots, _ = outgoing.shape
    for expert in range(experts):
        part = rows[expert * slots : (expert + 1) * slots, :].astype(BF16)
        for half in range(halves):
            outgoing[half, expert] = part


def share_of(place, scaled, near, far, offset, out):
    width = out.shape[1] // 2
    start = pl.multiple_of((place[2] ^ offset) * width, width)
    for index, source in enumerate((near, far)):
        product = jnp.dot(scaled, source[:, pl.ds(start, width)], preferred_element_type=F32)
        out[: scaled.shape[0], index * width : (index + 1) * width] = product.astype(BF16)


def tail_of(norm, lines):
    high = norm.astype(BF16).astype(F32)
    line = lax.broadcasted_iota(jnp.int32, (lines, norm.shape[1]), 0)
    return jnp.where(line == 0, high, jnp.where(line == 1, norm - high, 0.0)).astype(BF16)


def first_kernel(place, rows, gain, near, far, third, scaled_out, tail_out, taken, sems):
    count, depth = rows.shape
    width = third.shape[1] // 2
    start = pl.multiple_of((place[2] ^ 3) * width, width)
    copies = [
        pltpu.make_async_copy(source.at[:, pl.ds(start, width)], taken.at[index], sems.at[index])
        for index, source in enumerate((near, far))
    ]
    for copy in copies:
        copy.start()
    widened = rows[...].astype(F32)
    scaled = (widened * gain[...]).astype(BF16)
    scaled_out[...] = scaled
    square = widened * widened
    high = square.astype(BF16)
    low = (square - high.astype(F32)).astype(BF16)
    ones = jnp.ones((TAIL, depth), BF16)
    norm = (dot_nt(ones, high) + dot_nt(ones, low))[:1, :]
    norm = jnp.concatenate([norm, jnp.zeros((1, third.shape[1] - count), F32)], axis=1)
    tail = tail_of(norm, TAIL)
    third[count:, :] = tail
    tail_out[...] = tail
    for index, copy in enumerate(copies):
        copy.wait()
        product = jnp.dot(scaled, taken[index], preferred_element_type=F32)
        third[:count, index * width : (index + 1) * width] = product.astype(BF16)


def others_kernel(place, scaled, tail, near, far, second, first, own):
    for offset, out in ((2, second), (1, first), (0, own)):
        out[scaled.shape[0] :, :] = tail[...]
        share_of(place, scaled[...], near, far, offset, out)


def pair_kernel(own, arrived, first, pair, first_out):
    count = own.shape[0] - TAIL
    pair[:count, :] = (own[:count, :].astype(F32) + arrived[:count, :].astype(F32)).astype(BF16)
    tail = own[count:, :].astype(F32) + arrived[count:, :].astype(F32)
    pair[count:, :] = tail_of(tail[0:1, :] + tail[1:2, :], TAIL)
    first_out[...] = first[...]


def active_kernel(*refs):
    parts, out = refs[:-1], refs[-1]
    piece = out.shape[1]
    count = parts[0].shape[0] - TAIL
    tail = sum(part[count:, :].astype(F32) for part in parts)
    inverse = lax.rsqrt((tail[0:1, :] + tail[1:2, :]) / D + 1e-05)
    for group in range(count // piece):
        first = group * piece
        factor = jnp.broadcast_to(inverse[:, first : first + piece], (piece, piece)).T
        summed = sum(part[first : first + piece, :].astype(F32) for part in parts)
        for index in range(out.shape[0] // count):
            gate = summed[:, 2 * index * piece : (2 * index + 1) * piece] * factor
            up = summed[:, (2 * index + 1) * piece : 2 * (index + 1) * piece] * factor
            active = (gate / (1.0 + jnp.exp(-gate)) * up).astype(BF16)
            out[index * count + first : index * count + first + piece, :] = active


def down_kernel(active, near, far, out):
    count = out.shape[0]
    total = 0.0
    for index, weight in enumerate((near, far)):
        rows = slice(index * count, (index + 1) * count)
        left = jnp.concatenate([active[h, rows, :] for h in range(active.shape[0])], axis=1)
        total = total + jnp.dot(left, weight[...], preferred_element_type=F32)
    out[...] = total.astype(BF16)


def shards(
    queries,
    key_heads,
    value_heads,
    residual,
    out_weight,
    norm_gain,
    gate_weight,
    up_weight,
    down_weight,
    expert_ids,
    expert_weights,
):
    plane = lax.axis_size(PLANE)
    lines, halves = lax.axis_size("x"), lax.axis_size("yh")
    exp_count = lax.axis_size("exp")
    hid_count = lax.axis_size("hid")
    tok_rows = queries.shape[0]
    row_count = tok_rows // exp_count
    width_part = D // hid_count
    ff_part = gate_weight.shape[2]
    piece = ff_part // hid_count
    shape = jax.ShapeDtypeStruct

    with jax.named_scope("kv_gather"):
        near = spread(jnp.concatenate([key_heads, value_heads], axis=1), PLANE)
        near = near.reshape(plane * tok_rows, 2 * HEAD)
        far = other_core(near)
    with jax.named_scope("attention"):
        place = [lax.axis_index(CTX), lax.axis_index("core"), lax.axis_index("hid")]
        place = jnp.stack(place).astype(jnp.int32)
        partials, done = whole(
            attention_kernel,
            [shape((hid_count, tok_rows, width_part), BF16), shape((8, 128), F32)],
            flops=2 * tok_rows * HEAD * (4 * plane * tok_rows + D),
            smem=1,
        )(place, queries, near, far, out_weight)
    with jax.named_scope("prepare"):
        selector, mixer, near_weights, near_down = whole(
            prepare_kernel,
            [
                shape((EXPERTS * CAP, row_count), BF16),
                shape((EXPERTS * CAP, row_count), F32),
                shape((width_part, 2 * ff_part), BF16),
                shape((ff_part, width_part), BF16),
            ],
            flops=0,
            scratch=[pltpu.SemaphoreType.DMA((2 * hid_count + 1,))],
        )(done, expert_ids.T, expert_weights.T, gate_weight[0], up_weight[0], down_weight[0])
        far_weights, far_down = other_core(near_weights), other_core(near_down)
    with jax.named_scope("projection"):
        arrived = swap(partials.reshape(hid_count * exp_count, row_count, width_part), ("hid", "exp"))
        stream, outgoing = whole(
            select_kernel,
            [shape((row_count, width_part), F32), shape((halves, exp_count, CAP, width_part), BF16)],
            flops=2 * arrived.size,
        )(arrived, residual, selector)

    with jax.named_scope("dispatch"):
        arrived = swap(outgoing.reshape(halves * exp_count, CAP, width_part), ("yh", "exp"))
        arrived = spread(arrived.reshape(halves * exp_count * CAP, width_part), "x")
        count = lines * halves * exp_count * CAP
        rows = arrived.reshape(count, width_part)

    with jax.named_scope("gate_up"):
        part = shape((count + TAIL, 4 * piece), BF16)
        third, scaled, tail = whole(
            first_kernel,
            [part, shape((count, width_part), BF16), shape((TAIL, 4 * piece), BF16)],
            flops=2 * count * width_part * ff_part,
            smem=1,
            held=2,
            scratch=[pltpu.VMEM((2, width_part, 2 * piece), BF16), pltpu.SemaphoreType.DMA((2,))],
        )(place, rows, norm_gain.reshape(1, width_part), near_weights, far_weights)
        third = to_peer(third, 1)
        second, first, own = whole(
            others_kernel, [part] * 3, flops=6 * count * width_part * ff_part, smem=1
        )(place, scaled, tail, near_weights, far_weights)
        pair, first = whole(pair_kernel, [part] * 2, flops=count * piece * 8)(second, third, first)
        arrivals = [to_peer(pair, 2), to_peer(first, 1), own]
    with jax.named_scope("active"):
        (active,) = whole(active_kernel, [shape((2 * count, piece), BF16)], flops=count * piece * 40)(*arrivals)
        active = lax.all_gather(active, "hid", axis=0, tiled=False)
    with jax.named_scope("down"):
        (back,) = whole(
            down_kernel, [shape((count, width_part), BF16)], flops=4 * count * ff_part * width_part
        )(active, near_down, far_down)
        back = swap(back.reshape(lines, count // lines, width_part), "x")
        back = jnp.sum(back.astype(F32), axis=0).astype(BF16)
        back = swap(back.reshape(halves * exp_count, CAP, width_part), ("yh", "exp"))
        back = back.reshape(halves, EXPERTS * CAP, width_part).astype(F32)
        back = jnp.sum(back, axis=0)
    with jax.named_scope("combine"):
        combined = lax.dot_general(mixer, back, (((0,), (0,)), ((), ())), precision=lax.Precision.HIGHEST)
        return (stream + combined).astype(BF16)


def solution(mesh):
    ctx, exp, hid = mesh.devices.shape
    split = Mesh(mesh.devices.reshape(ctx // 4, 2, 2, exp, hid), CTX + ("exp", "hid"))
    return jax.shard_map(
        shards,
        mesh=split,
        in_specs=(
            P(CTX, ("exp", "hid")),
            P(CTX, "exp"),
            P(CTX, "exp"),
            P(CTX + ("exp",), "hid"),
            P(("exp", "hid"), None),
            P("hid"),
            P("exp", "hid", CTX),
            P("exp", "hid", CTX),
            P("exp", CTX, "hid"),
            P(CTX + ("exp",), None),
            P(CTX + ("exp",), None),
        ),
        out_specs=P(CTX + ("exp",), "hid"),
        check_vma=False,
    )
```

```python
import math

import jax
import jax.numpy as jnp
from jax import lax
from jax.experimental import pallas as pl
from jax.experimental.pallas import tpu as pltpu
from jax.sharding import Mesh
from jax.sharding import PartitionSpec as P

HEADS = 32
KV_HEADS = 8
HEAD = 128
D = 4096
TOP = 2
EXPERTS = 8
CAP = 6
CTX = ("x", "yh", "core")
PLANE = ("x", "yh")
F32, BF16 = jnp.float32, jnp.bfloat16
TAIL = 16


def swap(value, axes):
    return lax.all_to_all(value, axes, split_axis=0, concat_axis=0, tiled=True)


def spread(value, axes):
    return swap(jnp.broadcast_to(value[None], (lax.axis_size(axes),) + value.shape), axes)


def other_core(value):
    return lax.ppermute(value, "core", [(0, 1), (1, 0)])


def to_peer(value, offset):
    return lax.ppermute(value, "hid", [(h, h ^ offset) for h in range(lax.axis_size("hid"))])


def whole(kernel, out_shapes, flops, smem=0, held=0, scratch=()):
    def call(*operands):
        spaces = [pltpu.SMEM] * smem + [pltpu.VMEM] * (len(operands) - smem - held) + [pl.ANY] * held
        moved = sum(math.prod(a.shape) * a.dtype.itemsize for a in operands)
        moved += sum(math.prod(a.shape) * a.dtype.itemsize for a in out_shapes)
        return pl.pallas_call(
            kernel,
            out_shape=out_shapes,
            in_specs=[pl.BlockSpec(memory_space=space) for space in spaces],
            out_specs=[pl.BlockSpec(memory_space=pltpu.VMEM)] * len(out_shapes),
            scratch_shapes=scratch,
            compiler_params=pltpu.CompilerParams(vmem_limit_bytes=24 * 1024 * 1024),
            cost_estimate=pl.CostEstimate(flops=flops, bytes_accessed=moved, transcendentals=0),
        )(*operands)

    return call


def dot_nt(left, right):
    return lax.dot_general(left, right, (((1,), (1,)), ((), ())), preferred_element_type=F32)


def attention_kernel(place, query, near, far, weight, out, done):
    done[...] = jnp.zeros_like(done)
    ctx, core = place[0], place[1]
    rows, keys = query.shape[0], near.shape[0]
    spot = ctx * rows + lax.broadcasted_iota(jnp.int32, (rows, keys), 0)
    column = lax.broadcasted_iota(jnp.int32, (rows, keys), 1)
    base = (column // rows) * (2 * rows) + column % rows
    scores = []
    for half, source in enumerate((near, far)):
        key_spot = base + (core ^ half) * rows
        product = dot_nt(query[...], source[:, :HEAD]) * (1.0 / math.sqrt(HEAD))
        scores.append(jnp.where(spot >= key_spot, product, -1e30))
    top = jnp.maximum(*(jnp.max(score, axis=1, keepdims=True) for score in scores))
    denom, total = 0.0, 0.0
    for score, source in zip(scores, (near, far)):
        weights = jnp.exp(score - top)
        denom = denom + jnp.sum(weights, axis=1, keepdims=True)
        total = total + jnp.dot(weights.astype(BF16), source[:, HEAD:], preferred_element_type=F32)
    attended = (total / denom).astype(BF16)
    parts, _, width = out.shape
    for part in range(parts):
        columns = weight[:, part * width : (part + 1) * width]
        out[part] = jnp.dot(attended, columns, preferred_element_type=F32).astype(BF16)


def prepare_kernel(after, ids, shares, gate, up, selector, mixer, weights, sems):
    peers = sems.shape[0] // 2
    piece = gate.shape[1] // peers
    copies = []
    for index in range(peers):
        for which, source in enumerate((gate, up)):
            place = 2 * index + which
            taken = source.at[:, pl.ds(index * piece, piece)]
            copies.append(
                pltpu.make_async_copy(taken, weights.at[:, pl.ds(place * piece, piece)], sems.at[place])
            )
    for copy in copies:
        copy.start()
    slots, tokens = mixer.shape
    expert = lax.broadcasted_iota(jnp.int32, (EXPERTS, tokens), 0)
    named = [(expert == ids[k : k + 1, :]).astype(F32) for k in range(TOP)]
    later = lax.broadcasted_iota(jnp.int32, (tokens, tokens), 0) < lax.broadcasted_iota(
        jnp.int32, (tokens, tokens), 1
    )
    before = jnp.dot((named[0] + named[1]).astype(BF16), later.astype(BF16), preferred_element_type=F32)
    line = lax.broadcasted_iota(jnp.int32, (slots, tokens), 0)
    mixed, picked = 0.0, 0.0
    for k in range(TOP):
        slot = jnp.sum(before * named[k], axis=0, keepdims=True).astype(jnp.int32)
        hit = (line == ids[k : k + 1, :] * CAP + slot).astype(F32)
        picked = picked + hit
        mixed = mixed + hit * shares[k : k + 1, :]
    selector[...] = picked.astype(BF16)
    mixer[...] = mixed
    for copy in copies:
        copy.wait()


def select_kernel(arrived, residual, selector, stream, outgoing):
    mixed = sum(arrived[index].astype(F32) for index in range(arrived.shape[0]))
    total = residual[...].astype(F32) + mixed
    stream[...] = total
    rows = jnp.dot(selector[...], total.astype(BF16), preferred_element_type=F32)
    halves, experts, slots, _ = outgoing.shape
    for expert in range(experts):
        part = rows[expert * slots : (expert + 1) * slots, :].astype(BF16)
        for half in range(halves):
            outgoing[half, expert] = part


def arrange_kernel(arrived, weights, out):
    rows = jnp.concatenate([arrived[index].astype(F32) for index in range(arrived.shape[0])], axis=0).astype(BF16)
    for index in range(out.shape[0]):
        out[index] = rows


def share_of(place, scaled, near, far, offset, out):
    width = out.shape[1] // 2
    start = pl.multiple_of((place[2] ^ offset) * width, width)
    for index, source in enumerate((near, far)):
        product = jnp.dot(scaled, source[:, pl.ds(start, width)], preferred_element_type=F32)
        out[: scaled.shape[0], index * width : (index + 1) * width] = product.astype(BF16)


def tail_of(norm, lines):
    high = norm.astype(BF16).astype(F32)
    line = lax.broadcasted_iota(jnp.int32, (lines, norm.shape[1]), 0)
    return jnp.where(line == 0, high, jnp.where(line == 1, norm - high, 0.0)).astype(BF16)


def first_kernel(place, rows, gain, near, far, third, scaled_out, tail_out, taken, sems):
    count, depth = rows.shape
    width = third.shape[1] // 2
    start = pl.multiple_of((place[2] ^ 3) * width, width)
    copies = [
        pltpu.make_async_copy(source.at[:, pl.ds(start, width)], taken.at[index], sems.at[index])
        for index, source in enumerate((near, far))
    ]
    for copy in copies:
        copy.start()
    widened = rows[...].astype(F32)
    scaled = (widened * gain[...]).astype(BF16)
    scaled_out[...] = scaled
    square = widened * widened
    high = square.astype(BF16)
    low = (square - high.astype(F32)).astype(BF16)
    ones = jnp.ones((TAIL, depth), BF16)
    norm = (dot_nt(ones, high) + dot_nt(ones, low))[:1, :]
    norm = jnp.concatenate([norm, jnp.zeros((1, third.shape[1] - count), F32)], axis=1)
    tail = tail_of(norm, TAIL)
    third[count:, :] = tail
    tail_out[...] = tail
    for index, copy in enumerate(copies):
        copy.wait()
        product = jnp.dot(scaled, taken[index], preferred_element_type=F32)
        third[:count, index * width : (index + 1) * width] = product.astype(BF16)


def others_kernel(place, scaled, tail, near, far, second, first, own):
    for offset, out in ((2, second), (1, first), (0, own)):
        out[scaled.shape[0] :, :] = tail[...]
        share_of(place, scaled[...], near, far, offset, out)


def pair_kernel(own, arrived, first, pair, first_out):
    count = own.shape[0] - TAIL
    pair[:count, :] = (own[:count, :].astype(F32) + arrived[:count, :].astype(F32)).astype(BF16)
    tail = own[count:, :].astype(F32) + arrived[count:, :].astype(F32)
    pair[count:, :] = tail_of(tail[0:1, :] + tail[1:2, :], TAIL)
    first_out[...] = first[...]


def active_kernel(*refs):
    parts, out = refs[:-1], refs[-1]
    piece = out.shape[1]
    count = parts[0].shape[0] - TAIL
    tail = sum(part[count:, :].astype(F32) for part in parts)
    inverse = lax.rsqrt((tail[0:1, :] + tail[1:2, :]) / D + 1e-05)
    for group in range(count // piece):
        first = group * piece
        factor = jnp.broadcast_to(inverse[:, first : first + piece], (piece, piece)).T
        summed = sum(part[first : first + piece, :].astype(F32) for part in parts)
        for index in range(out.shape[0] // count):
            gate = summed[:, 2 * index * piece : (2 * index + 1) * piece] * factor
            up = summed[:, (2 * index + 1) * piece : 2 * (index + 1) * piece] * factor
            active = (gate / (1.0 + jnp.exp(-gate)) * up).astype(BF16)
            out[index * count + first : index * count + first + piece, :] = active


def down_kernel(active, near, far, out):
    count = out.shape[0]
    total = 0.0
    for index, weight in enumerate((near, far)):
        rows = slice(index * count, (index + 1) * count)
        left = jnp.concatenate([active[h, rows, :] for h in range(active.shape[0])], axis=1)
        total = total + jnp.dot(left, weight[...], preferred_element_type=F32)
    out[...] = total.astype(BF16)


def shards(
    queries,
    key_heads,
    value_heads,
    residual,
    out_weight,
    norm_gain,
    gate_weight,
    up_weight,
    down_weight,
    expert_ids,
    expert_weights,
):
    plane = lax.axis_size(PLANE)
    lines, halves = lax.axis_size("x"), lax.axis_size("yh")
    exp_count = lax.axis_size("exp")
    hid_count = lax.axis_size("hid")
    tok_rows = queries.shape[0]
    row_count = tok_rows // exp_count
    width_part = D // hid_count
    ff_part = gate_weight.shape[2]
    piece = ff_part // hid_count
    shape = jax.ShapeDtypeStruct

    with jax.named_scope("kv_gather"):
        near = spread(jnp.concatenate([key_heads, value_heads], axis=1), PLANE)
        near = near.reshape(plane * tok_rows, 2 * HEAD)
        far = other_core(near)
    with jax.named_scope("attention"):
        place = [lax.axis_index(CTX), lax.axis_index("core"), lax.axis_index("hid")]
        place = jnp.stack(place).astype(jnp.int32)
        partials, done = whole(
            attention_kernel,
            [shape((hid_count, tok_rows, width_part), BF16), shape((8, 128), F32)],
            flops=2 * tok_rows * HEAD * (4 * plane * tok_rows + D),
            smem=1,
        )(place, queries, near, far, out_weight)
    with jax.named_scope("prepare"):
        selector, mixer, near_weights = whole(
            prepare_kernel,
            [
                shape((EXPERTS * CAP, row_count), BF16),
                shape((EXPERTS * CAP, row_count), F32),
                shape((width_part, 2 * ff_part), BF16),
            ],
            flops=0,
            scratch=[pltpu.SemaphoreType.DMA((2 * hid_count,))],
        )(done, expert_ids.T, expert_weights.T, gate_weight[0], up_weight[0])
        near_down = down_weight[0]
        far_weights, far_down = other_core(near_weights), other_core(near_down)
    with jax.named_scope("projection"):
        arrived = swap(partials.reshape(hid_count * exp_count, row_count, width_part), ("hid", "exp"))
        stream, outgoing = whole(
            select_kernel,
            [shape((row_count, width_part), F32), shape((halves, exp_count, CAP, width_part), BF16)],
            flops=2 * arrived.size,
        )(arrived, residual, selector)

    with jax.named_scope("dispatch"):
        arrived = swap(outgoing.reshape(halves * exp_count, CAP, width_part), ("yh", "exp"))
        (copies,) = whole(
            arrange_kernel,
            [shape((lines, halves * exp_count * CAP, width_part), BF16)],
            flops=0,
            held=1,
        )(arrived, far_weights)
        arrived = swap(copies, "x")
        count = lines * halves * exp_count * CAP
        rows = arrived.reshape(count, width_part)

    with jax.named_scope("gate_up"):
        part = shape((count + TAIL, 4 * piece), BF16)
        third, scaled, tail = whole(
            first_kernel,
            [part, shape((count, width_part), BF16), shape((TAIL, 4 * piece), BF16)],
            flops=2 * count * width_part * ff_part,
            smem=1,
            held=2,
            scratch=[pltpu.VMEM((2, width_part, 2 * piece), BF16), pltpu.SemaphoreType.DMA((2,))],
        )(place, rows, norm_gain.reshape(1, width_part), near_weights, far_weights)
        third = to_peer(third, 1)
        second, first, own = whole(
            others_kernel, [part] * 3, flops=6 * count * width_part * ff_part, smem=1
        )(place, scaled, tail, near_weights, far_weights)
        pair, first = whole(pair_kernel, [part] * 2, flops=count * piece * 8)(second, third, first)
        arrivals = [to_peer(pair, 2), to_peer(first, 1), own]
    with jax.named_scope("active"):
        (active,) = whole(active_kernel, [shape((2 * count, piece), BF16)], flops=count * piece * 40)(*arrivals)
        active = lax.all_gather(active, "hid", axis=0, tiled=False)
    with jax.named_scope("down"):
        (back,) = whole(
            down_kernel, [shape((count, width_part), BF16)], flops=4 * count * ff_part * width_part
        )(active, near_down, far_down)
        back = swap(back.reshape(lines, count // lines, width_part), "x")
        back = jnp.sum(back.astype(F32), axis=0).astype(BF16)
        back = swap(back.reshape(halves * exp_count, CAP, width_part), ("yh", "exp"))
        back = back.reshape(halves, EXPERTS * CAP, width_part).astype(F32)
        back = jnp.sum(back, axis=0)
    with jax.named_scope("combine"):
        combined = lax.dot_general(mixer, back, (((0,), (0,)), ((), ())), precision=lax.Precision.HIGHEST)
        return (stream + combined).astype(BF16)


def solution(mesh):
    ctx, exp, hid = mesh.devices.shape
    split = Mesh(mesh.devices.reshape(ctx // 4, 2, 2, exp, hid), CTX + ("exp", "hid"))
    return jax.shard_map(
        shards,
        mesh=split,
        in_specs=(
            P(CTX, ("exp", "hid")),
            P(CTX, "exp"),
            P(CTX, "exp"),
            P(CTX + ("exp",), "hid"),
            P(("exp", "hid"), None),
            P("hid"),
            P("exp", "hid", CTX),
            P("exp", "hid", CTX),
            P("exp", CTX, "hid"),
            P(CTX + ("exp",), None),
            P(CTX + ("exp",), None),
        ),
        out_specs=P(CTX + ("exp",), "hid"),
        check_vma=False,
    )
```

```python
import math

import jax
import jax.numpy as jnp
from jax import lax
from jax.experimental import pallas as pl
from jax.experimental.pallas import tpu as pltpu
from jax.sharding import Mesh
from jax.sharding import PartitionSpec as P

HEADS = 32
KV_HEADS = 8
HEAD = 128
D = 4096
TOP = 2
EXPERTS = 8
CAP = 6
CTX = ("x", "yh", "core")
PLANE = ("x", "yh")
F32, BF16 = jnp.float32, jnp.bfloat16
TAIL = 16


def swap(value, axes):
    return lax.all_to_all(value, axes, split_axis=0, concat_axis=0, tiled=True)


def spread(value, axes):
    return swap(jnp.broadcast_to(value[None], (lax.axis_size(axes),) + value.shape), axes)


def other_core(value):
    return lax.ppermute(value, "core", [(0, 1), (1, 0)])


def to_peer(value, offset):
    return lax.ppermute(value, "hid", [(h, h ^ offset) for h in range(lax.axis_size("hid"))])


def whole(kernel, out_shapes, flops, smem=0, held=0, scratch=()):
    def call(*operands):
        spaces = [pltpu.SMEM] * smem + [pltpu.VMEM] * (len(operands) - smem - held) + [pl.ANY] * held
        moved = sum(math.prod(a.shape) * a.dtype.itemsize for a in operands)
        moved += sum(math.prod(a.shape) * a.dtype.itemsize for a in out_shapes)
        return pl.pallas_call(
            kernel,
            out_shape=out_shapes,
            in_specs=[pl.BlockSpec(memory_space=space) for space in spaces],
            out_specs=[pl.BlockSpec(memory_space=pltpu.VMEM)] * len(out_shapes),
            scratch_shapes=scratch,
            compiler_params=pltpu.CompilerParams(vmem_limit_bytes=24 * 1024 * 1024),
            cost_estimate=pl.CostEstimate(flops=flops, bytes_accessed=moved, transcendentals=0),
        )(*operands)

    return call


def dot_nt(left, right):
    return lax.dot_general(left, right, (((1,), (1,)), ((), ())), preferred_element_type=F32)


def attention_kernel(place, packed, near, far, weight, out, done):
    done[...] = jnp.zeros_like(done)
    ctx, core = place[0], place[1]
    rows, keys = packed.shape[0], near.shape[0]
    query = packed[:, 2 * HEAD :]
    spot = ctx * rows + lax.broadcasted_iota(jnp.int32, (rows, keys), 0)
    column = lax.broadcasted_iota(jnp.int32, (rows, keys), 1)
    base = (column // rows) * (2 * rows) + column % rows
    scores = []
    for half, source in enumerate((near, far)):
        key_spot = base + (core ^ half) * rows
        product = dot_nt(query, source[:, :HEAD]) * (1.0 / math.sqrt(HEAD))
        scores.append(jnp.where(spot >= key_spot, product, -1e30))
    top = jnp.maximum(*(jnp.max(score, axis=1, keepdims=True) for score in scores))
    denom, total = 0.0, 0.0
    for score, source in zip(scores, (near, far)):
        weights = jnp.exp(score - top)
        denom = denom + jnp.sum(weights, axis=1, keepdims=True)
        total = total + jnp.dot(weights.astype(BF16), source[:, HEAD:], preferred_element_type=F32)
    attended = (total / denom).astype(BF16)
    parts, _, width = out.shape
    for part in range(parts):
        columns = weight[:, part * width : (part + 1) * width]
        out[part] = jnp.dot(attended, columns, preferred_element_type=F32).astype(BF16)


def prepare_kernel(after, ids, shares, gate, up, selector, mixer, weights, sems):
    peers = sems.shape[0] // 2
    piece = gate.shape[1] // peers
    copies = []
    for index in range(peers):
        for which, source in enumerate((gate, up)):
            place = 2 * index + which
            taken = source.at[:, pl.ds(index * piece, piece)]
            copies.append(
                pltpu.make_async_copy(taken, weights.at[:, pl.ds(place * piece, piece)], sems.at[place])
            )
    for copy in copies:
        copy.start()
    slots, tokens = mixer.shape
    expert = lax.broadcasted_iota(jnp.int32, (EXPERTS, tokens), 0)
    named = [(expert == ids[k : k + 1, :]).astype(F32) for k in range(TOP)]
    later = lax.broadcasted_iota(jnp.int32, (tokens, tokens), 0) < lax.broadcasted_iota(
        jnp.int32, (tokens, tokens), 1
    )
    before = jnp.dot((named[0] + named[1]).astype(BF16), later.astype(BF16), preferred_element_type=F32)
    line = lax.broadcasted_iota(jnp.int32, (slots, tokens), 0)
    mixed, picked = 0.0, 0.0
    for k in range(TOP):
        slot = jnp.sum(before * named[k], axis=0, keepdims=True).astype(jnp.int32)
        hit = (line == ids[k : k + 1, :] * CAP + slot).astype(F32)
        picked = picked + hit
        mixed = mixed + hit * shares[k : k + 1, :]
    selector[...] = picked.astype(BF16)
    mixer[...] = mixed
    for copy in copies:
        copy.wait()


def select_kernel(arrived, residual, selector, stream, outgoing):
    mixed = sum(arrived[index].astype(F32) for index in range(arrived.shape[0]))
    total = residual[...].astype(F32) + mixed
    stream[...] = total
    rows = jnp.dot(selector[...], total.astype(BF16), preferred_element_type=F32)
    halves, experts, slots, _ = outgoing.shape
    for expert in range(experts):
        part = rows[expert * slots : (expert + 1) * slots, :].astype(BF16)
        for half in range(halves):
            outgoing[half, expert] = part


def arrange_kernel(arrived, weights, out):
    rows = jnp.concatenate([arrived[index].astype(F32) for index in range(arrived.shape[0])], axis=0).astype(BF16)
    for index in range(out.shape[0]):
        out[index] = rows


def share_of(place, scaled, near, far, offset, out):
    width = out.shape[1] // 2
    start = pl.multiple_of((place[2] ^ offset) * width, width)
    for index, source in enumerate((near, far)):
        product = jnp.dot(scaled, source[:, pl.ds(start, width)], preferred_element_type=F32)
        out[: scaled.shape[0], index * width : (index + 1) * width] = product.astype(BF16)


def tail_of(norm, lines):
    high = norm.astype(BF16).astype(F32)
    line = lax.broadcasted_iota(jnp.int32, (lines, norm.shape[1]), 0)
    return jnp.where(line == 0, high, jnp.where(line == 1, norm - high, 0.0)).astype(BF16)


def first_kernel(place, rows, gain, near, far, third, scaled_out, tail_out, taken, sems):
    count, depth = rows.shape
    width = third.shape[1] // 2
    start = pl.multiple_of((place[2] ^ 3) * width, width)
    copies = [
        pltpu.make_async_copy(source.at[:, pl.ds(start, width)], taken.at[index], sems.at[index])
        for index, source in enumerate((near, far))
    ]
    for copy in copies:
        copy.start()
    widened = rows[...].astype(F32)
    scaled = (widened * gain[...]).astype(BF16)
    scaled_out[...] = scaled
    square = widened * widened
    high = square.astype(BF16)
    low = (square - high.astype(F32)).astype(BF16)
    ones = jnp.ones((TAIL, depth), BF16)
    norm = (dot_nt(ones, high) + dot_nt(ones, low))[:1, :]
    norm = jnp.concatenate([norm, jnp.zeros((1, third.shape[1] - count), F32)], axis=1)
    tail = tail_of(norm, TAIL)
    third[count:, :] = tail
    tail_out[...] = tail
    for index, copy in enumerate(copies):
        copy.wait()
        product = jnp.dot(scaled, taken[index], preferred_element_type=F32)
        third[:count, index * width : (index + 1) * width] = product.astype(BF16)


def others_kernel(place, scaled, tail, near, far, second, first, own):
    for offset, out in ((2, second), (1, first), (0, own)):
        out[scaled.shape[0] :, :] = tail[...]
        share_of(place, scaled[...], near, far, offset, out)


def pair_kernel(own, arrived, first, pair, first_out):
    count = own.shape[0] - TAIL
    pair[:count, :] = (own[:count, :].astype(F32) + arrived[:count, :].astype(F32)).astype(BF16)
    tail = own[count:, :].astype(F32) + arrived[count:, :].astype(F32)
    pair[count:, :] = tail_of(tail[0:1, :] + tail[1:2, :], TAIL)
    first_out[...] = first[...]


def active_kernel(*refs):
    parts, out = refs[:-1], refs[-1]
    piece = out.shape[1]
    count = parts[0].shape[0] - TAIL
    tail = sum(part[count:, :].astype(F32) for part in parts)
    inverse = lax.rsqrt((tail[0:1, :] + tail[1:2, :]) / D + 1e-05)
    for group in range(count // piece):
        first = group * piece
        factor = jnp.broadcast_to(inverse[:, first : first + piece], (piece, piece)).T
        summed = sum(part[first : first + piece, :].astype(F32) for part in parts)
        for index in range(out.shape[0] // count):
            gate = summed[:, 2 * index * piece : (2 * index + 1) * piece] * factor
            up = summed[:, (2 * index + 1) * piece : 2 * (index + 1) * piece] * factor
            active = (gate / (1.0 + jnp.exp(-gate)) * up).astype(BF16)
            out[index * count + first : index * count + first + piece, :] = active


def down_kernel(active, near, far, out):
    count = out.shape[0]
    total = 0.0
    for index, weight in enumerate((near, far)):
        rows = slice(index * count, (index + 1) * count)
        left = jnp.concatenate([active[h, rows, :] for h in range(active.shape[0])], axis=1)
        total = total + jnp.dot(left, weight[...], preferred_element_type=F32)
    out[...] = total.astype(BF16)


def combine_kernel(back, mixer, stream, out):
    experts = back.shape[0] // 2
    rows = [back[e].astype(F32) + back[experts + e].astype(F32) for e in range(experts)]
    combined = lax.dot_general(
        mixer[...],
        jnp.concatenate(rows, axis=0),
        (((0,), (0,)), ((), ())),
        precision=lax.Precision.HIGHEST,
        preferred_element_type=F32,
    )
    out[...] = (stream[...] + combined).astype(BF16)


def shards(
    queries,
    key_heads,
    value_heads,
    residual,
    out_weight,
    norm_gain,
    gate_weight,
    up_weight,
    down_weight,
    expert_ids,
    expert_weights,
):
    plane = lax.axis_size(PLANE)
    lines, halves = lax.axis_size("x"), lax.axis_size("yh")
    exp_count = lax.axis_size("exp")
    hid_count = lax.axis_size("hid")
    tok_rows = queries.shape[0]
    row_count = tok_rows // exp_count
    width_part = D // hid_count
    ff_part = gate_weight.shape[2]
    piece = ff_part // hid_count
    shape = jax.ShapeDtypeStruct

    with jax.named_scope("kv_gather"):
        packed = lax.optimization_barrier(jnp.concatenate([key_heads, value_heads, queries], axis=1))
        near = spread(packed[:, : 2 * HEAD], PLANE)
        near = near.reshape(plane * tok_rows, 2 * HEAD)
        far = other_core(near)
    with jax.named_scope("attention"):
        place = [lax.axis_index(CTX), lax.axis_index("core"), lax.axis_index("hid")]
        place = jnp.stack(place).astype(jnp.int32)
        partials, done = whole(
            attention_kernel,
            [shape((hid_count, tok_rows, width_part), BF16), shape((8, 128), F32)],
            flops=2 * tok_rows * HEAD * (4 * plane * tok_rows + D),
            smem=1,
        )(place, packed, near, far, out_weight)
    with jax.named_scope("prepare"):
        selector, mixer, near_weights = whole(
            prepare_kernel,
            [
                shape((EXPERTS * CAP, row_count), BF16),
                shape((EXPERTS * CAP, row_count), F32),
                shape((width_part, 2 * ff_part), BF16),
            ],
            flops=0,
            scratch=[pltpu.SemaphoreType.DMA((2 * hid_count,))],
        )(done, expert_ids.T, expert_weights.T, gate_weight[0], up_weight[0])
        near_down = down_weight[0]
        far_weights, far_down = other_core(near_weights), other_core(near_down)
    with jax.named_scope("projection"):
        arrived = swap(partials.reshape(hid_count * exp_count, row_count, width_part), ("hid", "exp"))
        stream, outgoing = whole(
            select_kernel,
            [shape((row_count, width_part), F32), shape((halves, exp_count, CAP, width_part), BF16)],
            flops=2 * arrived.size,
        )(arrived, residual, selector)

    with jax.named_scope("dispatch"):
        arrived = swap(outgoing.reshape(halves * exp_count, CAP, width_part), ("yh", "exp"))
        (copies,) = whole(
            arrange_kernel,
            [shape((lines, halves * exp_count * CAP, width_part), BF16)],
            flops=0,
            held=1,
        )(arrived, far_weights)
        arrived = swap(copies, "x")
        count = lines * halves * exp_count * CAP
        rows = arrived.reshape(count, width_part)

    with jax.named_scope("gate_up"):
        part = shape((count + TAIL, 4 * piece), BF16)
        third, scaled, tail = whole(
            first_kernel,
            [part, shape((count, width_part), BF16), shape((TAIL, 4 * piece), BF16)],
            flops=2 * count * width_part * ff_part,
            smem=1,
            held=2,
            scratch=[pltpu.VMEM((2, width_part, 2 * piece), BF16), pltpu.SemaphoreType.DMA((2,))],
        )(place, rows, norm_gain.reshape(1, width_part), near_weights, far_weights)
        third = to_peer(third, 1)
        second, first, own = whole(
            others_kernel, [part] * 3, flops=6 * count * width_part * ff_part, smem=1
        )(place, scaled, tail, near_weights, far_weights)
        pair, first = whole(pair_kernel, [part] * 2, flops=count * piece * 8)(second, third, first)
        arrivals = [to_peer(pair, 2), to_peer(first, 1), own]
    with jax.named_scope("active"):
        (active,) = whole(active_kernel, [shape((2 * count, piece), BF16)], flops=count * piece * 40)(*arrivals)
        active = lax.all_gather(active, "hid", axis=0, tiled=False)
    with jax.named_scope("down"):
        (back,) = whole(
            down_kernel, [shape((count, width_part), BF16)], flops=4 * count * ff_part * width_part
        )(active, near_down, far_down)
        back = swap(back.reshape(lines, count // lines, width_part), "x")
        back = jnp.sum(back.astype(F32), axis=0).astype(BF16)
        back = swap(back.reshape(halves * exp_count, CAP, width_part), ("yh", "exp"))
    with jax.named_scope("combine"):
        (out,) = whole(combine_kernel, [shape((row_count, width_part), BF16)], flops=2 * back.size)(
            back, mixer, stream
        )
    return out


def solution(mesh):
    ctx, exp, hid = mesh.devices.shape
    split = Mesh(mesh.devices.reshape(ctx // 4, 2, 2, exp, hid), CTX + ("exp", "hid"))
    return jax.shard_map(
        shards,
        mesh=split,
        in_specs=(
            P(CTX, ("exp", "hid")),
            P(CTX, "exp"),
            P(CTX, "exp"),
            P(CTX + ("exp",), "hid"),
            P(("exp", "hid"), None),
            P("hid"),
            P("exp", "hid", CTX),
            P("exp", "hid", CTX),
            P("exp", CTX, "hid"),
            P(CTX + ("exp",), None),
            P(CTX + ("exp",), None),
        ),
        out_specs=P(CTX + ("exp",), "hid"),
        check_vma=False,
    )
```

```python
import functools
import math

import jax
import jax.numpy as jnp
from jax import lax
from jax.experimental import pallas as pl
from jax.experimental.pallas import tpu as pltpu
from jax.sharding import Mesh
from jax.sharding import PartitionSpec as P

HEADS = 32
KV_HEADS = 8
HEAD = 128
D = 4096
TOP = 2
EXPERTS = 8
CAP = 6
CTX = ("x", "yh", "core")
PLANE = ("yh", "x")
F32, BF16 = jnp.float32, jnp.bfloat16
TAIL = 16


def swap(value, axes):
    return lax.all_to_all(value, axes, split_axis=0, concat_axis=0, tiled=True)


def spread(value, axes):
    return swap(jnp.broadcast_to(value[None], (lax.axis_size(axes),) + value.shape), axes)


def other_core(value):
    return lax.ppermute(value, "core", [(0, 1), (1, 0)])


def to_peer(value, offset):
    return lax.ppermute(value, "hid", [(h, h ^ offset) for h in range(lax.axis_size("hid"))])


def whole(kernel, out_shapes, flops, smem=0, held=0, scratch=()):
    def call(*operands):
        spaces = [pltpu.SMEM] * smem + [pltpu.VMEM] * (len(operands) - smem - held) + [pl.ANY] * held
        moved = sum(math.prod(a.shape) * a.dtype.itemsize for a in operands)
        moved += sum(math.prod(a.shape) * a.dtype.itemsize for a in out_shapes)
        return pl.pallas_call(
            kernel,
            out_shape=out_shapes,
            in_specs=[pl.BlockSpec(memory_space=space) for space in spaces],
            out_specs=[pl.BlockSpec(memory_space=pltpu.VMEM)] * len(out_shapes),
            scratch_shapes=scratch,
            compiler_params=pltpu.CompilerParams(vmem_limit_bytes=24 * 1024 * 1024),
            cost_estimate=pl.CostEstimate(flops=flops, bytes_accessed=moved, transcendentals=0),
        )(*operands)

    return call


def dot_nt(left, right):
    return lax.dot_general(left, right, (((1,), (1,)), ((), ())), preferred_element_type=F32)


def attention_kernel(lines, place, packed, near, far, weight, out, done):
    done[...] = jnp.zeros_like(done)
    ctx, core = place[0], place[1]
    rows, keys = packed.shape[0], near.shape[0]
    query = packed[:, 2 * HEAD :]
    spot = ctx * rows + lax.broadcasted_iota(jnp.int32, (rows, keys), 0)
    column = lax.broadcasted_iota(jnp.int32, (rows, keys), 1)
    block = column // rows
    base = ((block % lines) * (keys // rows // lines) + block // lines) * (2 * rows) + column % rows
    scores = []
    for half, source in enumerate((near, far)):
        key_spot = base + (core ^ half) * rows
        product = dot_nt(query, source[:, :HEAD]) * (1.0 / math.sqrt(HEAD))
        scores.append(jnp.where(spot >= key_spot, product, -1e30))
    top = jnp.maximum(*(jnp.max(score, axis=1, keepdims=True) for score in scores))
    denom, total = 0.0, 0.0
    for score, source in zip(scores, (near, far)):
        weights = jnp.exp(score - top)
        denom = denom + jnp.sum(weights, axis=1, keepdims=True)
        total = total + jnp.dot(weights.astype(BF16), source[:, HEAD:], preferred_element_type=F32)
    attended = (total / denom).astype(BF16)
    blocks, parts, tokens, width = out.shape
    for part in range(parts):
        columns = weight[:, part * width : (part + 1) * width]
        product = jnp.dot(attended, columns, preferred_element_type=F32).astype(BF16)
        for index in range(blocks):
            out[index, part] = product[index * tokens : (index + 1) * tokens, :]


def prepare_kernel(after, ids, shares, gate, up, selector, mixer, weights, sems):
    peers = sems.shape[0] // 2
    piece = gate.shape[1] // peers
    copies = []
    for index in range(peers):
        for which, source in enumerate((gate, up)):
            place = 2 * index + which
            taken = source.at[:, pl.ds(index * piece, piece)]
            copies.append(
                pltpu.make_async_copy(taken, weights.at[:, pl.ds(place * piece, piece)], sems.at[place])
            )
    for copy in copies:
        copy.start()
    slots, tokens = mixer.shape
    expert = lax.broadcasted_iota(jnp.int32, (EXPERTS, tokens), 0)
    named = [(expert == ids[k : k + 1, :]).astype(F32) for k in range(TOP)]
    later = lax.broadcasted_iota(jnp.int32, (tokens, tokens), 0) < lax.broadcasted_iota(
        jnp.int32, (tokens, tokens), 1
    )
    before = jnp.dot((named[0] + named[1]).astype(BF16), later.astype(BF16), preferred_element_type=F32)
    line = lax.broadcasted_iota(jnp.int32, (slots, tokens), 0)
    mixed, picked = 0.0, 0.0
    for k in range(TOP):
        slot = jnp.sum(before * named[k], axis=0, keepdims=True).astype(jnp.int32)
        hit = (line == ids[k : k + 1, :] * CAP + slot).astype(F32)
        picked = picked + hit
        mixed = mixed + hit * shares[k : k + 1, :]
    selector[...] = picked.astype(BF16)
    mixer[...] = mixed
    for copy in copies:
        copy.wait()


def select_kernel(arrived, residual, selector, stream, outgoing):
    mixed = sum(arrived[index].astype(F32) for index in range(arrived.shape[0]))
    total = residual[...].astype(F32) + mixed
    stream[...] = total
    rows = jnp.dot(selector[...], total.astype(BF16), preferred_element_type=F32)
    experts, halves, slots, _ = outgoing.shape
    for expert in range(experts):
        part = rows[expert * slots : (expert + 1) * slots, :].astype(BF16)
        for half in range(halves):
            outgoing[expert, half] = part


def arrange_kernel(arrived, weights, out):
    rows = jnp.concatenate([arrived[index].astype(F32) for index in range(arrived.shape[0])], axis=0).astype(BF16)
    for index in range(out.shape[0]):
        out[index] = rows


def share_of(place, scaled, near, far, offset, out):
    width = out.shape[1] // 2
    start = pl.multiple_of((place[2] ^ offset) * width, width)
    for index, source in enumerate((near, far)):
        product = jnp.dot(scaled, source[:, pl.ds(start, width)], preferred_element_type=F32)
        out[: scaled.shape[0], index * width : (index + 1) * width] = product.astype(BF16)


def tail_of(norm, lines):
    high = norm.astype(BF16).astype(F32)
    line = lax.broadcasted_iota(jnp.int32, (lines, norm.shape[1]), 0)
    return jnp.where(line == 0, high, jnp.where(line == 1, norm - high, 0.0)).astype(BF16)


def first_kernel(place, rows, gain, near, far, third, scaled_out, tail_out, taken, sems):
    count, depth = rows.shape
    width = third.shape[1] // 2
    start = pl.multiple_of((place[2] ^ 3) * width, width)
    copies = [
        pltpu.make_async_copy(source.at[:, pl.ds(start, width)], taken.at[index], sems.at[index])
        for index, source in enumerate((near, far))
    ]
    for copy in copies:
        copy.start()
    widened = rows[...].astype(F32)
    scaled = (widened * gain[...]).astype(BF16)
    scaled_out[...] = scaled
    square = widened * widened
    high = square.astype(BF16)
    low = (square - high.astype(F32)).astype(BF16)
    ones = jnp.ones((TAIL, depth), BF16)
    norm = (dot_nt(ones, high) + dot_nt(ones, low))[:1, :]
    norm = jnp.concatenate([norm, jnp.zeros((1, third.shape[1] - count), F32)], axis=1)
    tail = tail_of(norm, TAIL)
    third[count:, :] = tail
    tail_out[...] = tail
    for index, copy in enumerate(copies):
        copy.wait()
        product = jnp.dot(scaled, taken[index], preferred_element_type=F32)
        third[:count, index * width : (index + 1) * width] = product.astype(BF16)


def others_kernel(place, scaled, tail, near, far, second, first, own):
    for offset, out in ((2, second), (1, first), (0, own)):
        out[scaled.shape[0] :, :] = tail[...]
        share_of(place, scaled[...], near, far, offset, out)


def pair_kernel(own, arrived, first, pair, first_out):
    count = own.shape[0] - TAIL
    pair[:count, :] = (own[:count, :].astype(F32) + arrived[:count, :].astype(F32)).astype(BF16)
    tail = own[count:, :].astype(F32) + arrived[count:, :].astype(F32)
    pair[count:, :] = tail_of(tail[0:1, :] + tail[1:2, :], TAIL)
    first_out[...] = first[...]


def active_kernel(*refs):
    parts, out = refs[:-1], refs[-1]
    piece = out.shape[1]
    count = parts[0].shape[0] - TAIL
    tail = sum(part[count:, :].astype(F32) for part in parts)
    inverse = lax.rsqrt((tail[0:1, :] + tail[1:2, :]) / D + 1e-05)
    for group in range(count // piece):
        first = group * piece
        factor = jnp.broadcast_to(inverse[:, first : first + piece], (piece, piece)).T
        summed = sum(part[first : first + piece, :].astype(F32) for part in parts)
        for index in range(out.shape[0] // count):
            gate = summed[:, 2 * index * piece : (2 * index + 1) * piece] * factor
            up = summed[:, (2 * index + 1) * piece : 2 * (index + 1) * piece] * factor
            active = (gate / (1.0 + jnp.exp(-gate)) * up).astype(BF16)
            out[index * count + first : index * count + first + piece, :] = active


def down_kernel(active, near, far, out):
    count = out.shape[0]
    total = 0.0
    for index, weight in enumerate((near, far)):
        rows = slice(index * count, (index + 1) * count)
        left = jnp.concatenate([active[h, rows, :] for h in range(active.shape[0])], axis=1)
        total = total + jnp.dot(left, weight[...], preferred_element_type=F32)
    out[...] = total.astype(BF16)


def combine_kernel(back, mixer, stream, out):
    rows = [back[2 * e].astype(F32) + back[2 * e + 1].astype(F32) for e in range(back.shape[0] // 2)]
    combined = lax.dot_general(
        mixer[...],
        jnp.concatenate(rows, axis=0),
        (((0,), (0,)), ((), ())),
        precision=lax.Precision.HIGHEST,
        preferred_element_type=F32,
    )
    out[...] = (stream[...] + combined).astype(BF16)


def shards(
    queries,
    key_heads,
    value_heads,
    residual,
    out_weight,
    norm_gain,
    gate_weight,
    up_weight,
    down_weight,
    expert_ids,
    expert_weights,
):
    plane = lax.axis_size(PLANE)
    lines, halves = lax.axis_size("x"), lax.axis_size("yh")
    exp_count = lax.axis_size("exp")
    hid_count = lax.axis_size("hid")
    tok_rows = queries.shape[0]
    row_count = tok_rows // exp_count
    width_part = D // hid_count
    ff_part = gate_weight.shape[2]
    piece = ff_part // hid_count
    shape = jax.ShapeDtypeStruct

    with jax.named_scope("kv_gather"):
        packed = lax.optimization_barrier(jnp.concatenate([key_heads, value_heads, queries], axis=1))
        near = spread(packed[:, : 2 * HEAD], PLANE)
        near = near.reshape(plane * tok_rows, 2 * HEAD)
        far = other_core(near)
    with jax.named_scope("attention"):
        place = [lax.axis_index(CTX), lax.axis_index("core"), lax.axis_index("hid")]
        place = jnp.stack(place).astype(jnp.int32)
        partials, done = whole(
            functools.partial(attention_kernel, lines),
            [shape((exp_count, hid_count, row_count, width_part), BF16), shape((8, 128), F32)],
            flops=2 * tok_rows * HEAD * (4 * plane * tok_rows + D),
            smem=1,
        )(place, packed, near, far, out_weight)
    with jax.named_scope("prepare"):
        selector, mixer, near_weights = whole(
            prepare_kernel,
            [
                shape((EXPERTS * CAP, row_count), BF16),
                shape((EXPERTS * CAP, row_count), F32),
                shape((width_part, 2 * ff_part), BF16),
            ],
            flops=0,
            scratch=[pltpu.SemaphoreType.DMA((2 * hid_count,))],
        )(done, expert_ids.T, expert_weights.T, gate_weight[0], up_weight[0])
        near_down = down_weight[0]
        far_weights, far_down = other_core(near_weights), other_core(near_down)
    with jax.named_scope("projection"):
        arrived = swap(partials.reshape(exp_count * hid_count, row_count, width_part), ("exp", "hid"))
        stream, outgoing = whole(
            select_kernel,
            [shape((row_count, width_part), F32), shape((exp_count, halves, CAP, width_part), BF16)],
            flops=2 * arrived.size,
        )(arrived, residual, selector)

    with jax.named_scope("dispatch"):
        arrived = swap(outgoing.reshape(exp_count * halves, CAP, width_part), ("exp", "yh"))
        (copies,) = whole(
            arrange_kernel,
            [shape((lines, halves * exp_count * CAP, width_part), BF16)],
            flops=0,
            held=1,
        )(arrived, far_weights)
        arrived = swap(copies, "x")
        count = lines * halves * exp_count * CAP
        rows = arrived.reshape(count, width_part)

    with jax.named_scope("gate_up"):
        part = shape((count + TAIL, 4 * piece), BF16)
        third, scaled, tail = whole(
            first_kernel,
            [part, shape((count, width_part), BF16), shape((TAIL, 4 * piece), BF16)],
            flops=2 * count * width_part * ff_part,
            smem=1,
            held=2,
            scratch=[pltpu.VMEM((2, width_part, 2 * piece), BF16), pltpu.SemaphoreType.DMA((2,))],
        )(place, rows, norm_gain.reshape(1, width_part), near_weights, far_weights)
        third = to_peer(third, 1)
        second, first, own = whole(
            others_kernel, [part] * 3, flops=6 * count * width_part * ff_part, smem=1
        )(place, scaled, tail, near_weights, far_weights)
        pair, first = whole(pair_kernel, [part] * 2, flops=count * piece * 8)(second, third, first)
        arrivals = [to_peer(pair, 2), to_peer(first, 1), own]
    with jax.named_scope("active"):
        (active,) = whole(active_kernel, [shape((2 * count, piece), BF16)], flops=count * piece * 40)(*arrivals)
        active = lax.all_gather(active, "hid", axis=0, tiled=False)
    with jax.named_scope("down"):
        (back,) = whole(
            down_kernel, [shape((count, width_part), BF16)], flops=4 * count * ff_part * width_part
        )(active, near_down, far_down)
        back = swap(back.reshape(lines, count // lines, width_part), "x")
        back = jnp.sum(back.astype(F32), axis=0).astype(BF16)
        back = swap(back.reshape(exp_count * halves, CAP, width_part), ("exp", "yh"))
    with jax.named_scope("combine"):
        (out,) = whole(combine_kernel, [shape((row_count, width_part), BF16)], flops=2 * back.size)(
            back, mixer, stream
        )
    return out


def solution(mesh):
    ctx, exp, hid = mesh.devices.shape
    split = Mesh(mesh.devices.reshape(ctx // 4, 2, 2, exp, hid), CTX + ("exp", "hid"))
    return jax.shard_map(
        shards,
        mesh=split,
        in_specs=(
            P(CTX, ("exp", "hid")),
            P(CTX, "exp"),
            P(CTX, "exp"),
            P(CTX + ("exp",), "hid"),
            P(("exp", "hid"), None),
            P("hid"),
            P("exp", "hid", CTX),
            P("exp", "hid", CTX),
            P("exp", CTX, "hid"),
            P(CTX + ("exp",), None),
            P(CTX + ("exp",), None),
        ),
        out_specs=P(CTX + ("exp",), "hid"),
        check_vma=False,
    )
```

```python
import math

import jax
import jax.numpy as jnp
from jax import lax
from jax.experimental import pallas as pl
from jax.experimental.pallas import tpu as pltpu
from jax.sharding import Mesh
from jax.sharding import PartitionSpec as P

HEADS = 32
KV_HEADS = 8
HEAD = 128
D = 4096
TOP = 2
EXPERTS = 8
CAP = 6
CTX = ("x", "yh", "core")
PLANE = ("x", "yh")
F32, BF16 = jnp.float32, jnp.bfloat16
TAIL = 16


def swap(value, axes):
    return lax.all_to_all(value, axes, split_axis=0, concat_axis=0, tiled=True)


def spread(value, axes):
    return swap(jnp.broadcast_to(value[None], (lax.axis_size(axes),) + value.shape), axes)


def other_core(value):
    return lax.ppermute(value, "core", [(0, 1), (1, 0)])


def to_peer(value, offset):
    return lax.ppermute(value, "hid", [(h, h ^ offset) for h in range(lax.axis_size("hid"))])


def whole(kernel, out_shapes, flops, smem=0, held=0, scratch=()):
    def call(*operands):
        spaces = [pltpu.SMEM] * smem + [pltpu.VMEM] * (len(operands) - smem - held) + [pl.ANY] * held
        moved = sum(math.prod(a.shape) * a.dtype.itemsize for a in operands)
        moved += sum(math.prod(a.shape) * a.dtype.itemsize for a in out_shapes)
        return pl.pallas_call(
            kernel,
            out_shape=out_shapes,
            in_specs=[pl.BlockSpec(memory_space=space) for space in spaces],
            out_specs=[pl.BlockSpec(memory_space=pltpu.VMEM)] * len(out_shapes),
            scratch_shapes=scratch,
            compiler_params=pltpu.CompilerParams(vmem_limit_bytes=24 * 1024 * 1024),
            cost_estimate=pl.CostEstimate(flops=flops, bytes_accessed=moved, transcendentals=0),
        )(*operands)

    return call


def dot_nt(left, right):
    return lax.dot_general(left, right, (((1,), (1,)), ((), ())), preferred_element_type=F32)


def attention_kernel(place, packed, near, far, weight, out, done):
    done[...] = jnp.zeros_like(done)
    ctx, core = place[0], place[1]
    rows, keys = packed.shape[0], near.shape[0]
    query = packed[:, 2 * HEAD :]
    spot = ctx * rows + lax.broadcasted_iota(jnp.int32, (rows, keys), 0)
    column = lax.broadcasted_iota(jnp.int32, (rows, keys), 1)
    base = (column // rows) * (2 * rows) + column % rows
    scores = []
    for half, source in enumerate((near, far)):
        key_spot = base + (core ^ half) * rows
        product = dot_nt(query, source[:, :HEAD]) * (1.0 / math.sqrt(HEAD))
        scores.append(jnp.where(spot >= key_spot, product, -1e30))
    top = jnp.maximum(*(jnp.max(score, axis=1, keepdims=True) for score in scores))
    denom, total = 0.0, 0.0
    for score, source in zip(scores, (near, far)):
        weights = jnp.exp(score - top)
        denom = denom + jnp.sum(weights, axis=1, keepdims=True)
        total = total + jnp.dot(weights.astype(BF16), source[:, HEAD:], preferred_element_type=F32)
    attended = (total / denom).astype(BF16)
    blocks, parts, tokens, width = out.shape
    for part in range(parts):
        columns = weight[:, part * width : (part + 1) * width]
        product = jnp.dot(attended, columns, preferred_element_type=F32).astype(BF16)
        for index in range(blocks):
            out[index, part] = product[index * tokens : (index + 1) * tokens, :]


def prepare_kernel(after, ids, shares, gate, up, selector, mixer, weights, sems):
    peers = sems.shape[0] // 2
    piece = gate.shape[1] // peers
    copies = []
    for index in range(peers):
        for which, source in enumerate((gate, up)):
            place = 2 * index + which
            taken = source.at[:, pl.ds(index * piece, piece)]
            copies.append(
                pltpu.make_async_copy(taken, weights.at[:, pl.ds(place * piece, piece)], sems.at[place])
            )
    for copy in copies:
        copy.start()
    slots, tokens = mixer.shape
    expert = lax.broadcasted_iota(jnp.int32, (EXPERTS, tokens), 0)
    named = [(expert == ids[k : k + 1, :]).astype(F32) for k in range(TOP)]
    later = lax.broadcasted_iota(jnp.int32, (tokens, tokens), 0) < lax.broadcasted_iota(
        jnp.int32, (tokens, tokens), 1
    )
    before = jnp.dot((named[0] + named[1]).astype(BF16), later.astype(BF16), preferred_element_type=F32)
    line = lax.broadcasted_iota(jnp.int32, (slots, tokens), 0)
    mixed, picked = 0.0, 0.0
    for k in range(TOP):
        slot = jnp.sum(before * named[k], axis=0, keepdims=True).astype(jnp.int32)
        hit = (line == ids[k : k + 1, :] * CAP + slot).astype(F32)
        picked = picked + hit
        mixed = mixed + hit * shares[k : k + 1, :]
    selector[...] = picked.astype(BF16)
    mixer[...] = mixed
    for copy in copies:
        copy.wait()


def select_kernel(arrived, residual, selector, stream, outgoing):
    mixed = sum(arrived[index].astype(F32) for index in range(arrived.shape[0]))
    total = residual[...].astype(F32) + mixed
    stream[...] = total
    rows = jnp.dot(selector[...], total.astype(BF16), preferred_element_type=F32)
    halves, experts, slots, _ = outgoing.shape
    for expert in range(experts):
        part = rows[expert * slots : (expert + 1) * slots, :].astype(BF16)
        for half in range(halves):
            outgoing[half, expert] = part


def arrange_kernel(arrived, weights, out):
    rows = jnp.concatenate([arrived[index].astype(F32) for index in range(arrived.shape[0])], axis=0).astype(BF16)
    for index in range(out.shape[0]):
        out[index] = rows


def share_of(place, scaled, near, far, offset, out):
    width = out.shape[1] // 2
    start = pl.multiple_of((place[2] ^ offset) * width, width)
    for index, source in enumerate((near, far)):
        product = jnp.dot(scaled, source[:, pl.ds(start, width)], preferred_element_type=F32)
        out[: scaled.shape[0], index * width : (index + 1) * width] = product.astype(BF16)


def tail_of(norm, lines):
    high = norm.astype(BF16).astype(F32)
    line = lax.broadcasted_iota(jnp.int32, (lines, norm.shape[1]), 0)
    return jnp.where(line == 0, high, jnp.where(line == 1, norm - high, 0.0)).astype(BF16)


def first_kernel(place, rows, gain, near, far, third, scaled_out, tail_out, taken, sems):
    count, depth = rows.shape
    width = third.shape[1] // 2
    start = pl.multiple_of((place[2] ^ 3) * width, width)
    copies = [
        pltpu.make_async_copy(source.at[:, pl.ds(start, width)], taken.at[index], sems.at[index])
        for index, source in enumerate((near, far))
    ]
    for copy in copies:
        copy.start()
    widened = rows[...].astype(F32)
    scaled = (widened * gain[...]).astype(BF16)
    scaled_out[...] = scaled
    same = lax.broadcasted_iota(jnp.int32, (128, 128), 0) == lax.broadcasted_iota(jnp.int32, (128, 128), 1)
    norms = []
    for first in range(0, count, 128):
        block = rows[first : first + 128, :]
        norms.append(jnp.sum(jnp.where(same, dot_nt(block, block), 0.0), axis=0, keepdims=True))
    norm = jnp.concatenate(norms + [jnp.zeros((1, third.shape[1] - count), F32)], axis=1)
    tail = tail_of(norm, TAIL)
    third[count:, :] = tail
    tail_out[...] = tail
    for index, copy in enumerate(copies):
        copy.wait()
        product = jnp.dot(scaled, taken[index], preferred_element_type=F32)
        third[:count, index * width : (index + 1) * width] = product.astype(BF16)


def others_kernel(place, scaled, tail, near, far, second, first, own):
    for offset, out in ((2, second), (1, first), (0, own)):
        out[scaled.shape[0] :, :] = tail[...]
        share_of(place, scaled[...], near, far, offset, out)


def pair_kernel(own, arrived, first, pair, first_out):
    count = own.shape[0] - TAIL
    pair[:count, :] = (own[:count, :].astype(F32) + arrived[:count, :].astype(F32)).astype(BF16)
    tail = own[count:, :].astype(F32) + arrived[count:, :].astype(F32)
    pair[count:, :] = tail_of(tail[0:1, :] + tail[1:2, :], TAIL)
    first_out[...] = first[...]


def active_kernel(*refs):
    parts, out = refs[:-1], refs[-1]
    piece = out.shape[1]
    count = parts[0].shape[0] - TAIL
    tail = sum(part[count:, :].astype(F32) for part in parts)
    inverse = lax.rsqrt((tail[0:1, :] + tail[1:2, :]) / D + 1e-05)
    for group in range(count // piece):
        first = group * piece
        factor = jnp.broadcast_to(inverse[:, first : first + piece], (piece, piece)).T
        summed = sum(part[first : first + piece, :].astype(F32) for part in parts)
        for index in range(out.shape[0] // count):
            gate = summed[:, 2 * index * piece : (2 * index + 1) * piece] * factor
            up = summed[:, (2 * index + 1) * piece : 2 * (index + 1) * piece] * factor
            active = (gate / (1.0 + jnp.exp(-gate)) * up).astype(BF16)
            out[index * count + first : index * count + first + piece, :] = active


def down_kernel(active, near, far, out):
    count = out.shape[0]
    total = 0.0
    for index, weight in enumerate((near, far)):
        rows = slice(index * count, (index + 1) * count)
        left = jnp.concatenate([active[h, rows, :] for h in range(active.shape[0])], axis=1)
        total = total + jnp.dot(left, weight[...], preferred_element_type=F32)
    out[...] = total.astype(BF16)


def combine_kernel(back, mixer, stream, out):
    experts = back.shape[0] // 2
    rows = [back[e].astype(F32) + back[experts + e].astype(F32) for e in range(experts)]
    combined = lax.dot_general(
        mixer[...],
        jnp.concatenate(rows, axis=0),
        (((0,), (0,)), ((), ())),
        precision=lax.Precision.HIGHEST,
        preferred_element_type=F32,
    )
    out[...] = (stream[...] + combined).astype(BF16)


def shards(
    queries,
    key_heads,
    value_heads,
    residual,
    out_weight,
    norm_gain,
    gate_weight,
    up_weight,
    down_weight,
    expert_ids,
    expert_weights,
):
    plane = lax.axis_size(PLANE)
    lines, halves = lax.axis_size("x"), lax.axis_size("yh")
    exp_count = lax.axis_size("exp")
    hid_count = lax.axis_size("hid")
    tok_rows = queries.shape[0]
    row_count = tok_rows // exp_count
    width_part = D // hid_count
    ff_part = gate_weight.shape[2]
    piece = ff_part // hid_count
    shape = jax.ShapeDtypeStruct

    with jax.named_scope("kv_gather"):
        packed = lax.optimization_barrier(jnp.concatenate([key_heads, value_heads, queries], axis=1))
        near = spread(packed[:, : 2 * HEAD], PLANE)
        near = near.reshape(plane * tok_rows, 2 * HEAD)
        far = other_core(near)
    with jax.named_scope("attention"):
        place = [lax.axis_index(CTX), lax.axis_index("core"), lax.axis_index("hid")]
        place = jnp.stack(place).astype(jnp.int32)
        partials, done = whole(
            attention_kernel,
            [shape((exp_count, hid_count, row_count, width_part), BF16), shape((8, 128), F32)],
            flops=2 * tok_rows * HEAD * (4 * plane * tok_rows + D),
            smem=1,
        )(place, packed, near, far, out_weight)
    with jax.named_scope("prepare"):
        selector, mixer, near_weights = whole(
            prepare_kernel,
            [
                shape((EXPERTS * CAP, row_count), BF16),
                shape((EXPERTS * CAP, row_count), F32),
                shape((width_part, 2 * ff_part), BF16),
            ],
            flops=0,
            scratch=[pltpu.SemaphoreType.DMA((2 * hid_count,))],
        )(done, expert_ids.T, expert_weights.T, gate_weight[0], up_weight[0])
        near_down = down_weight[0]
        far_weights, far_down = other_core(near_weights), other_core(near_down)
    with jax.named_scope("projection"):
        arrived = swap(partials.reshape(exp_count * hid_count, row_count, width_part), ("exp", "hid"))
        stream, outgoing = whole(
            select_kernel,
            [shape((row_count, width_part), F32), shape((halves, exp_count, CAP, width_part), BF16)],
            flops=2 * arrived.size,
        )(arrived, residual, selector)

    with jax.named_scope("dispatch"):
        arrived = swap(outgoing.reshape(halves * exp_count, CAP, width_part), ("yh", "exp"))
        (copies,) = whole(
            arrange_kernel,
            [shape((lines, halves * exp_count * CAP, width_part), BF16)],
            flops=0,
            held=1,
        )(arrived, far_weights)
        arrived = swap(copies, "x")
        count = lines * halves * exp_count * CAP
        rows = arrived.reshape(count, width_part)

    with jax.named_scope("gate_up"):
        part = shape((count + TAIL, 4 * piece), BF16)
        third, scaled, tail = whole(
            first_kernel,
            [part, shape((count, width_part), BF16), shape((TAIL, 4 * piece), BF16)],
            flops=2 * count * width_part * ff_part,
            smem=1,
            held=2,
            scratch=[pltpu.VMEM((2, width_part, 2 * piece), BF16), pltpu.SemaphoreType.DMA((2,))],
        )(place, rows, norm_gain.reshape(1, width_part), near_weights, far_weights)
        third = to_peer(third, 1)
        second, first, own = whole(
            others_kernel, [part] * 3, flops=6 * count * width_part * ff_part, smem=1
        )(place, scaled, tail, near_weights, far_weights)
        pair, first = whole(pair_kernel, [part] * 2, flops=count * piece * 8)(second, third, first)
        arrivals = [to_peer(pair, 2), to_peer(first, 1), own]
    with jax.named_scope("active"):
        (active,) = whole(active_kernel, [shape((2 * count, piece), BF16)], flops=count * piece * 40)(*arrivals)
        active = lax.all_gather(active, "hid", axis=0, tiled=False)
    with jax.named_scope("down"):
        (back,) = whole(
            down_kernel, [shape((count, width_part), BF16)], flops=4 * count * ff_part * width_part
        )(active, near_down, far_down)
        back = swap(back.reshape(lines, count // lines, width_part), "x")
        back = jnp.sum(back.astype(F32), axis=0).astype(BF16)
        back = swap(back.reshape(halves * exp_count, CAP, width_part), ("yh", "exp"))
    with jax.named_scope("combine"):
        (out,) = whole(combine_kernel, [shape((row_count, width_part), BF16)], flops=2 * back.size)(
            back, mixer, stream
        )
    return out


def solution(mesh):
    ctx, exp, hid = mesh.devices.shape
    split = Mesh(mesh.devices.reshape(ctx // 4, 2, 2, exp, hid), CTX + ("exp", "hid"))
    return jax.shard_map(
        shards,
        mesh=split,
        in_specs=(
            P(CTX, ("exp", "hid")),
            P(CTX, "exp"),
            P(CTX, "exp"),
            P(CTX + ("exp",), "hid"),
            P(("exp", "hid"), None),
            P("hid"),
            P("exp", "hid", CTX),
            P("exp", "hid", CTX),
            P("exp", CTX, "hid"),
            P(CTX + ("exp",), None),
            P(CTX + ("exp",), None),
        ),
        out_specs=P(CTX + ("exp",), "hid"),
        check_vma=False,
    )
```

```python
import math

import jax
import jax.numpy as jnp
from jax import lax
from jax.experimental import pallas as pl
from jax.experimental.pallas import tpu as pltpu
from jax.sharding import Mesh
from jax.sharding import PartitionSpec as P

HEADS = 32
KV_HEADS = 8
HEAD = 128
D = 4096
TOP = 2
EXPERTS = 8
CAP = 6
CTX = ("x", "yh", "core")
PLANE = ("x", "yh")
F32, BF16 = jnp.float32, jnp.bfloat16
TAIL = 16


def swap(value, axes):
    return lax.all_to_all(value, axes, split_axis=0, concat_axis=0, tiled=True)


def spread(value, axes):
    return swap(jnp.broadcast_to(value[None], (lax.axis_size(axes),) + value.shape), axes)


def other_core(value):
    return lax.ppermute(value, "core", [(0, 1), (1, 0)])


def to_peer(value, offset):
    return lax.ppermute(value, "hid", [(h, h ^ offset) for h in range(lax.axis_size("hid"))])


def whole(kernel, out_shapes, flops, smem=0, held=0, scratch=()):
    def call(*operands):
        spaces = [pltpu.SMEM] * smem + [pltpu.VMEM] * (len(operands) - smem - held) + [pl.ANY] * held
        moved = sum(math.prod(a.shape) * a.dtype.itemsize for a in operands)
        moved += sum(math.prod(a.shape) * a.dtype.itemsize for a in out_shapes)
        return pl.pallas_call(
            kernel,
            out_shape=out_shapes,
            in_specs=[pl.BlockSpec(memory_space=space) for space in spaces],
            out_specs=[pl.BlockSpec(memory_space=pltpu.VMEM)] * len(out_shapes),
            scratch_shapes=scratch,
            compiler_params=pltpu.CompilerParams(vmem_limit_bytes=24 * 1024 * 1024),
            cost_estimate=pl.CostEstimate(flops=flops, bytes_accessed=moved, transcendentals=0),
        )(*operands)

    return call


def dot_nt(left, right):
    return lax.dot_general(left, right, (((1,), (1,)), ((), ())), preferred_element_type=F32)


def attention_kernel(place, packed, near, far, weight, out, done):
    done[...] = jnp.zeros_like(done)
    ctx, core = place[0], place[1]
    rows, keys = packed.shape[0], near.shape[0]
    query = packed[:, 2 * HEAD :]
    spot = ctx * rows + lax.broadcasted_iota(jnp.int32, (rows, keys), 0)
    column = lax.broadcasted_iota(jnp.int32, (rows, keys), 1)
    base = (column // rows) * (2 * rows) + column % rows
    scores = []
    for half, source in enumerate((near, far)):
        key_spot = base + (core ^ half) * rows
        product = dot_nt(query, source[:, :HEAD]) * (1.0 / math.sqrt(HEAD))
        scores.append(jnp.where(spot >= key_spot, product, -1e30))
    top = jnp.maximum(*(jnp.max(score, axis=1, keepdims=True) for score in scores))
    denom, total = 0.0, 0.0
    for score, source in zip(scores, (near, far)):
        weights = jnp.exp(score - top)
        denom = denom + jnp.sum(weights, axis=1, keepdims=True)
        total = total + jnp.dot(weights.astype(BF16), source[:, HEAD:], preferred_element_type=F32)
    attended = (total / denom).astype(BF16)
    parts, _, width = out.shape
    for part in range(parts):
        columns = weight[:, part * width : (part + 1) * width]
        out[part] = jnp.dot(attended, columns, preferred_element_type=F32).astype(BF16)


def prepare_kernel(after, ids, shares, gate, up, selector, mixer, weights, sems):
    peers = sems.shape[0] // 2
    piece = gate.shape[1] // peers
    copies = []
    for index in range(peers):
        for which, source in enumerate((gate, up)):
            place = 2 * index + which
            taken = source.at[:, pl.ds(index * piece, piece)]
            copies.append(
                pltpu.make_async_copy(taken, weights.at[:, pl.ds(place * piece, piece)], sems.at[place])
            )
    for copy in copies:
        copy.start()
    slots, tokens = mixer.shape
    expert = lax.broadcasted_iota(jnp.int32, (EXPERTS, tokens), 0)
    named = [(expert == ids[k : k + 1, :]).astype(F32) for k in range(TOP)]
    later = lax.broadcasted_iota(jnp.int32, (tokens, tokens), 0) < lax.broadcasted_iota(
        jnp.int32, (tokens, tokens), 1
    )
    before = jnp.dot((named[0] + named[1]).astype(BF16), later.astype(BF16), preferred_element_type=F32)
    line = lax.broadcasted_iota(jnp.int32, (slots, tokens), 0)
    mixed, picked = 0.0, 0.0
    for k in range(TOP):
        slot = jnp.sum(before * named[k], axis=0, keepdims=True).astype(jnp.int32)
        hit = (line == ids[k : k + 1, :] * CAP + slot).astype(F32)
        picked = picked + hit
        mixed = mixed + hit * shares[k : k + 1, :]
    selector[...] = picked.astype(BF16)
    mixer[...] = mixed
    for copy in copies:
        copy.wait()


def select_kernel(arrived, residual, selector, stream, outgoing):
    mixed = sum(arrived[index].astype(F32) for index in range(arrived.shape[0]))
    total = residual[...].astype(F32) + mixed
    stream[...] = total
    rows = jnp.dot(selector[...], total.astype(BF16), preferred_element_type=F32)
    halves, experts, slots, _ = outgoing.shape
    for expert in range(experts):
        part = rows[expert * slots : (expert + 1) * slots, :].astype(BF16)
        for half in range(halves):
            outgoing[half, expert] = part


def arrange_kernel(arrived, weights, down, out):
    rows = jnp.concatenate([arrived[index].astype(F32) for index in range(arrived.shape[0])], axis=0).astype(BF16)
    for index in range(out.shape[0]):
        out[index] = rows


def share_of(place, scaled, near, far, offset, out):
    width = out.shape[1] // 2
    start = pl.multiple_of((place[2] ^ offset) * width, width)
    for index, source in enumerate((near, far)):
        product = jnp.dot(scaled, source[:, pl.ds(start, width)], preferred_element_type=F32)
        out[: scaled.shape[0], index * width : (index + 1) * width] = product.astype(BF16)


def tail_of(norm, lines):
    high = norm.astype(BF16).astype(F32)
    line = lax.broadcasted_iota(jnp.int32, (lines, norm.shape[1]), 0)
    return jnp.where(line == 0, high, jnp.where(line == 1, norm - high, 0.0)).astype(BF16)


def first_kernel(place, rows, gain, near, far, third, scaled_out, tail_out, taken, sems):
    count, depth = rows.shape
    width = third.shape[1] // 2
    start = pl.multiple_of((place[2] ^ 3) * width, width)
    copies = [
        pltpu.make_async_copy(source.at[:, pl.ds(start, width)], taken.at[index], sems.at[index])
        for index, source in enumerate((near, far))
    ]
    for copy in copies:
        copy.start()
    widened = rows[...].astype(F32)
    scaled = (widened * gain[...]).astype(BF16)
    scaled_out[...] = scaled
    square = widened * widened
    high = square.astype(BF16)
    low = (square - high.astype(F32)).astype(BF16)
    ones = jnp.ones((TAIL, depth), BF16)
    norm = (dot_nt(ones, high) + dot_nt(ones, low))[:1, :]
    norm = jnp.concatenate([norm, jnp.zeros((1, third.shape[1] - count), F32)], axis=1)
    tail = tail_of(norm, TAIL)
    third[count:, :] = tail
    tail_out[...] = tail
    for index, copy in enumerate(copies):
        copy.wait()
        product = jnp.dot(scaled, taken[index], preferred_element_type=F32)
        third[:count, index * width : (index + 1) * width] = product.astype(BF16)


def others_kernel(place, scaled, tail, near, far, second, first, own):
    for offset, out in ((2, second), (1, first), (0, own)):
        out[scaled.shape[0] :, :] = tail[...]
        share_of(place, scaled[...], near, far, offset, out)


def pair_kernel(own, arrived, first, pair, first_out):
    count = own.shape[0] - TAIL
    pair[:count, :] = (own[:count, :].astype(F32) + arrived[:count, :].astype(F32)).astype(BF16)
    tail = own[count:, :].astype(F32) + arrived[count:, :].astype(F32)
    pair[count:, :] = tail_of(tail[0:1, :] + tail[1:2, :], TAIL)
    first_out[...] = first[...]


def active_kernel(*refs):
    parts, out = refs[:-1], refs[-1]
    piece = out.shape[1]
    count = parts[0].shape[0] - TAIL
    tail = sum(part[count:, :].astype(F32) for part in parts)
    inverse = lax.rsqrt((tail[0:1, :] + tail[1:2, :]) / D + 1e-05)
    for group in range(count // piece):
        first = group * piece
        factor = jnp.broadcast_to(inverse[:, first : first + piece], (piece, piece)).T
        summed = sum(part[first : first + piece, :].astype(F32) for part in parts)
        for index in range(out.shape[0] // count):
            gate = summed[:, 2 * index * piece : (2 * index + 1) * piece] * factor
            up = summed[:, (2 * index + 1) * piece : 2 * (index + 1) * piece] * factor
            active = (gate / (1.0 + jnp.exp(-gate)) * up).astype(BF16)
            out[index * count + first : index * count + first + piece, :] = active


def down_kernel(active, near, far, out):
    count = out.shape[0]
    total = 0.0
    for index, weight in enumerate((near, far)):
        rows = slice(index * count, (index + 1) * count)
        left = jnp.concatenate([active[h, rows, :] for h in range(active.shape[0])], axis=1)
        total = total + jnp.dot(left, weight[...], preferred_element_type=F32)
    out[...] = total.astype(BF16)


def combine_kernel(back, mixer, stream, out):
    experts = back.shape[0] // 2
    rows = [back[e].astype(F32) + back[experts + e].astype(F32) for e in range(experts)]
    combined = lax.dot_general(
        mixer[...],
        jnp.concatenate(rows, axis=0),
        (((0,), (0,)), ((), ())),
        precision=lax.Precision.HIGHEST,
        preferred_element_type=F32,
    )
    out[...] = (stream[...] + combined).astype(BF16)


def shards(
    queries,
    key_heads,
    value_heads,
    residual,
    out_weight,
    norm_gain,
    gate_weight,
    up_weight,
    down_weight,
    expert_ids,
    expert_weights,
):
    plane = lax.axis_size(PLANE)
    lines, halves = lax.axis_size("x"), lax.axis_size("yh")
    exp_count = lax.axis_size("exp")
    hid_count = lax.axis_size("hid")
    tok_rows = queries.shape[0]
    row_count = tok_rows // exp_count
    width_part = D // hid_count
    ff_part = gate_weight.shape[2]
    piece = ff_part // hid_count
    shape = jax.ShapeDtypeStruct

    with jax.named_scope("kv_gather"):
        packed = lax.optimization_barrier(jnp.concatenate([key_heads, value_heads, queries], axis=1))
        near = spread(packed[:, : 2 * HEAD], PLANE)
        near = near.reshape(plane * tok_rows, 2 * HEAD)
        far = other_core(near)
    with jax.named_scope("attention"):
        place = [lax.axis_index(CTX), lax.axis_index("core"), lax.axis_index("hid")]
        place = jnp.stack(place).astype(jnp.int32)
        partials, done = whole(
            attention_kernel,
            [shape((hid_count, tok_rows, width_part), BF16), shape((8, 128), F32)],
            flops=2 * tok_rows * HEAD * (4 * plane * tok_rows + D),
            smem=1,
        )(place, packed, near, far, out_weight)
    with jax.named_scope("prepare"):
        selector, mixer, near_weights = whole(
            prepare_kernel,
            [
                shape((EXPERTS * CAP, row_count), BF16),
                shape((EXPERTS * CAP, row_count), F32),
                shape((width_part, 2 * ff_part), BF16),
            ],
            flops=0,
            scratch=[pltpu.SemaphoreType.DMA((2 * hid_count,))],
        )(done, expert_ids.T, expert_weights.T, gate_weight[0], up_weight[0])
        near_down = down_weight[0]
        far_weights, far_down = other_core(near_weights), other_core(near_down)
    with jax.named_scope("projection"):
        arrived = swap(partials.reshape(hid_count * exp_count, row_count, width_part), ("hid", "exp"))
        stream, outgoing = whole(
            select_kernel,
            [shape((row_count, width_part), F32), shape((halves, exp_count, CAP, width_part), BF16)],
            flops=2 * arrived.size,
        )(arrived, residual, selector)

    with jax.named_scope("dispatch"):
        arrived = swap(outgoing.reshape(halves * exp_count, CAP, width_part), ("yh", "exp"))
        (copies,) = whole(
            arrange_kernel,
            [shape((lines, halves * exp_count * CAP, width_part), BF16)],
            flops=0,
            held=2,
        )(arrived, far_weights, far_down)
        arrived = swap(copies, "x")
        count = lines * halves * exp_count * CAP
        rows = arrived.reshape(count, width_part)

    with jax.named_scope("gate_up"):
        part = shape((count + TAIL, 4 * piece), BF16)
        third, scaled, tail = whole(
            first_kernel,
            [part, shape((count, width_part), BF16), shape((TAIL, 4 * piece), BF16)],
            flops=2 * count * width_part * ff_part,
            smem=1,
            held=2,
            scratch=[pltpu.VMEM((2, width_part, 2 * piece), BF16), pltpu.SemaphoreType.DMA((2,))],
        )(place, rows, norm_gain.reshape(1, width_part), near_weights, far_weights)
        third = to_peer(third, 1)
        second, first, own = whole(
            others_kernel, [part] * 3, flops=6 * count * width_part * ff_part, smem=1
        )(place, scaled, tail, near_weights, far_weights)
        pair, first = whole(pair_kernel, [part] * 2, flops=count * piece * 8)(second, third, first)
        arrivals = [to_peer(pair, 2), to_peer(first, 1), own]
    with jax.named_scope("active"):
        (active,) = whole(active_kernel, [shape((2 * count, piece), BF16)], flops=count * piece * 40)(*arrivals)
        active = lax.all_gather(active, "hid", axis=0, tiled=False)
    with jax.named_scope("down"):
        (back,) = whole(
            down_kernel, [shape((count, width_part), BF16)], flops=4 * count * ff_part * width_part
        )(active, near_down, far_down)
        back = swap(back.reshape(lines, count // lines, width_part), "x")
        back = jnp.sum(back.astype(F32), axis=0).astype(BF16)
        back = swap(back.reshape(halves * exp_count, CAP, width_part), ("yh", "exp"))
    with jax.named_scope("combine"):
        (out,) = whole(combine_kernel, [shape((row_count, width_part), BF16)], flops=2 * back.size)(
            back, mixer, stream
        )
    return out


def solution(mesh):
    ctx, exp, hid = mesh.devices.shape
    split = Mesh(mesh.devices.reshape(ctx // 4, 2, 2, exp, hid), CTX + ("exp", "hid"))
    return jax.shard_map(
        shards,
        mesh=split,
        in_specs=(
            P(CTX, ("exp", "hid")),
            P(CTX, "exp"),
            P(CTX, "exp"),
            P(CTX + ("exp",), "hid"),
            P(("exp", "hid"), None),
            P("hid"),
            P("exp", "hid", CTX),
            P("exp", "hid", CTX),
            P("exp", CTX, "hid"),
            P(CTX + ("exp",), None),
            P(CTX + ("exp",), None),
        ),
        out_specs=P(CTX + ("exp",), "hid"),
        check_vma=False,
    )
```

```python
import math

import jax
import jax.numpy as jnp
from jax import lax
from jax.experimental import pallas as pl
from jax.experimental.pallas import tpu as pltpu
from jax.sharding import Mesh
from jax.sharding import PartitionSpec as P

HEADS = 32
KV_HEADS = 8
HEAD = 128
D = 4096
TOP = 2
EXPERTS = 8
CAP = 6
CTX = ("x", "yh", "core")
PLANE = ("x", "yh")
F32, BF16 = jnp.float32, jnp.bfloat16
TAIL = 16


def swap(value, axes):
    return lax.all_to_all(value, axes, split_axis=0, concat_axis=0, tiled=True)


def spread(value, axes):
    return swap(jnp.broadcast_to(value[None], (lax.axis_size(axes),) + value.shape), axes)


def other_core(value):
    return lax.ppermute(value, "core", [(0, 1), (1, 0)])


def to_peer(value, offset):
    return lax.ppermute(value, "hid", [(h, h ^ offset) for h in range(lax.axis_size("hid"))])


def whole(kernel, out_shapes, flops, smem=0, held=0, scratch=()):
    def call(*operands):
        spaces = [pltpu.SMEM] * smem + [pltpu.VMEM] * (len(operands) - smem - held) + [pl.ANY] * held
        moved = sum(math.prod(a.shape) * a.dtype.itemsize for a in operands)
        moved += sum(math.prod(a.shape) * a.dtype.itemsize for a in out_shapes)
        return pl.pallas_call(
            kernel,
            out_shape=out_shapes,
            in_specs=[pl.BlockSpec(memory_space=space) for space in spaces],
            out_specs=[pl.BlockSpec(memory_space=pltpu.VMEM)] * len(out_shapes),
            scratch_shapes=scratch,
            compiler_params=pltpu.CompilerParams(vmem_limit_bytes=24 * 1024 * 1024),
            cost_estimate=pl.CostEstimate(flops=flops, bytes_accessed=moved, transcendentals=0),
        )(*operands)

    return call


def dot_nt(left, right):
    return lax.dot_general(left, right, (((1,), (1,)), ((), ())), preferred_element_type=F32)


def attention_kernel(place, packed, near, far, weight, out, done):
    done[...] = jnp.zeros_like(done)
    ctx, core = place[0], place[1]
    rows, keys = packed.shape[0], near.shape[0]
    query = packed[:, 2 * HEAD :]
    spot = ctx * rows + lax.broadcasted_iota(jnp.int32, (rows, keys), 0)
    column = lax.broadcasted_iota(jnp.int32, (rows, keys), 1)
    base = (column // rows) * (2 * rows) + column % rows
    scores = []
    for half, source in enumerate((near, far)):
        key_spot = base + (core ^ half) * rows
        product = dot_nt(query, source[:, :HEAD]) * (1.0 / math.sqrt(HEAD))
        scores.append(jnp.where(spot >= key_spot, product, -1e30))
    top = jnp.maximum(*(jnp.max(score, axis=1, keepdims=True) for score in scores))
    denom, total = 0.0, 0.0
    for score, source in zip(scores, (near, far)):
        weights = jnp.exp(score - top)
        denom = denom + jnp.sum(weights, axis=1, keepdims=True)
        total = total + jnp.dot(weights.astype(BF16), source[:, HEAD:], preferred_element_type=F32)
    attended = (total / denom).astype(BF16)
    blocks, parts, tokens, width = out.shape
    for part in range(parts):
        columns = weight[:, part * width : (part + 1) * width]
        product = jnp.dot(attended, columns, preferred_element_type=F32).astype(BF16)
        for index in range(blocks):
            out[index, part] = product[index * tokens : (index + 1) * tokens, :]


def prepare_kernel(after, ids, shares, gate, up, selector, mixer, weights, sems):
    peers = sems.shape[0] // 2
    piece = gate.shape[1] // peers
    copies = []
    for index in range(peers):
        for which, source in enumerate((gate, up)):
            place = 2 * index + which
            taken = source.at[:, pl.ds(index * piece, piece)]
            copies.append(
                pltpu.make_async_copy(taken, weights.at[:, pl.ds(place * piece, piece)], sems.at[place])
            )
    for copy in copies:
        copy.start()
    slots, tokens = mixer.shape
    expert = lax.broadcasted_iota(jnp.int32, (EXPERTS, tokens), 0)
    named = [(expert == ids[k : k + 1, :]).astype(F32) for k in range(TOP)]
    later = lax.broadcasted_iota(jnp.int32, (tokens, tokens), 0) < lax.broadcasted_iota(
        jnp.int32, (tokens, tokens), 1
    )
    before = jnp.dot((named[0] + named[1]).astype(BF16), later.astype(BF16), preferred_element_type=F32)
    line = lax.broadcasted_iota(jnp.int32, (slots, tokens), 0)
    mixed, picked = 0.0, 0.0
    for k in range(TOP):
        slot = jnp.sum(before * named[k], axis=0, keepdims=True).astype(jnp.int32)
        hit = (line == ids[k : k + 1, :] * CAP + slot).astype(F32)
        picked = picked + hit
        mixed = mixed + hit * shares[k : k + 1, :]
    selector[...] = picked.astype(BF16)
    mixer[...] = mixed
    for copy in copies:
        copy.wait()


def select_kernel(arrived, residual, selector, stream, outgoing):
    mixed = sum(arrived[index].astype(F32) for index in range(arrived.shape[0]))
    total = residual[...].astype(F32) + mixed
    stream[...] = total
    rows = jnp.dot(selector[...], total.astype(BF16), preferred_element_type=F32)
    halves, experts, slots, _ = outgoing.shape
    for expert in range(experts):
        part = rows[expert * slots : (expert + 1) * slots, :].astype(BF16)
        for half in range(halves):
            outgoing[half, expert] = part


def arrange_kernel(arrived, weights, out):
    rows = jnp.concatenate([arrived[index].astype(F32) for index in range(arrived.shape[0])], axis=0).astype(BF16)
    for index in range(out.shape[0]):
        out[index] = rows


def share_of(place, scaled, near, far, offset, out):
    width = out.shape[1] // 2
    start = pl.multiple_of((place[2] ^ offset) * width, width)
    for index, source in enumerate((near, far)):
        product = jnp.dot(scaled, source[:, pl.ds(start, width)], preferred_element_type=F32)
        out[: scaled.shape[0], index * width : (index + 1) * width] = product.astype(BF16)


def tail_of(norm, lines):
    high = norm.astype(BF16).astype(F32)
    line = lax.broadcasted_iota(jnp.int32, (lines, norm.shape[1]), 0)
    return jnp.where(line == 0, high, jnp.where(line == 1, norm - high, 0.0)).astype(BF16)


def first_kernel(place, rows, gain, near, far, third, scaled_out, tail_out, taken, sems):
    count, depth = rows.shape
    width = third.shape[1] // 2
    start = pl.multiple_of((place[2] ^ 3) * width, width)
    copies = [
        pltpu.make_async_copy(source.at[:, pl.ds(start, width)], taken.at[index], sems.at[index])
        for index, source in enumerate((near, far))
    ]
    for copy in copies:
        copy.start()
    widened = rows[...].astype(F32)
    scaled = (widened * gain[...]).astype(BF16)
    scaled_out[...] = scaled
    square = widened * widened
    high = square.astype(BF16)
    low = (square - high.astype(F32)).astype(BF16)
    ones = jnp.ones((TAIL, depth), BF16)
    norm = (dot_nt(ones, high) + dot_nt(ones, low))[:1, :]
    norm = jnp.concatenate([norm, jnp.zeros((1, third.shape[1] - count), F32)], axis=1)
    tail = tail_of(norm, TAIL)
    third[count:, :] = tail
    tail_out[...] = tail
    for index, copy in enumerate(copies):
        copy.wait()
        product = jnp.dot(scaled, taken[index], preferred_element_type=F32)
        third[:count, index * width : (index + 1) * width] = product.astype(BF16)


def others_kernel(place, scaled, tail, near, far, second, first, own):
    for offset, out in ((2, second), (1, first), (0, own)):
        out[scaled.shape[0] :, :] = tail[...]
        share_of(place, scaled[...], near, far, offset, out)


def pair_kernel(own, arrived, first, pair, first_out):
    count = own.shape[0] - TAIL
    pair[:count, :] = (own[:count, :].astype(F32) + arrived[:count, :].astype(F32)).astype(BF16)
    tail = own[count:, :].astype(F32) + arrived[count:, :].astype(F32)
    pair[count:, :] = tail_of(tail[0:1, :] + tail[1:2, :], TAIL)
    first_out[...] = first[...]


def active_kernel(*refs):
    parts, out = refs[:-1], refs[-1]
    piece = out.shape[1]
    count = parts[0].shape[0] - TAIL
    tail = sum(part[count:, :].astype(F32) for part in parts)
    inverse = lax.rsqrt((tail[0:1, :] + tail[1:2, :]) / D + 1e-05)
    for group in range(count // piece):
        first = group * piece
        factor = jnp.broadcast_to(inverse[:, first : first + piece], (piece, piece)).T
        summed = sum(part[first : first + piece, :].astype(F32) for part in parts)
        for index in range(out.shape[0] // count):
            gate = summed[:, 2 * index * piece : (2 * index + 1) * piece] * factor
            up = summed[:, (2 * index + 1) * piece : 2 * (index + 1) * piece] * factor
            active = (gate / (1.0 + jnp.exp(-gate)) * up).astype(BF16)
            out[index * count + first : index * count + first + piece, :] = active


def down_kernel(active, near, far, out):
    count = out.shape[0]
    total = 0.0
    for index, weight in enumerate((near, far)):
        rows = slice(index * count, (index + 1) * count)
        left = jnp.concatenate([active[h, rows, :] for h in range(active.shape[0])], axis=1)
        total = total + jnp.dot(left, weight[...], preferred_element_type=F32)
    out[...] = total.astype(BF16)


def combine_kernel(back, mixer, stream, out):
    experts = back.shape[0] // 2
    rows = [back[e].astype(F32) + back[experts + e].astype(F32) for e in range(experts)]
    combined = lax.dot_general(
        mixer[...],
        jnp.concatenate(rows, axis=0),
        (((0,), (0,)), ((), ())),
        precision=lax.Precision.HIGHEST,
        preferred_element_type=F32,
    )
    out[...] = (stream[...] + combined).astype(BF16)


def shards(
    queries,
    key_heads,
    value_heads,
    residual,
    out_weight,
    norm_gain,
    gate_weight,
    up_weight,
    down_weight,
    expert_ids,
    expert_weights,
):
    plane = lax.axis_size(PLANE)
    lines, halves = lax.axis_size("x"), lax.axis_size("yh")
    exp_count = lax.axis_size("exp")
    hid_count = lax.axis_size("hid")
    tok_rows = queries.shape[0]
    row_count = tok_rows // exp_count
    width_part = D // hid_count
    ff_part = gate_weight.shape[2]
    piece = ff_part // hid_count
    shape = jax.ShapeDtypeStruct

    with jax.named_scope("kv_gather"):
        packed = lax.optimization_barrier(jnp.concatenate([key_heads, value_heads, queries], axis=1))
        near = spread(packed[:, : 2 * HEAD], PLANE)
        near = near.reshape(plane * tok_rows, 2 * HEAD)
        far = other_core(near)
    with jax.named_scope("attention"):
        place = [lax.axis_index(CTX), lax.axis_index("core"), lax.axis_index("hid")]
        place = jnp.stack(place).astype(jnp.int32)
        partials, done = whole(
            attention_kernel,
            [shape((exp_count, hid_count, row_count, width_part), BF16), shape((8, 128), F32)],
            flops=2 * tok_rows * HEAD * (4 * plane * tok_rows + D),
            smem=1,
        )(place, packed, near, far, out_weight)
    with jax.named_scope("prepare"):
        selector, mixer, near_weights = whole(
            prepare_kernel,
            [
                shape((EXPERTS * CAP, row_count), BF16),
                shape((EXPERTS * CAP, row_count), F32),
                shape((width_part, 2 * ff_part), BF16),
            ],
            flops=0,
            scratch=[pltpu.SemaphoreType.DMA((2 * hid_count,))],
        )(done, expert_ids.T, expert_weights.T, gate_weight[0], up_weight[0])
        near_down = down_weight[0]
        far_weights, far_down = other_core(near_weights), other_core(near_down)
    with jax.named_scope("projection"):
        arrived = swap(partials.reshape(exp_count * hid_count, row_count, width_part), ("exp", "hid"))
        stream, outgoing = whole(
            select_kernel,
            [shape((row_count, width_part), F32), shape((halves, exp_count, CAP, width_part), BF16)],
            flops=2 * arrived.size,
        )(arrived, residual, selector)

    with jax.named_scope("dispatch"):
        arrived = swap(outgoing.reshape(halves * exp_count, CAP, width_part), ("yh", "exp"))
        (copies,) = whole(
            arrange_kernel,
            [shape((lines, halves * exp_count * CAP, width_part), BF16)],
            flops=0,
            held=1,
        )(arrived, far_weights)
        arrived = swap(copies, "x")
        count = lines * halves * exp_count * CAP
        rows = arrived.reshape(count, width_part)

    with jax.named_scope("gate_up"):
        part = shape((count + TAIL, 4 * piece), BF16)
        third, scaled, tail = whole(
            first_kernel,
            [part, shape((count, width_part), BF16), shape((TAIL, 4 * piece), BF16)],
            flops=2 * count * width_part * ff_part,
            smem=1,
            held=2,
            scratch=[pltpu.VMEM((2, width_part, 2 * piece), BF16), pltpu.SemaphoreType.DMA((2,))],
        )(place, rows, norm_gain.reshape(1, width_part), near_weights, far_weights)
        third = to_peer(third, 1)
        second, first, own = whole(
            others_kernel, [part] * 3, flops=6 * count * width_part * ff_part, smem=1
        )(place, scaled, tail, near_weights, far_weights)
        pair, first = whole(pair_kernel, [part] * 2, flops=count * piece * 8)(second, third, first)
        arrivals = [to_peer(pair, 2), to_peer(first, 1), own]
    with jax.named_scope("active"):
        (active,) = whole(active_kernel, [shape((2 * count, piece), BF16)], flops=count * piece * 40)(*arrivals)
        active = lax.all_gather(active, "hid", axis=0, tiled=False)
    with jax.named_scope("down"):
        (back,) = whole(
            down_kernel, [shape((count, width_part), BF16)], flops=4 * count * ff_part * width_part
        )(active, near_down, far_down)
        back = swap(back.reshape(lines, count // lines, width_part), "x")
        back = jnp.sum(back.astype(F32), axis=0).astype(BF16)
        back = swap(back.reshape(halves * exp_count, CAP, width_part), ("yh", "exp"))
    with jax.named_scope("combine"):
        (out,) = whole(combine_kernel, [shape((row_count, width_part), BF16)], flops=2 * back.size)(
            back, mixer, stream
        )
    return out


def solution(mesh):
    ctx, exp, hid = mesh.devices.shape
    split = Mesh(mesh.devices.reshape(ctx // 4, 2, 2, exp, hid), CTX + ("exp", "hid"))
    return jax.shard_map(
        shards,
        mesh=split,
        in_specs=(
            P(CTX, ("exp", "hid")),
            P(CTX, "exp"),
            P(CTX, "exp"),
            P(CTX + ("exp",), "hid"),
            P(("exp", "hid"), None),
            P("hid"),
            P("exp", "hid", CTX),
            P("exp", "hid", CTX),
            P("exp", CTX, "hid"),
            P(CTX + ("exp",), None),
            P(CTX + ("exp",), None),
        ),
        out_specs=P(CTX + ("exp",), "hid"),
        check_vma=False,
    )
```
